32 devices in a mesh: replica: 8 (over z, x), shard: 4 (over y, core).
Axes of the slice: x: 2, y: 2, z: 4, core: 2. Of those that a mesh axis runs over, the one named last changes fastest.
Arguments:
- tokens: bfloat16 [192, 160, 1024], P(('replica', 'shard')), may hold values from -6 to 6
- out_grad: bfloat16 [192, 160, 1024], P(('replica', 'shard')), may hold values from -6 to 6
- kept_count: int32 [192], P(('replica', 'shard')), may hold values from 0 to 96
- attn_w: float32 [1024, 4096], P('shard')
- mlp_w: float32 [1024, 8192], P('shard')
- vectors: float32 [1024, 12], P('shard'), as said below
- attn_m: float32 [1024, 4096], P('shard')
- mlp_m: float32 [1024, 8192], P('shard')
- small_m: float32 [1024, 12], P('shard')
- attn_v: float32 [1024, 4096], P('shard'), as said below
- mlp_v: float32 [1024, 8192], P('shard'), as said below
- small_v: float32 [1024, 12], P('shard'), as said below
Outputs:
- out_tokens: bfloat16 [192, 160, 1024], P(('replica', 'shard'))
- in_grad: bfloat16 [192, 160, 1024], P(('replica', 'shard'))
- attn_grad: float32 [1024, 4096], P('shard')
- attn_first: float32 [1024, 4096], P('shard')
- attn_second: float32 [1024, 4096], P('shard')
- attn_new: float32 [1024, 4096], P('shard')
- attn_low: bfloat16 [1024, 4096], P('shard')
- mlp_grad: float32 [1024, 8192], P('shard')
- mlp_first: float32 [1024, 8192], P('shard')
- mlp_second: float32 [1024, 8192], P('shard')
- mlp_new: float32 [1024, 8192], P('shard')
- mlp_low: bfloat16 [1024, 8192], P('shard')
- small_grad: float32 [1024, 12], P('shard')
- small_first: float32 [1024, 12], P('shard')
- small_second: float32 [1024, 12], P('shard')
- small_new: float32 [1024, 12], P('shard')
- small_low: bfloat16 [1024, 12], P('shard')
The draws below stay inside these ranges and needn't reach their ends.
Inputs may be any that keep to these rules, and one draw needn't show every extreme that they name: Slot s of image i is a real token where s < 64 + kept_count[i]; later slots are padding. `vectors`: columns 0 and 5 are gains near one, the others biases. `attn_v`: Positive. `mlp_v`: Positive. `small_v`: Positive.
All inputs are finite; a program needn't handle non-finite values.
Results may differ from the reference program's by a relative error of at most 0.025.
Values may be sent and summed in bfloat16 or wider, within the bound.
No kernel may reach another device: no remote copies, remote signals or barrier semaphores. Data moves between devices by JAX's collectives and lax.ppermute only.
A program may use at most 320 MiB of HBM per device.

```python
import math
import jax
import jax.numpy as jnp
from jax import lax

D = 1024
HEADS = 16
HEAD_DIM = 64
FF = 4096
BUF = 64
KEEP = 96
SLOTS = 160
STEP = 10
IMAGES = 192


BETA_ONE = 0.9


BETA_TWO = 0.999


SMALL_FACTORS = [1.4, 1.4, 0.8, 0.8, 1.0, 0.5, 0.5, 1.0, 0.25, 0.25, 0.25, 0.25]


def grad_size():
    return math.sqrt((BUF + KEEP / 2.0) * IMAGES) / IMAGES


def column_factors(spans):
    return jnp.concatenate([jnp.full((span_len,), factor, jnp.float32) for span_len, factor in spans])


def attn_factors():
    return column_factors([(3 * D, 0.8), (D, 0.1)])


def mlp_factors():
    return column_factors([(FF, 0.25), (FF, 0.6)])


def small_factors():
    return jnp.array(SMALL_FACTORS, jnp.float32)


def first_moment(key, rows, factors):
    base = jax.random.truncated_normal(key, -4.0, 4.0, (rows, factors.shape[0]), jnp.float32)
    return base * factors[None, :] * (grad_size() * (1.0 - BETA_ONE) / BETA_ONE)


def second_moment(key, rows, factors):
    spread = jnp.exp(jax.random.uniform(key, (rows, factors.shape[0]), jnp.float32, 0.0, math.log(4.0)))
    scale_sq = (factors[None, :] * grad_size()) ** 2
    return spread * scale_sq * ((1.0 - BETA_TWO) / BETA_TWO)


def draw_attn_w(key, part):
    key = jax.random.fold_in(key, 11)
    base = jax.random.truncated_normal(key, -4.0, 4.0, (D, 4 * D), jnp.float32)
    out_fan = max(D // 64, 1)
    factors = column_factors([(3 * D, D ** (-0.5)), (D, out_fan ** (-0.5))])
    return base * factors[None, :]


def draw_mlp_w(key, part):
    key = jax.random.fold_in(key, 12)
    base = jax.random.truncated_normal(key, -4.0, 4.0, (D, 2 * FF), jnp.float32)
    factors = column_factors([(FF, D ** (-0.5)), (FF, FF ** (-0.5))])
    return base * factors[None, :]


def draw_vectors(key, part):
    key = jax.random.fold_in(key, 13)
    base = jax.random.truncated_normal(key, -4.0, 4.0, (D, 12), jnp.float32)
    is_gain = jnp.zeros((12,), jnp.float32).at[0].set(1.0).at[5].set(1.0)
    spread = 0.2 - 0.1 * is_gain
    return is_gain[None, :] + base * spread[None, :]


def draw_attn_m(key, part):
    key = jax.random.fold_in(key, 21)
    return first_moment(key, D, attn_factors())


def draw_mlp_m(key, part):
    key = jax.random.fold_in(key, 22)
    return first_moment(key, D, mlp_factors())


def draw_small_m(key, part):
    key = jax.random.fold_in(key, 23)
    return first_moment(key, D, small_factors())


def draw_attn_v(key, part):
    key = jax.random.fold_in(key, 31)
    return second_moment(key, D, attn_factors())


def draw_mlp_v(key, part):
    key = jax.random.fold_in(key, 32)
    return second_moment(key, D, mlp_factors())


def draw_small_v(key, part):
    key = jax.random.fold_in(key, 33)
    return second_moment(key, D, small_factors())


def with_ends(values, rng, least, high):
    longest = values.shape.index(max(values.shape))
    spots = []
    for shift in (0, 1):
        where = [jax.random.randint(jax.random.fold_in(rng, axis), (), 0, length) for axis, length in enumerate(values.shape)]
        where[longest] = (where[longest] + shift) % values.shape[longest]
        spots.append(tuple(where))
    return values.at[spots[0]].set(least).at[spots[1]].set(high)


def block_levels(own_key, extent, shards, least, largest):
    factor_of = 1.0
    for axis_at, parts in shards:
        draws = jax.random.uniform(jax.random.fold_in(jax.random.fold_in(own_key, 6), axis_at), (parts,), jnp.float32, least / len(shards), largest / len(shards))
        factor_of = factor_of * jnp.repeat(jnp.exp(draws), extent[axis_at] // parts).reshape((-1,) + (1,) * (len(extent) - 1 - axis_at))
    return factor_of


def scatter_about(own_key, extent, scale, most, cuts=(), kind=jnp.bfloat16):
    values = jax.random.normal(own_key, extent, jnp.float32) * scale
    if len(cuts) > 0:
        values = block_levels(own_key, extent, cuts, -0.22, 0.18) * values
    return jnp.clip(values, min=-most, max=most).astype(kind)


def setup_inputs(seed: int = 0) -> dict:
    arg_keys = jax.random.split(jax.random.key(seed), 13)
    tokens = scatter_about(arg_keys[0], (IMAGES, SLOTS, D), 1.0, 6.0, ((0, 32),))
    out_grad = scatter_about(arg_keys[1], (IMAGES, SLOTS, D), 1.0, 6.0, ((0, 32),))
    kept_count = with_ends(jax.random.randint(arg_keys[2], (IMAGES,), 0, KEEP + 1), jax.random.fold_in(arg_keys[2], 1), 0, KEEP).astype(jnp.int32)
    attn_w = draw_attn_w(jax.random.fold_in(arg_keys[12], 71), 0)
    mlp_w = draw_mlp_w(jax.random.fold_in(arg_keys[12], 71), 0)
    vectors = draw_vectors(jax.random.fold_in(arg_keys[12], 71), 0)
    attn_m = draw_attn_m(jax.random.fold_in(arg_keys[12], 71), 0)
    mlp_m = draw_mlp_m(jax.random.fold_in(arg_keys[12], 71), 0)
    small_m = draw_small_m(jax.random.fold_in(arg_keys[12], 71), 0)
    attn_v = draw_attn_v(jax.random.fold_in(arg_keys[12], 71), 0)
    mlp_v = draw_mlp_v(jax.random.fold_in(arg_keys[12], 71), 0)
    small_v = draw_small_v(jax.random.fold_in(arg_keys[12], 71), 0)
    return dict(tokens=tokens, out_grad=out_grad, kept_count=kept_count, attn_w=attn_w, mlp_w=mlp_w, vectors=vectors, attn_m=attn_m, mlp_m=mlp_m, small_m=small_m, attn_v=attn_v, mlp_v=mlp_v, small_v=small_v)


@jax.custom_vjp
def low(v):
    return lax.optimization_barrier(v.astype(jnp.bfloat16)).astype(jnp.float32)

@jax.custom_vjp
def low_back(v):
    return v

def low_keep(v):
    return (low(v), None)

def low_pass(kept, grad):
    return (grad,)

def back_keep(v):
    return (v, None)

def back_low(kept, grad):
    return (low(grad),)
low.defvjp(low_keep, low_pass)
low_back.defvjp(back_keep, back_low)
EPS_NORM = 1e-06
MASKED = -1000000000.0
PRECISE = lax.Precision.HIGHEST
BETA_ONE = 0.9
BETA_TWO = 0.999
EPS_ADAM = 1e-08

def normalize(values):
    average = lax.optimization_barrier(jnp.mean(values, axis=-1, keepdims=True))
    centred = values - average
    inverse = lax.rsqrt(lax.optimization_barrier(jnp.mean(centred * centred, axis=-1, keepdims=True)) + EPS_NORM)
    return centred * inverse

def gelu_exact(values):
    return jax.nn.gelu(values, approximate=False)

def block_layer(attn_low, mlp_low, small_low, block_in, block_valid):
    image_count = block_in.shape[0]
    slot_count = block_in.shape[1]
    total_rows = image_count * slot_count
    inputs = block_in.reshape(total_rows, D)
    valid_rows = block_valid.reshape(total_rows, 1)
    key_shift = jnp.where(block_valid > 0.5, 0.0, MASKED)[:, None, None, :]
    gain_one, shift_one = (small_low[:, 0], small_low[:, 1])
    query_bias, value_bias, out_bias = (small_low[:, 2], small_low[:, 3], small_low[:, 4])
    gain_two, shift_two, down_bias = (small_low[:, 5], small_low[:, 6], small_low[:, 7])
    up_bias = small_low[:, 8:12].T.reshape(FF)
    hidden_one = low(normalize(inputs) * gain_one + shift_one)
    qkv_bias = jnp.concatenate([query_bias, jnp.zeros_like(query_bias), value_bias])
    projected = low_back(low(jnp.dot(hidden_one, attn_low[:, :3 * D], precision=PRECISE) + qkv_bias))
    projected = projected.reshape(image_count, slot_count, 3, HEADS, HEAD_DIM)
    queries, key_rows, values = (projected[:, :, 0], projected[:, :, 1], projected[:, :, 2])
    score_scale = HEAD_DIM ** (-0.5)
    scores = low_back(jnp.einsum('ishd,ithd->ihst', queries, key_rows, precision=PRECISE) * score_scale + key_shift)
    attn_probs = jax.nn.softmax(scores, axis=-1)
    attn_mixed = jnp.einsum('ihst,ithd->ishd', low(attn_probs), values, precision=PRECISE).reshape(total_rows, D)
    attn_mixed = low_back(low(attn_mixed))
    branch = low_back(jnp.dot(attn_mixed, attn_low[:, 3 * D:], precision=PRECISE) + out_bias)
    middle = inputs + branch
    hidden_two = low(normalize(middle) * gain_two + shift_two)
    pre_act = low_back(jnp.dot(hidden_two, mlp_low[:, :FF], precision=PRECISE) + up_bias)
    act_low = low(gelu_exact(pre_act))
    down_out = low_back(jnp.dot(act_low, mlp_low[:, FF:].T, precision=PRECISE) + down_bias)
    return ((middle + down_out) * valid_rows).reshape(image_count, slot_count, D)

def adam_update(weight, first_mom, second_mom, gradient, rate, decay):
    first_new = BETA_ONE * first_mom + (1.0 - BETA_ONE) * gradient
    second_new = BETA_TWO * second_mom + (1.0 - BETA_TWO) * gradient * gradient
    first_hat = first_new / (1.0 - BETA_ONE ** STEP)
    second_hat = second_new / (1.0 - BETA_TWO ** STEP)
    weight_new = weight - rate * (first_hat / (jnp.sqrt(second_hat) + EPS_ADAM) + decay * weight)
    return (gradient, first_new, second_new, weight_new, weight_new.astype(jnp.bfloat16))

def reference(tokens, out_grad, kept_count, attn_w, mlp_w, vectors, attn_m, mlp_m, small_m, attn_v, mlp_v, small_v):
    positions = jnp.arange(SLOTS, dtype=jnp.int32)
    valid_mask = (positions[None, :] < (BUF + kept_count)[:, None]).astype(jnp.float32)
    block_count = IMAGES // 16

    def whole_layer(attn_full, mlp_full, small_full, inputs):
        attn_low, mlp_low, small_low = (low(attn_full), low(mlp_full), low(small_full))
        blocks_in = inputs.reshape(block_count, 16, SLOTS, D)
        blocks_valid = valid_mask.reshape(block_count, 16, SLOTS)

        def one_block(state_in, pieces):
            return (state_in, jax.checkpoint(block_layer)(attn_low, mlp_low, small_low, pieces[0], pieces[1]))
        _, outputs = lax.scan(one_block, jnp.zeros((), jnp.float32), (blocks_in, blocks_valid))
        return outputs.reshape(IMAGES, SLOTS, D)
    result, pullback = jax.vjp(whole_layer, attn_w, mlp_w, vectors, tokens.astype(jnp.float32))
    attn_sum, mlp_sum, small_sum, input_sum = pullback(out_grad.astype(jnp.float32))
    attn_out = adam_update(attn_w, attn_m, attn_v, attn_sum / IMAGES, 0.1, 0.05)
    mlp_out = adam_update(mlp_w, mlp_m, mlp_v, mlp_sum / IMAGES, 0.05, 0.05)
    small_out = adam_update(vectors, small_m, small_v, small_sum / IMAGES, 1.0, 0.0)
    return (result.astype(jnp.bfloat16), input_sum.astype(jnp.bfloat16), attn_out[0], attn_out[1], attn_out[2], attn_out[3], attn_out[4], mlp_out[0], mlp_out[1], mlp_out[2], mlp_out[3], mlp_out[4], small_out[0], small_out[1], small_out[2], small_out[3], small_out[4])
```

```python
import jax
import jax.numpy as jnp
from jax import lax
from jax.experimental import pallas as pl
from jax.experimental.pallas import tpu as pltpu
from jax.sharding import PartitionSpec as P

D = 1024
HEADS = 16
HEAD_DIM = 64
FF = 4096
BUF = 64
STEP = 10
BLOCKS = 4
BLOCK = D // BLOCKS
PARTS = 4
PART = FF // PARTS
GROUP = 4
GROUP_W = GROUP * HEAD_DIM

EPS_NORM = 1e-06
MASKED = -1000000000.0
BETA_ONE = 0.9
BETA_TWO = 0.999
EPS_ADAM = 1e-08

BF16 = jnp.bfloat16
F32 = jnp.float32
MIB = 1 << 20


def normalize(values):
    average = jnp.mean(values, axis=-1, keepdims=True)
    centred = values - average
    inverse = lax.rsqrt(jnp.mean(centred * centred, axis=-1, keepdims=True) + EPS_NORM)
    return (centred * inverse, inverse)


def norm_back(upstream, normed, inverse):
    first_term = jnp.mean(upstream, axis=-1, keepdims=True)
    second_term = normed * jnp.mean(upstream * normed, axis=-1, keepdims=True)
    return inverse * (upstream - first_term - second_term)


def dot(left, right):
    return jnp.dot(left, right, preferred_element_type=F32)


def dot_nt(left, right):
    return lax.dot_general(left, right, (((1,), (1,)), ((), ())), preferred_element_type=F32)


def dot_tn(left, right):
    return lax.dot_general(left, right, (((0,), (0,)), ((), ())), preferred_element_type=F32)


def gelu_pair(values):
    size = jnp.abs(values)
    denominator = 1.0 + size * (0.3275911 * 0.7071067811865476)
    ratio = pl.reciprocal(denominator, approx=True)
    ratio = ratio * (2.0 - denominator * ratio)
    bell = jnp.exp(values * values * (-0.5))
    poly = 0.5 * 1.061405429 * ratio - 0.5 * 1.453152027
    poly = poly * ratio + 0.5 * 1.421413741
    poly = poly * ratio - 0.5 * 0.284496736
    poly = poly * ratio + 0.5 * 0.254829592
    tail = poly * ratio * bell
    below = jnp.where(values >= 0, 1.0 - tail, tail)
    return (values * below, below + values * bell * 0.3989422804014327)


def whole(array):
    rank = len(array.shape)
    return pl.BlockSpec(array.shape, lambda *_: (0,) * rank, pipeline_mode=pl.Buffered(1))


def params(limit):
    return pltpu.CompilerParams(vmem_limit_bytes=limit * MIB)


def cost(flops, nbytes):
    return pl.CostEstimate(flops=int(flops), bytes_accessed=int(nbytes), transcendentals=0)


def place(order_ref, target, pieces):
    for j, piece in enumerate(pieces):
        at = pl.multiple_of(order_ref[j] * BLOCK, BLOCK)
        target[pl.ds(at, BLOCK), :] = piece[...]


def heads_apart(values, scale=None):
    lane = lax.broadcasted_iota(jnp.int32, values.shape, 1) // HEAD_DIM
    if scale is not None:
        values = values * jnp.asarray(scale, values.dtype)
    zero = jnp.zeros_like(values)
    return jnp.concatenate([jnp.where(lane == h, values, zero) for h in range(GROUP)], axis=0)


def heads_together(values, slots):
    lane = lax.broadcasted_iota(jnp.int32, (slots, GROUP_W), 1) // HEAD_DIM
    out = values[:slots]
    for h in range(1, GROUP):
        out = jnp.where(lane == h, values[h * slots : (h + 1) * slots], out)
    return out


def probs_of(keys, queries_apart, shift):
    scores = dot_nt(keys, queries_apart) + shift
    scores = jnp.exp(scores - jnp.max(scores, axis=0, keepdims=True))
    return scores * (1.0 / jnp.sum(scores, axis=0, keepdims=True))


def key_shift(kept, slots):
    at = lax.broadcasted_iota(jnp.int32, (slots, 1), 0)
    return jnp.where(at < BUF + kept, 0.0, MASKED).astype(F32)


def attn_forward(order, kept, x, wqkv, wo, vec):
    images, slots, _ = x.shape
    rows = images * slots

    def body(order_ref, kept_ref, x_ref, *refs):
        wq_refs, wo_refs = refs[:BLOCKS], refs[BLOCKS : 2 * BLOCKS]
        vec_ref, h1_ref, qkv_ref, mixed_ref, middle_ref, h2_ref, wq_s, wo_s = refs[2 * BLOCKS :]
        image = pl.program_id(0)

        @pl.when(image == 0)
        def _():
            place(order_ref, wq_s, wq_refs)
            place(order_ref, wo_s, wo_refs)

        inputs = x_ref[0].astype(F32)
        normed, _ = normalize(inputs)
        hidden = (normed * vec_ref[0:1, :] + vec_ref[1:2, :]).astype(BF16)
        h1_ref[...] = hidden
        shift = key_shift(kept_ref[image], slots)
        for g in range(HEADS // GROUP):
            at = g * GROUP_W
            span = slice(at, at + GROUP_W)
            q = (dot(hidden, wq_s[:, span]) + vec_ref[2:3, span]).astype(BF16)
            k = dot(hidden, wq_s[:, D + at : D + at + GROUP_W]).astype(BF16)
            v = (
                dot(hidden, wq_s[:, 2 * D + at : 2 * D + at + GROUP_W]) + vec_ref[3:4, span]
            ).astype(BF16)
            qkv_ref[:, span] = q
            qkv_ref[:, D + at : D + at + GROUP_W] = k
            qkv_ref[:, 2 * D + at : 2 * D + at + GROUP_W] = v
            probs = probs_of(k, heads_apart(q, HEAD_DIM**-0.5), shift).astype(BF16)
            mixed_ref[:, span] = heads_together(dot_tn(probs, v), slots).astype(BF16)
        middle = inputs + dot(mixed_ref[...], wo_s[...]) + vec_ref[4:5, :]
        middle_ref[...] = middle
        normed, _ = normalize(middle)
        h2_ref[...] = (normed * vec_ref[5:6, :] + vec_ref[6:7, :]).astype(BF16)

    row = lambda width: pl.BlockSpec((slots, width), lambda i, *_: (i, 0))
    return pl.pallas_call(
        body,
        grid_spec=pltpu.PrefetchScalarGridSpec(
            num_scalar_prefetch=2,
            grid=(images,),
            in_specs=[pl.BlockSpec((1, slots, D), lambda i, *_: (i, 0, 0))]
            + [whole(w) for w in wqkv]
            + [whole(w) for w in wo]
            + [whole(vec)],
            out_specs=[row(D), row(3 * D), row(D), row(D), row(D)],
            scratch_shapes=[pltpu.VMEM((D, 3 * D), BF16), pltpu.VMEM((D, D), BF16)],
        ),
        out_shape=[
            jax.ShapeDtypeStruct((rows, D), BF16),
            jax.ShapeDtypeStruct((rows, 3 * D), BF16),
            jax.ShapeDtypeStruct((rows, D), BF16),
            jax.ShapeDtypeStruct((rows, D), F32),
            jax.ShapeDtypeStruct((rows, D), BF16),
        ],
        compiler_params=params(40),
        cost_estimate=cost(12 * rows * D * D, 30 * MIB),
        name="attn_forward",
    )(order, kept, x, *wqkv, *wo, vec)


def mlp_part(order, h2, h2t, dm, dmt, wup, wdn, bu, width=256):
    rows = h2.shape[0]
    steps = PART // width

    def body(order_ref, h2_ref, h2t_ref, dm_ref, dmt_ref, *refs):
        up_refs, dn_refs = refs[:BLOCKS], refs[BLOCKS : 2 * BLOCKS]
        bu_ref, act_ref, dpre_ref, ups, upk, dns, dnk, gbu_ref, up_s, dn_s = refs[2 * BLOCKS :]
        place(order_ref, up_s, up_refs)
        place(order_ref, dn_s, dn_refs)
        pre = dot(h2_ref[...], up_s[...]) + bu_ref[...]
        act, slope = gelu_pair(pre)
        act = act.astype(BF16)
        act_ref[...] = act
        dpre = (dot(dm_ref[...], dn_s[...]) * slope).astype(BF16)
        dpre_ref[...] = dpre
        gbu_ref[...] = jnp.sum(dpre.astype(F32), axis=0, keepdims=True)
        for left_ref, right, keep, send in ((dmt_ref, act, dnk, dns), (h2t_ref, dpre, upk, ups)):
            for j in range(BLOCKS):
                at = pl.multiple_of(order_ref[j] * BLOCK, BLOCK)
                grad = dot(left_ref[pl.ds(at, BLOCK), :rows], right).astype(BF16)
                (send if j % 2 else keep)[j // 2] = grad

    weight = pl.BlockSpec((BLOCK, width), lambda i, *_: (0, i))
    column = pl.BlockSpec((rows, width), lambda i, *_: (0, i))
    grads = pl.BlockSpec((2, BLOCK, width), lambda i, *_: (0, 0, i))
    one = pl.BlockSpec((1, width), lambda i, *_: (0, i))
    return pl.pallas_call(
        body,
        grid_spec=pltpu.PrefetchScalarGridSpec(
            num_scalar_prefetch=1,
            grid=(steps,),
            in_specs=[whole(a) for a in (h2, h2t, dm, dmt)] + [weight] * (2 * BLOCKS) + [one],
            out_specs=[column] * 2 + [grads] * 4 + [one],
            scratch_shapes=[pltpu.VMEM((D, width), BF16)] * 2,
        ),
        out_shape=[jax.ShapeDtypeStruct((rows, PART), BF16)] * 2
        + [jax.ShapeDtypeStruct((2, BLOCK, PART), BF16)] * 4
        + [jax.ShapeDtypeStruct((1, PART), F32)],
        compiler_params=params(30),
        cost_estimate=cost(8 * rows * D * PART, 12 * MIB),
        name="mlp_part",
    )(order, h2, h2t, dm, dmt, *wup, *wdn, bu)


def mlp_back(order, dpres, wups, middle, gy, vec):
    rows = middle.shape[0]

    def body(order_ref, *refs):
        dpre_refs, refs = refs[:PARTS], refs[PARTS:]
        up_refs, refs = refs[: PARTS * BLOCKS], refs[PARTS * BLOCKS :]
        middle_ref, gy_ref, vec_ref, dmid_ref, da_ref, sums_ref, acc = refs
        part = pl.program_id(0)
        for p in range(PARTS):

            @pl.when(part == p)
            def _():
                for j in range(BLOCKS):
                    at = pl.multiple_of(order_ref[j] * BLOCK, BLOCK)
                    term = dot_nt(dpre_refs[p][...], up_refs[p * BLOCKS + j][...])
                    if p == 0:
                        acc[:, pl.ds(at, BLOCK)] = term
                    else:
                        acc[:, pl.ds(at, BLOCK)] += term

        @pl.when(part == PARTS - 1)
        def _():
            gain, shift, bias = (jnp.zeros((1, D), F32) for _ in range(3))
            step = rows // 6
            for r in range(0, rows, step):
                span = slice(r, r + step)
                dh2 = acc[span, :]
                normed, inverse = normalize(middle_ref[span, :])
                gain += jnp.sum(dh2 * normed, axis=0, keepdims=True)
                shift += jnp.sum(dh2, axis=0, keepdims=True)
                dmid = norm_back(dh2 * vec_ref[5:6, :], normed, inverse) + gy_ref[span, :].astype(F32)
                dmid_ref[span, :] = dmid
                da = dmid.astype(BF16)
                da_ref[span, :] = da
                bias += jnp.sum(da.astype(F32), axis=0, keepdims=True)
            sums_ref[...] = jnp.concatenate([gain, shift, bias, jnp.zeros((5, D), F32)], axis=0)

    def once(array, p):
        return pl.BlockSpec(array.shape, lambda i, *_: (0, 0), pipeline_mode=pl.Buffered(1))

    flat = [w for part in wups for w in part]
    ins = [*dpres, *flat, middle, gy, vec]
    return pl.pallas_call(
        body,
        grid_spec=pltpu.PrefetchScalarGridSpec(
            num_scalar_prefetch=1,
            grid=(PARTS,),
            in_specs=[whole(a) for a in ins],
            out_specs=[
                pl.BlockSpec((rows, D), lambda i, *_: (0, 0)),
                pl.BlockSpec((rows, D), lambda i, *_: (0, 0)),
                pl.BlockSpec((8, D), lambda i, *_: (0, 0)),
            ],
            scratch_shapes=[pltpu.VMEM((rows, D), F32)],
        ),
        out_shape=[
            jax.ShapeDtypeStruct((rows, D), F32),
            jax.ShapeDtypeStruct((rows, D), BF16),
            jax.ShapeDtypeStruct((8, D), F32),
        ],
        compiler_params=params(50),
        cost_estimate=cost(2 * rows * D * FF, 30 * MIB),
        name="mlp_back",
    )(order, *ins)


def mlp_out(order, acts, wdns, middle, valid, vec):
    rows = middle.shape[0]

    def body(order_ref, *refs):
        act_refs, refs = refs[:PARTS], refs[PARTS:]
        dn_refs, refs = refs[: PARTS * BLOCKS], refs[PARTS * BLOCKS :]
        middle_ref, valid_ref, vec_ref, out_ref = refs
        for j in range(BLOCKS):

            @pl.when(pl.program_id(0) == j)
            def _():
                at = pl.multiple_of(order_ref[j] * BLOCK, BLOCK)
                total = middle_ref[:, pl.ds(at, BLOCK)] + vec_ref[7:8, pl.ds(at, BLOCK)]
                for p in range(PARTS):
                    total = total + dot_nt(act_refs[p][...], dn_refs[p * BLOCKS + j][...])
                out_ref[:, pl.ds(at, BLOCK)] = (total * valid_ref[...]).astype(BF16)

    flat = [w for part in wdns for w in part]
    ins = [*acts, *flat, middle, valid, vec]
    return pl.pallas_call(
        body,
        grid_spec=pltpu.PrefetchScalarGridSpec(
            num_scalar_prefetch=1,
            grid=(BLOCKS,),
            in_specs=[whole(a) for a in ins],
            out_specs=pl.BlockSpec((rows, D), lambda i, *_: (0, 0)),
        ),
        out_shape=jax.ShapeDtypeStruct((rows, D), BF16),
        compiler_params=params(50),
        cost_estimate=cost(2 * rows * D * FF, 24 * MIB),
        name="mlp_out",
    )(order, *ins)


def attn_back(order, kept, da, wo, qkv, slots):
    rows = da.shape[0]
    images = rows // slots

    def body(order_ref, kept_ref, da_ref, *refs):
        wo_refs, (qkv_ref, dqkv_ref, sums_ref, wo_s) = refs[:BLOCKS], refs[BLOCKS:]
        image = pl.program_id(0)

        @pl.when(image == 0)
        def _():
            place(order_ref, wo_s, wo_refs)
            sums_ref[...] = jnp.zeros_like(sums_ref)

        shift = key_shift(kept_ref[image], slots)
        da = da_ref[...]
        scale = HEAD_DIM**-0.5
        for g in range(HEADS // GROUP):
            at = g * GROUP_W
            spans = [slice(n * D + at, n * D + at + GROUP_W) for n in range(3)]
            q, k, v = (qkv_ref[:, span] for span in spans)
            dmix = dot_nt(da, wo_s[at : at + GROUP_W, :]).astype(BF16)
            apart = heads_apart(q, scale)
            probs = probs_of(k, apart, shift)
            dmix_apart = heads_apart(dmix)
            dv = dot(probs.astype(BF16), dmix_apart).astype(BF16)
            dprob = dot_nt(v, dmix_apart)
            product = probs * dprob
            dsc = (product - probs * jnp.sum(product, axis=0, keepdims=True)).astype(BF16)
            dk = dot(dsc, apart).astype(BF16)
            dq = (heads_together(dot_tn(dsc, k), slots) * scale).astype(BF16)
            for n, grad in enumerate((dq, dk, dv)):
                dqkv_ref[:, spans[n]] = grad
                if n != 1:
                    sums_ref[n : n + 1, at : at + GROUP_W] += jnp.sum(
                        grad.astype(F32), axis=0, keepdims=True
                    )

    row = lambda width: pl.BlockSpec((slots, width), lambda i, *_: (i, 0))
    return pl.pallas_call(
        body,
        grid_spec=pltpu.PrefetchScalarGridSpec(
            num_scalar_prefetch=2,
            grid=(images,),
            in_specs=[row(D)] + [whole(w) for w in wo] + [row(3 * D)],
            out_specs=[row(3 * D), pl.BlockSpec((8, D), lambda i, *_: (0, 0))],
            scratch_shapes=[pltpu.VMEM((D, D), BF16)],
        ),
        out_shape=[
            jax.ShapeDtypeStruct((rows, 3 * D), BF16),
            jax.ShapeDtypeStruct((8, D), F32),
        ],
        compiler_params=params(30),
        cost_estimate=cost(8 * rows * D * D, 18 * MIB),
        name="attn_back",
    )(order, kept, da, *wo, qkv)


def input_back(order, dqkv, wqkv, x, dmid, vec):
    images, slots, _ = x.shape
    rows = images * slots

    def body(order_ref, dqkv_ref, *refs):
        wq_refs = refs[:BLOCKS]
        x_ref, dmid_ref, vec_ref, out_ref, sums_ref, acc = refs[BLOCKS:]

        @pl.when(pl.program_id(0) == 0)
        def _():
            sums_ref[...] = jnp.zeros_like(sums_ref)

        grad = dqkv_ref[...]
        for j in range(BLOCKS):
            at = pl.multiple_of(order_ref[j] * BLOCK, BLOCK)
            acc[:, pl.ds(at, BLOCK)] = dot_nt(grad, wq_refs[j][...])
        dh1 = acc[...]
        normed, inverse = normalize(x_ref[0].astype(F32))
        sums_ref[0:1, :] += jnp.sum(dh1 * normed, axis=0, keepdims=True)
        sums_ref[1:2, :] += jnp.sum(dh1, axis=0, keepdims=True)
        total = norm_back(dh1 * vec_ref[0:1, :], normed, inverse) + dmid_ref[...]
        out_ref[0] = total.astype(BF16)

    row = lambda width: pl.BlockSpec((slots, width), lambda i, *_: (i, 0))
    image = pl.BlockSpec((1, slots, D), lambda i, *_: (i, 0, 0))
    return pl.pallas_call(
        body,
        grid_spec=pltpu.PrefetchScalarGridSpec(
            num_scalar_prefetch=1,
            grid=(images,),
            in_specs=[row(3 * D)] + [whole(w) for w in wqkv] + [image, row(D), whole(vec)],
            out_specs=[image, pl.BlockSpec((8, D), lambda i, *_: (0, 0))],
            scratch_shapes=[pltpu.VMEM((slots, D), F32)],
        ),
        out_shape=[
            jax.ShapeDtypeStruct((images, slots, D), BF16),
            jax.ShapeDtypeStruct((8, D), F32),
        ],
        compiler_params=params(30),
        cost_estimate=cost(6 * rows * D * D, 24 * MIB),
        name="input_back",
    )(order, dqkv, *wqkv, x, dmid, vec)


def weight_grad(order, left_t, right, width=512):
    rows, columns = right.shape

    def body(order_ref, left_ref, right_ref, send, keep):
        for j in range(BLOCKS):
            at = pl.multiple_of(order_ref[j] * BLOCK, BLOCK)
            grad = dot(left_ref[pl.ds(at, BLOCK), :rows], right_ref[...]).astype(BF16)
            (send if j % 2 else keep)[j // 2] = grad

    grads = pl.BlockSpec((2, BLOCK, width), lambda i, *_: (0, 0, i))
    return pl.pallas_call(
        body,
        grid_spec=pltpu.PrefetchScalarGridSpec(
            num_scalar_prefetch=1,
            grid=(columns // width,),
            in_specs=[whole(left_t), pl.BlockSpec((rows, width), lambda i, *_: (0, i))],
            out_specs=[grads] * 2,
        ),
        out_shape=[jax.ShapeDtypeStruct((2, BLOCK, columns), BF16)] * 2,
        compiler_params=params(30),
        cost_estimate=cost(2 * rows * D * columns, 12 * MIB),
        name="weight_grad",
    )(order, left_t, right)


def transposed(values):
    rows = values.shape[0]
    return jnp.pad(values.T, ((0, 0), (0, -rows % 256)))


def swap(values, axis, bit):
    size = lax.axis_size(axis)
    return lax.ppermute(values, axis, [(i, i ^ bit) for i in range(size)])


def my_bit(axis, bit):
    return (lax.axis_index(axis) & bit) != 0


def bits_of(size):
    return [1 << n for n in range(size.bit_length() - 1)]


class Distances:
    def __init__(self):
        self.shards = lax.axis_size("shard")
        self.replicas = lax.axis_size("replica")
        self.direct = self.shards == BLOCKS and self.replicas & (self.replicas - 1) == 0
        index = jnp.arange(BLOCKS, dtype=jnp.int32)
        self.order = index ^ lax.axis_index("shard") if self.direct else index

    def gather(self, own):
        if not self.direct:
            full = lax.all_gather(own, "shard", axis=0, tiled=True)
            return [full[j * BLOCK : (j + 1) * BLOCK] for j in range(BLOCKS)]
        far = swap(own, "shard", 2)
        return [own, swap(own, "shard", 1), far, swap(far, "shard", 1)]

    def reduce(self, send, keep, stages):
        if not self.direct:
            full = jnp.stack([keep[0], send[0], keep[1], send[1]]).reshape(D, -1)
            part = lax.psum_scatter(full, "shard", scatter_dimension=0, tiled=True)
            return lax.psum(part, "replica")
        now = keep.astype(F32) + swap(send, "shard", 1).astype(F32)
        now = now.astype(BF16)
        taken = []
        for axis, bit in stages:
            if axis == "shard":
                now = (now[:1].astype(F32) + swap(now[1:], axis, bit).astype(F32)).astype(BF16)
                continue
            half = now.shape[1] // 2
            up = my_bit(axis, bit).astype(jnp.int32)
            mine = lax.dynamic_slice_in_dim(now, up * half, half, 1)
            other = lax.dynamic_slice_in_dim(now, (1 - up) * half, half, 1)
            now = (mine.astype(F32) + swap(other, axis, bit).astype(F32)).astype(BF16)
            taken.append((axis, bit))
        now = now[0]
        for axis, bit in reversed(taken):
            other = swap(now, axis, bit)
            now = jnp.where(
                my_bit(axis, bit),
                jnp.concatenate([other, now], axis=0),
                jnp.concatenate([now, other], axis=0),
            )
        return now

    def total(self, values):
        if not self.direct:
            return lax.psum(values, ("replica", "shard"))
        for axis, size in (("shard", self.shards), ("replica", self.replicas)):
            for bit in bits_of(size):
                values = values + swap(values, axis, bit)
        return values

    def stages(self, first):
        far = [("shard", 2)]
        rest = [("replica", bit) for bit in bits_of(self.replicas)]
        return far + rest if first == "shard" else rest + far


def adam_update(weight, first_mom, second_mom, gradient, rate, decay):
    first_new = BETA_ONE * first_mom + (1.0 - BETA_ONE) * gradient
    second_new = BETA_TWO * second_mom + (1.0 - BETA_TWO) * gradient * gradient
    first_hat = first_new / (1.0 - BETA_ONE**STEP)
    second_hat = second_new / (1.0 - BETA_TWO**STEP)
    weight_new = weight - rate * (first_hat / (jnp.sqrt(second_hat) + EPS_ADAM) + decay * weight)
    return (gradient, first_new, second_new, weight_new, weight_new.astype(BF16))


def on_device(
    tokens,
    out_grad,
    kept_count,
    attn_w,
    mlp_w,
    vectors,
    attn_m,
    mlp_m,
    small_m,
    attn_v,
    mlp_v,
    small_v,
):
    images, slots, _ = tokens.shape
    rows = images * slots
    links = Distances()
    order = links.order
    owned = vectors.shape[0]

    small_low = jnp.pad(vectors.astype(BF16).T, ((0, 4), (0, 0)))
    if links.direct:
        pieces = links.gather(small_low)
        stacked = jnp.stack(pieces)[order]
        small_full = stacked.transpose(1, 0, 2).reshape(16, D)
    else:
        small_full = lax.all_gather(small_low, "shard", axis=1, tiled=True)
    vec = small_full.astype(F32)
    wqkv = links.gather(attn_w[:, : 3 * D].astype(BF16))
    wo = links.gather(attn_w[:, 3 * D :].astype(BF16))
    wups, wdns = [], []
    for p in range(PARTS):
        span = slice(p * PART, (p + 1) * PART)
        wups.append(links.gather(mlp_w[:, :FF][:, span].astype(BF16)))
        wdns.append(links.gather(mlp_w[:, FF:][:, span].astype(BF16)))

    h1, qkv, mixed, middle, h2 = attn_forward(order, kept_count, tokens, wqkv, wo, vec)

    at = jnp.arange(slots, dtype=jnp.int32)
    valid = (at[None, :] < (BUF + kept_count)[:, None]).reshape(rows, 1)
    gy = jnp.where(valid, out_grad.reshape(rows, D), jnp.zeros((), BF16))
    gyt = transposed(gy)
    h2t = transposed(h2)
    acts, dpres, ups, dns, gbus = [], [], [], [], []
    for p in range(PARTS):
        act, dpre, up_send, up_keep, dn_send, dn_keep, gbu = mlp_part(
            order, h2, h2t, gy, gyt, wups[p], wdns[p], vec[8 + p : 9 + p]
        )
        acts.append(act)
        dpres.append(dpre)
        dns.append(links.reduce(dn_send, dn_keep, links.stages("shard")))
        ups.append(links.reduce(up_send, up_keep, links.stages("replica")))
        gbus.append(gbu)
    dmid, da, two_sums = mlp_back(order, dpres, wups, middle, gy, vec)

    out_send, out_keep = weight_grad(order, transposed(mixed), da)
    g_out = links.reduce(out_send, out_keep, links.stages("replica"))
    dqkv, qkv_sums = attn_back(order, kept_count, da, wo, qkv, slots)
    qkv_send, qkv_keep = weight_grad(order, transposed(h1), dqkv)
    g_qkv = links.reduce(qkv_send, qkv_keep, links.stages("shard"))
    in_grad, one_sums = input_back(order, dqkv, wqkv, tokens, dmid, vec)
    result = mlp_out(order, acts, wdns, middle, valid.astype(F32), vec)
    result = result.reshape(images, slots, D)

    g_down = jnp.sum(gy, axis=0, dtype=F32, keepdims=True)
    small = jnp.concatenate(
        [
            one_sums[0:2],
            qkv_sums[0:1],
            qkv_sums[2:3],
            two_sums[2:3],
            two_sums[0:2],
            g_down,
            *gbus,
            jnp.zeros((4, D), F32),
        ],
        axis=0,
    )
    small = links.total(small)
    small = lax.dynamic_slice_in_dim(small, lax.axis_index("shard") * owned, owned, 1)[:12].T

    image_total = images * links.replicas * links.shards
    attn_sum = jnp.concatenate([g_qkv, g_out], axis=1).astype(F32)
    mlp_sum = jnp.concatenate([*ups, *dns], axis=1).astype(F32)
    attn_out = adam_update(attn_w, attn_m, attn_v, attn_sum / image_total, 0.1, 0.05)
    mlp_out_ = adam_update(mlp_w, mlp_m, mlp_v, mlp_sum / image_total, 0.05, 0.05)
    small_out = adam_update(vectors, small_m, small_v, small / image_total, 1.0, 0.0)
    return (result, in_grad, *attn_out, *mlp_out_, *small_out)


def solution(mesh):
    tokens = P(("replica", "shard"), None, None)
    owned = P("shard", None)
    in_specs = (tokens, tokens, P(("replica", "shard")), *[owned] * 9)
    out_specs = (tokens, tokens, *[owned] * 15)
    return jax.shard_map(
        on_device, mesh=mesh, in_specs=in_specs, out_specs=out_specs, check_vma=False
    )
```

```python
import jax
import jax.numpy as jnp
from jax import lax
from jax.experimental import pallas as pl
from jax.experimental.pallas import tpu as pltpu
from jax.sharding import PartitionSpec as P

D = 1024
HEADS = 16
HEAD_DIM = 64
FF = 4096
BUF = 64
STEP = 10
BLOCKS = 4
BLOCK = D // BLOCKS
PARTS = 4
PART = FF // PARTS
GROUP = 4
GROUP_W = GROUP * HEAD_DIM

EPS_NORM = 1e-06
MASKED = -1000000000.0
BETA_ONE = 0.9
BETA_TWO = 0.999
EPS_ADAM = 1e-08

BF16 = jnp.bfloat16
F32 = jnp.float32
MIB = 1 << 20


def normalize(values):
    average = jnp.mean(values, axis=-1, keepdims=True)
    centred = values - average
    inverse = lax.rsqrt(jnp.mean(centred * centred, axis=-1, keepdims=True) + EPS_NORM)
    return (centred * inverse, inverse)


def norm_back(upstream, normed, inverse):
    first_term = jnp.mean(upstream, axis=-1, keepdims=True)
    second_term = normed * jnp.mean(upstream * normed, axis=-1, keepdims=True)
    return inverse * (upstream - first_term - second_term)


def dot(left, right):
    return jnp.dot(left, right, preferred_element_type=F32)


def dot_nt(left, right):
    return lax.dot_general(left, right, (((1,), (1,)), ((), ())), preferred_element_type=F32)


def dot_tn(left, right):
    return lax.dot_general(left, right, (((0,), (0,)), ((), ())), preferred_element_type=F32)


def gelu_pair(values):
    size = jnp.abs(values)
    denominator = 1.0 + size * (0.3275911 * 0.7071067811865476)
    ratio = pl.reciprocal(denominator, approx=True)
    ratio = ratio * (2.0 - denominator * ratio)
    bell = jnp.exp(values * values * (-0.5))
    poly = 0.5 * 1.061405429 * ratio - 0.5 * 1.453152027
    poly = poly * ratio + 0.5 * 1.421413741
    poly = poly * ratio - 0.5 * 0.284496736
    poly = poly * ratio + 0.5 * 0.254829592
    tail = poly * ratio * bell
    below = jnp.where(values >= 0, 1.0 - tail, tail)
    return (values * below, below + values * bell * 0.3989422804014327)


def whole(array):
    rank = len(array.shape)
    return pl.BlockSpec(array.shape, lambda *_: (0,) * rank, pipeline_mode=pl.Buffered(1))


def params(limit):
    return pltpu.CompilerParams(vmem_limit_bytes=limit * MIB)


def cost(flops, nbytes):
    return pl.CostEstimate(flops=int(flops), bytes_accessed=int(nbytes), transcendentals=0)


def call(body, *, scalars, ins, in_specs, outs, out_specs, grid, name, limit, work, scratch=(), after=(), aliases=None):
    first = len(scalars) + len(ins)
    ins = [
        pltpu.with_memory_space_constraint(a, pltpu.HBM)
        if a.size * a.dtype.itemsize >= MIB // 4
        else a
        for a in ins
    ]

    def with_after(*refs):
        body(*refs[:first], *refs[first + len(after) :])

    return pl.pallas_call(
        with_after,
        grid_spec=pltpu.PrefetchScalarGridSpec(
            num_scalar_prefetch=len(scalars),
            grid=grid,
            in_specs=[*in_specs, *[pl.BlockSpec(memory_space=pl.ANY)] * len(after)],
            out_specs=out_specs,
            scratch_shapes=list(scratch),
        ),
        out_shape=outs,
        input_output_aliases=aliases or {},
        compiler_params=params(limit),
        cost_estimate=cost(*work),
        name=name,
    )(*scalars, *ins, *after)


def like(shape, dtype):
    return pltpu.HBM(shape, dtype)


def place(order_ref, target, pieces):
    for j, piece in enumerate(pieces):
        at = pl.multiple_of(order_ref[j] * BLOCK, BLOCK)
        target[pl.ds(at, BLOCK), :] = piece[...]


ANY = pl.BlockSpec(memory_space=pl.ANY)


class Piece:
    def __init__(self, array, row, column):
        self.array, self.row, self.column = array, row, column

    def spec(self, width):
        return pl.BlockSpec(
            (BLOCK, width), lambda *_: (self.row, self.column), pipeline_mode=pl.Buffered(1)
        )

    def view(self, ref, width):
        return ref.at[
            self.row * BLOCK : (self.row + 1) * BLOCK,
            self.column * width : (self.column + 1) * width,
        ]


def arrays(pieces):
    return [piece.array for piece in pieces]


def heads_apart(values, scale=None):
    lane = lax.broadcasted_iota(jnp.int32, values.shape, 1) // HEAD_DIM
    if scale is not None:
        values = values * jnp.asarray(scale, values.dtype)
    zero = jnp.zeros_like(values)
    return jnp.concatenate([jnp.where(lane == h, values, zero) for h in range(GROUP)], axis=0)


def heads_together(values, slots):
    lane = lax.broadcasted_iota(jnp.int32, (slots, GROUP_W), 1) // HEAD_DIM
    out = values[:slots]
    for h in range(1, GROUP):
        out = jnp.where(lane == h, values[h * slots : (h + 1) * slots], out)
    return out


def probs_of(keys, queries_apart, shift):
    scores = dot_nt(keys, queries_apart) + shift
    scores = jnp.exp(scores - jnp.max(scores, axis=0, keepdims=True))
    return scores * (1.0 / jnp.sum(scores, axis=0, keepdims=True))


def key_shift(kept, slots):
    at = lax.broadcasted_iota(jnp.int32, (slots, 1), 0)
    return jnp.where(at < BUF + kept, 0.0, MASKED).astype(F32)


def row_spec(slots, width):
    return pl.BlockSpec((slots, width), lambda i, *_: (i, 0))


def qkv_forward(order, x, wqkv, vec, after, width=512):
    images, slots, _ = x.shape
    rows = images * slots

    def body(order_ref, x_ref, *refs):
        w_refs, (vec_ref, bias_ref, h1_ref, qkv_ref, w_s) = refs[:BLOCKS], refs[BLOCKS:]

        @pl.when(pl.program_id(0) == 0)
        def _():
            for n in range(images):
                normed, _ = normalize(x_ref[n].astype(F32))
                hidden = normed * vec_ref[0:1, :] + vec_ref[1:2, :]
                h1_ref[n * slots : (n + 1) * slots, :] = hidden.astype(BF16)

        place(order_ref, w_s, w_refs)
        qkv_ref[...] = (dot(h1_ref[...], w_s[...]) + bias_ref[...]).astype(BF16)

    bias = jnp.concatenate([vec[2:3], jnp.zeros_like(vec[2:3]), vec[3:4]], axis=1)
    return call(
        body,
        scalars=[order],
        ins=[x, *arrays(wqkv), vec, bias],
        in_specs=[whole(x)]
        + [pl.BlockSpec((BLOCK, width), lambda i, *_, row=w.row: (row, i)) for w in wqkv]
        + [whole(vec), pl.BlockSpec((1, width), lambda i, *_: (0, i))],
        outs=[like((rows, D), BF16), like((rows, 3 * D), BF16)],
        out_specs=[
            pl.BlockSpec((rows, D), lambda i, *_: (0, 0)),
            pl.BlockSpec((rows, width), lambda i, *_: (0, i)),
        ],
        scratch=[pltpu.VMEM((D, width), BF16)],
        grid=(3 * D // width,),
        name="qkv_forward",
        limit=30,
        work=(10 * rows * D * D, 18 * MIB),
        after=after,
    )


def attn_mix(kept, qkv, images, after):
    rows = qkv.shape[0]
    slots = rows // images

    def body(kept_ref, qkv_ref, mixed_ref):
        shift = key_shift(kept_ref[pl.program_id(0)], slots)
        for g in range(HEADS // GROUP):
            at = g * GROUP_W
            q, k, v = (qkv_ref[:, n * D + at : n * D + at + GROUP_W] for n in range(3))
            probs = probs_of(k, heads_apart(q, HEAD_DIM**-0.5), shift).astype(BF16)
            mixed_ref[:, at : at + GROUP_W] = heads_together(dot_tn(probs, v), slots).astype(BF16)

    return call(
        body,
        scalars=[kept],
        ins=[qkv],
        in_specs=[row_spec(slots, 3 * D)],
        outs=[like((rows, D), BF16)],
        out_specs=[row_spec(slots, D)],
        grid=(images,),
        name="attn_mix",
        limit=30,
        work=(14 * rows * D * D, 8 * MIB),
        after=after,
    )[0]


def out_project(order, x, mixed, wo, vec, after):
    images, slots, _ = x.shape
    rows = images * slots

    def body(order_ref, x_ref, mixed_ref, *refs):
        wo_refs, (vec_ref, middle_ref, h2_ref, wo_s) = refs[:BLOCKS], refs[BLOCKS:]

        @pl.when(pl.program_id(0) == 0)
        def _():
            place(order_ref, wo_s, wo_refs)

        branch = dot(mixed_ref[...], wo_s[...]) + vec_ref[4:5, :]
        for n in range(2):
            span = slice(n * slots, (n + 1) * slots)
            middle = x_ref[n].astype(F32) + branch[span]
            middle_ref[span, :] = middle
            normed, _ = normalize(middle)
            h2_ref[span, :] = (normed * vec_ref[5:6, :] + vec_ref[6:7, :]).astype(BF16)

    return call(
        body,
        scalars=[order],
        ins=[x, mixed, *arrays(wo), vec],
        in_specs=[pl.BlockSpec((2, slots, D), lambda i, *_: (i, 0, 0)), row_spec(2 * slots, D)]
        + [w.spec(D) for w in wo]
        + [whole(vec)],
        outs=[like((rows, D), F32), like((rows, D), BF16)],
        out_specs=[row_spec(2 * slots, D)] * 2,
        scratch=[pltpu.VMEM((D, D), BF16)],
        grid=(images // 2,),
        name="out_project",
        limit=30,
        work=(6 * rows * D * D, 12 * MIB),
        after=after,
    )


def mlp_part(order, h2, dm, wup, wdn, bu, after, width=512):
    rows = h2.shape[0]
    weights = [*wup, *wdn]

    def body(order_ref, h2_hbm, dm_hbm, *refs):
        weight_refs, (bu_ref, *outs, gbu_ref) = refs[: 2 * BLOCKS], refs[2 * BLOCKS : -10]
        h2_ref, dm_ref, up_s, dn_s, act_ref, dpre_ref, send, keep, in_sems, out_sems = refs[-10:]
        flying = []

        def put(n, source, index):
            copy = pltpu.make_async_copy(
                source.at[index], outs[n].at[index], out_sems.at[len(flying)]
            )
            copy.start()
            flying.append(copy)

        def fetch(n, source, target, first):
            copies = [pltpu.make_async_copy(source, target, in_sems.at[n])]
            for j in range(BLOCKS):
                at = pl.multiple_of(order_ref[j] * BLOCK, BLOCK)
                copies.append(
                    pltpu.make_async_copy(
                        weights[first + j].view(weight_refs[first + j], PART),
                        (dn_s if first else up_s).at[pl.ds(at, BLOCK), :],
                        in_sems.at[n + 1 + j],
                    )
                )
            for copy in copies:
                copy.start()
            return copies

        def arrive(copies):
            for copy in copies:
                copy.wait()

        ups = fetch(0, h2_hbm, h2_ref, 0)
        dns = fetch(1 + BLOCKS, dm_hbm, dm_ref, BLOCKS)

        def front(n, span):
            if n == 0:
                arrive(ups)
            pre = dot(h2_ref[...], up_s[:, span]) + bu_ref[:, span]
            if n == 0:
                arrive(dns)
            return (pre, dot(dm_ref[...], dn_s[:, span]))

        def middle(span, pre, dact):
            act, slope = gelu_pair(pre)
            act = act.astype(BF16)
            dpre = (dact * slope).astype(BF16)
            act_ref[:, span] = act
            dpre_ref[:, span] = dpre
            gbu_ref[:, span] = jnp.sum(dpre.astype(F32), axis=0, keepdims=True)
            return (act, dpre)

        def back(span, act, dpre):
            for first, left_ref, right in ((0, dm_ref, act), (PART, h2_ref, dpre)):
                there = slice(first + span.start, first + span.stop)
                for j in range(BLOCKS):
                    at = pl.multiple_of(order_ref[j] * BLOCK, BLOCK)
                    grad = dot_tn(left_ref[:, pl.ds(at, BLOCK)], right).astype(BF16)
                    (send if j % 2 else keep)[j // 2, :, there] = grad

        def out(span):
            put(0, act_ref, (slice(None), span))
            put(1, dpre_ref, (slice(None), span))
            for first in (0, PART):
                there = slice(first + span.start, first + span.stop)
                put(2, send, (slice(None), slice(None), there))
                put(3, keep, (slice(None), slice(None), there))

        spans = [slice(at, at + width) for at in range(0, PART, width)]
        fresh = front(0, spans[0])
        held = None
        for n, span in enumerate(spans):
            later = front(n + 1, spans[n + 1]) if n + 1 < len(spans) else None
            now = middle(span, *fresh)
            if held is not None:
                back(spans[n - 1], *held)
                out(spans[n - 1])
            held, fresh = now, later
        back(spans[-1], *held)
        out(spans[-1])
        for copy in flying:
            copy.wait()

    one = pl.BlockSpec((1, PART), lambda i, *_: (0, 0))
    return call(
        body,
        scalars=[order],
        ins=[h2, dm, *arrays(weights), bu],
        in_specs=[ANY] * (2 + len(weights)) + [whole(bu)],
        outs=[like((rows, PART), BF16)] * 2
        + [like((2, BLOCK, 2 * PART), BF16)] * 2
        + [like((1, PART), F32)],
        out_specs=[ANY] * 4 + [one],
        scratch=[pltpu.VMEM((rows, D), BF16)] * 2
        + [pltpu.VMEM((D, PART), BF16)] * 2
        + [pltpu.VMEM((rows, PART), BF16)] * 2
        + [pltpu.VMEM((2, BLOCK, 2 * PART), BF16)] * 2
        + [
            pltpu.SemaphoreType.DMA((2 + 2 * BLOCKS,)),
            pltpu.SemaphoreType.DMA((PART // width * 6,)),
        ],
        grid=(1,),
        name="mlp_part",
        limit=40,
        work=(12 * rows * D * PART, 12 * MIB),
        after=after,
    )


def streamed(order_ref, sides, side_refs, weights, weight_refs, side_s, weight_s, sems, use):
    def copies(p):
        slot = p % 2
        yield pltpu.make_async_copy(side_refs[p], side_s.at[slot], sems.at[slot, BLOCKS])
        for j in range(BLOCKS):
            at = pl.multiple_of(order_ref[j] * BLOCK, BLOCK)
            piece = weights[p][j]
            yield pltpu.make_async_copy(
                piece.view(weight_refs[p * BLOCKS + j], PART),
                weight_s.at[slot, pl.ds(at, BLOCK), :],
                sems.at[slot, j],
            )

    for copy in copies(0):
        copy.start()
    for p in range(PARTS):
        if p + 1 < PARTS:
            for copy in copies(p + 1):
                copy.start()
        for copy in copies(p):
            copy.wait()
        use(p, side_s[p % 2], weight_s[p % 2])


def stream_scratch(rows):
    return [
        pltpu.VMEM((2, rows, PART), BF16),
        pltpu.VMEM((2, D, PART), BF16),
        pltpu.SemaphoreType.DMA((2, BLOCKS + 1)),
        pltpu.VMEM((rows, D), F32),
        pltpu.VMEM((rows, D), F32),
        pltpu.SemaphoreType.DMA((1,)),
    ]


def mlp_back(order, dpres, wups, middle, gy, vec, mixed, after):
    rows = middle.shape[0]
    flat = [w for part in wups for w in part]

    def body(order_ref, *refs):
        dpre_refs, refs = refs[:PARTS], refs[PARTS:]
        up_refs, refs = refs[: PARTS * BLOCKS], refs[PARTS * BLOCKS :]
        middle_ref, gy_ref, vec_ref, mixed_ref, dmid_ref, da_ref, sums_ref, send, keep = refs[:9]
        side_s, weight_s, sems, acc, middle_s, middle_sem = refs[9:]

        def use(p, side, weight):
            if p == 0:
                pltpu.make_async_copy(middle_ref, middle_s, middle_sem.at[0]).start()
                acc[...] = dot_nt(side, weight)
            else:
                acc[...] += dot_nt(side, weight)

        streamed(order_ref, dpres, dpre_refs, wups, up_refs, side_s, weight_s, sems, use)
        pltpu.make_async_copy(middle_ref, middle_s, middle_sem.at[0]).wait()
        gain, shift, bias = (jnp.zeros((1, D), F32) for _ in range(3))
        step = rows // 6
        for r in range(0, rows, step):
            span = slice(r, r + step)
            dh2 = acc[span, :]
            normed, inverse = normalize(middle_s[span, :])
            gain += jnp.sum(dh2 * normed, axis=0, keepdims=True)
            shift += jnp.sum(dh2, axis=0, keepdims=True)
            dmid = norm_back(dh2 * vec_ref[5:6, :], normed, inverse) + gy_ref[span, :].astype(F32)
            dmid_ref[span, :] = dmid
            da = dmid.astype(BF16)
            da_ref[span, :] = da
            bias += jnp.sum(da.astype(F32), axis=0, keepdims=True)
        sums_ref[...] = jnp.concatenate([gain, shift, bias, jnp.zeros((5, D), F32)], axis=0)
        for j in range(BLOCKS):
            at = pl.multiple_of(order_ref[j] * BLOCK, BLOCK)
            grad = dot_tn(mixed_ref[:, pl.ds(at, BLOCK)], da_ref[...]).astype(BF16)
            (send if j % 2 else keep)[j // 2] = grad

    return call(
        body,
        scalars=[order],
        ins=[*dpres, *arrays(flat), middle, gy, vec, mixed],
        in_specs=[ANY] * (PARTS + len(flat) + 1) + [whole(gy), whole(vec), whole(mixed)],
        outs=[like((rows, D), F32), like((rows, D), BF16), like((8, D), F32)]
        + [like((2, BLOCK, D), BF16)] * 2,
        out_specs=[
            pl.BlockSpec((rows, D), lambda i, *_: (0, 0)),
            pl.BlockSpec((rows, D), lambda i, *_: (0, 0)),
            pl.BlockSpec((8, D), lambda i, *_: (0, 0)),
            pl.BlockSpec((2, BLOCK, D), lambda i, *_: (0, 0, 0)),
            pl.BlockSpec((2, BLOCK, D), lambda i, *_: (0, 0, 0)),
        ],
        scratch=stream_scratch(rows),
        grid=(1,),
        name="mlp_back",
        limit=40,
        work=(3 * rows * D * FF, 30 * MIB),
        after=after,
    )


def mlp_out(order, acts, wdns, middle, valid, vec, after):
    rows = middle.shape[0]
    flat = [w for part in wdns for w in part]

    def body(order_ref, *refs):
        act_refs, refs = refs[:PARTS], refs[PARTS:]
        dn_refs, refs = refs[: PARTS * BLOCKS], refs[PARTS * BLOCKS :]
        middle_ref, valid_ref, vec_ref, out_ref = refs[:4]
        side_s, weight_s, sems, acc, middle_s, middle_sem = refs[4:]

        def use(p, side, weight):
            if p == 0:
                pltpu.make_async_copy(middle_ref, middle_s, middle_sem.at[0]).start()
                acc[...] = dot_nt(side, weight)
            elif p + 1 < PARTS:
                acc[...] += dot_nt(side, weight)
            else:
                pltpu.make_async_copy(middle_ref, middle_s, middle_sem.at[0]).wait()
                total = acc[...] + dot_nt(side, weight) + middle_s[...] + vec_ref[7:8, :]
                out_ref[...] = (total * valid_ref[...]).astype(BF16)

        streamed(order_ref, acts, act_refs, wdns, dn_refs, side_s, weight_s, sems, use)

    return call(
        body,
        scalars=[order],
        ins=[*acts, *arrays(flat), middle, valid, vec],
        in_specs=[ANY] * (PARTS + len(flat) + 1) + [whole(valid), whole(vec)],
        outs=[like((rows, D), BF16)],
        out_specs=[pl.BlockSpec((rows, D), lambda i, *_: (0, 0))],
        scratch=stream_scratch(rows),
        grid=(1,),
        name="mlp_out",
        limit=40,
        work=(3 * rows * D * FF, 24 * MIB),
        after=after,
    )[0]


def attn_back(order, kept, da, wo, qkv, slots, first, count, before, after):
    rows = da.shape[0]

    def body(order_ref, kept_ref, da_ref, *refs):
        wo_refs, refs = refs[:BLOCKS], refs[BLOCKS:]
        qkv_ref, dqkv_ref, sums_ref, wo_s = refs[0], *refs[-3:]
        image = pl.program_id(0)

        @pl.when(image == 0)
        def _():
            place(order_ref, wo_s, wo_refs)
            sums_ref[...] = jnp.zeros_like(sums_ref)

        shift = key_shift(kept_ref[first + image], slots)
        da = da_ref[...]
        scale = HEAD_DIM**-0.5
        for g in range(HEADS // GROUP):
            at = g * GROUP_W
            spans = [slice(n * D + at, n * D + at + GROUP_W) for n in range(3)]
            q, k, v = (qkv_ref[:, span] for span in spans)
            dmix = dot_nt(da, wo_s[at : at + GROUP_W, :]).astype(BF16)
            apart = heads_apart(q, scale)
            probs = probs_of(k, apart, shift)
            dmix_apart = heads_apart(dmix)
            dv = dot(probs.astype(BF16), dmix_apart).astype(BF16)
            dprob = dot_nt(v, dmix_apart)
            product = probs * dprob
            dsc = (product - probs * jnp.sum(product, axis=0, keepdims=True)).astype(BF16)
            dk = dot(dsc, apart).astype(BF16)
            dq = (heads_together(dot_tn(dsc, k), slots) * scale).astype(BF16)
            for n, grad in enumerate((dq, dk, dv)):
                dqkv_ref[:, spans[n]] = grad
                if n != 1:
                    sums_ref[n : n + 1, at : at + GROUP_W] += jnp.sum(
                        grad.astype(F32), axis=0, keepdims=True
                    )

    row = lambda width: pl.BlockSpec((slots, width), lambda i, *_: (first + i, 0))
    extra = [] if before is None else [before]
    return call(
        body,
        scalars=[order, kept],
        ins=[da, *arrays(wo), qkv, *extra],
        in_specs=[row(D)]
        + [w.spec(D) for w in wo]
        + [row(3 * D)]
        + [pl.BlockSpec(memory_space=pl.ANY)] * len(extra),
        outs=[like((rows, 3 * D), BF16), like((8, D), F32)],
        out_specs=[row(3 * D), pl.BlockSpec((8, D), lambda i, *_: (0, 0))],
        scratch=[pltpu.VMEM((D, D), BF16)],
        grid=(count,),
        aliases={4 + BLOCKS: 0} if extra else None,
        name="attn_back",
        limit=30,
        work=(12 * rows * D * D, 18 * MIB),
        after=after,
    )


def input_back(order, dqkv, wqkv, x, dmid, vec, after):
    images, slots, _ = x.shape
    rows = images * slots

    def body(order_ref, dqkv_ref, *refs):
        wq_refs = refs[:BLOCKS]
        x_ref, dmid_ref, vec_ref, out_ref, sums_ref, acc = refs[BLOCKS:]

        @pl.when(pl.program_id(0) == 0)
        def _():
            sums_ref[...] = jnp.zeros_like(sums_ref)

        grad = dqkv_ref[...]
        for j in range(BLOCKS):
            at = pl.multiple_of(order_ref[j] * BLOCK, BLOCK)
            acc[:, pl.ds(at, BLOCK)] = dot_nt(grad, wq_refs[j][...])
        for n in range(2):
            dh1 = acc[n * slots : (n + 1) * slots, :]
            normed, inverse = normalize(x_ref[n].astype(F32))
            sums_ref[0:1, :] += jnp.sum(dh1 * normed, axis=0, keepdims=True)
            sums_ref[1:2, :] += jnp.sum(dh1, axis=0, keepdims=True)
            total = norm_back(dh1 * vec_ref[0:1, :], normed, inverse)
            out_ref[n] = (total + dmid_ref[n * slots : (n + 1) * slots, :]).astype(BF16)

    image = pl.BlockSpec((2, slots, D), lambda i, *_: (i, 0, 0))
    return call(
        body,
        scalars=[order],
        ins=[dqkv, *arrays(wqkv), x, dmid, vec],
        in_specs=[row_spec(2 * slots, 3 * D)]
        + [w.spec(3 * D) for w in wqkv]
        + [image, row_spec(2 * slots, D), whole(vec)],
        outs=[like((images, slots, D), BF16), like((8, D), F32)],
        out_specs=[image, pl.BlockSpec((8, D), lambda i, *_: (0, 0))],
        scratch=[pltpu.VMEM((2 * slots, D), F32)],
        grid=(images // 2,),
        name="input_back",
        limit=30,
        work=(8 * rows * D * D, 24 * MIB),
        after=after,
    )


def weight_grad(order, left, right, first, after, columns=D, width=512):
    rows = right.shape[0]
    at_block = first // width

    def body(order_ref, left_ref, right_ref, send, keep):
        for j in range(BLOCKS):
            at = pl.multiple_of(order_ref[j] * BLOCK, BLOCK)
            grad = dot_tn(left_ref[:, pl.ds(at, BLOCK)], right_ref[...]).astype(BF16)
            (send if j % 2 else keep)[j // 2] = grad

    grads = pl.BlockSpec((2, BLOCK, width), lambda i, *_: (0, 0, i))
    return call(
        body,
        scalars=[order],
        ins=[left, right],
        in_specs=[whole(left), pl.BlockSpec((rows, width), lambda i, *_: (0, at_block + i))],
        outs=[like((2, BLOCK, columns), BF16)] * 2,
        out_specs=[grads] * 2,
        grid=(columns // width,),
        name="weight_grad",
        limit=30,
        work=(3 * rows * D * columns, 12 * MIB),
        after=after,
    )


def adam_terms(weight, first_mom, second_mom, gradient, rate, decay):
    first_new = BETA_ONE * first_mom + (1.0 - BETA_ONE) * gradient
    second_new = BETA_TWO * second_mom + (1.0 - BETA_TWO) * gradient * gradient
    first_hat = first_new * (1.0 / (1.0 - BETA_ONE**STEP))
    second_hat = second_new * (1.0 / (1.0 - BETA_TWO**STEP))
    weight_new = weight - rate * (first_hat / (jnp.sqrt(second_hat) + EPS_ADAM) + decay * weight)
    return (gradient, first_new, second_new, weight_new, weight_new.astype(BF16))


def adam_part(total, first, columns, weight, first_mom, second_mom, count, rate, decay, before, after, width=512):
    rows = total.shape[0]
    steps = D // width

    def body(columns_ref, g_ref, w_ref, m_ref, v_ref, *refs):
        gradient = g_ref[...].astype(F32) * (1.0 / count)
        outs = adam_terms(w_ref[...], m_ref[...], v_ref[...], gradient, rate, decay)
        for ref, value in zip(refs[-6:], outs):
            ref[...] = value
        refs[-1][...] = jnp.zeros_like(refs[-1])

    there = pl.BlockSpec((rows, width), lambda i, n, where: (0, where[i] * steps + n))
    shape = weight.shape
    *outs, mark = call(
        body,
        scalars=[jnp.array(columns, jnp.int32)],
        ins=[total, weight, first_mom, second_mom, *before],
        in_specs=[pl.BlockSpec((rows, width), lambda i, n, where: (0, (first + i) * steps + n))]
        + [there] * 3
        + [ANY] * len(before),
        outs=[jax.ShapeDtypeStruct(shape, F32)] * 4
        + [jax.ShapeDtypeStruct(shape, BF16), jax.ShapeDtypeStruct((8, 128), F32)],
        out_specs=[there] * 5 + [pl.BlockSpec((8, 128), lambda i, n, where: (0, 0))],
        grid=(len(columns), steps),
        aliases={5 + n: n for n in range(len(before))},
        name="adam_part",
        limit=30,
        work=(3 * MIB * 1024 * len(columns), 10 * MIB),
        after=after,
    )
    return (outs, mark)


def swap(values, axis, bit):
    size = lax.axis_size(axis)
    return lax.ppermute(values, axis, [(i, i ^ bit) for i in range(size)])


def bits_of(size):
    return [1 << n for n in range(size.bit_length() - 1)]


def beside(bit):
    return "x" if bit == 1 else f"z{bit}"


def added(terms):
    return sum(t.astype(F32) for t in terms).astype(BF16)


class Links:
    def __init__(self):
        self.shards = lax.axis_size("shard")
        self.replicas = lax.axis_size("replica")
        self.direct = self.shards == BLOCKS and self.replicas >= 4
        self.direct = self.direct and self.replicas & (self.replicas - 1) == 0
        index = jnp.arange(BLOCKS, dtype=jnp.int32)
        self.order = index ^ lax.axis_index("shard") if self.direct else index
        self.replica = lax.axis_index("replica")

    def bit(self, bit):
        return (self.replica & bit) != 0

    def place(self, bit):
        return self.bit(bit).astype(jnp.int32)

    def both(self, bit, mine, other, axis):
        return jnp.where(
            self.bit(bit),
            jnp.concatenate([other, mine], axis=axis),
            jnp.concatenate([mine, other], axis=axis),
        )


    def halving(self, terms, bits):
        for bit in bits:
            half = terms[0].shape[1] // 2
            up = self.place(bit)
            piece = lambda at: [lax.dynamic_slice_in_dim(t, at * half, half, 1) for t in terms]
            (got,) = yield [(beside(bit), "replica", bit, added(piece(1 - up)))]
            terms = piece(up) + [got]
        return terms

    def part_steps(self, send, keep, y_first):
        (got,) = yield [("core", "shard", 1, send)]
        terms = [keep, got]
        if y_first:
            (got,) = yield [("y/", "shard", 2, added([t[1] for t in terms]))]
            terms = [t[:1] for t in terms] + [got[None]]
        terms = yield from self.halving(terms, bits_of(self.replicas)[:1])
        return added(terms)

    def chunk_steps(self, parts):
        while not all(part.done for part in parts):
            yield []
        bits = bits_of(self.replicas)
        terms = [jnp.concatenate([part.value for part in parts], axis=2)]
        terms = yield from self.halving(terms, bits[1:])
        if terms[0].shape[0] == 2:
            (got,) = yield [("y", "shard", 2, added([t[1] for t in terms]))]
            terms = [t[0] for t in terms] + [got]
        now = added(terms)
        now = now.reshape(-1, now.shape[-1])
        for bit in reversed(bits):
            (got,) = yield [(beside(bit), "replica", bit, now)]
            now = self.both(bit, now, got, 0)
        return now

    def total_steps(self, values):
        for axis, size in (("shard", self.shards), ("replica", self.replicas)):
            for bit in bits_of(size):
                (got,) = yield [("small", axis, bit, values)]
                values = values + got
        return values

    def small_steps(self, own):
        (got,) = yield [("small", "shard", 1, own)]
        pair = jnp.stack([own, got])
        (got,) = yield [("small", "shard", 2, pair)]
        return jnp.concatenate([pair, got])[self.order]

    def near_steps(self, own):
        (got,) = yield [("core", "shard", 1, own)]
        return got

    def far_steps(self, own):
        (far,) = yield [("y", "shard", 2, own)]
        (behind,) = yield [("core", "shard", 1, far)]
        return (far, behind)

    def shared_steps(self, sent, whole_block):
        (got,) = yield [("y" if whole_block else "y/", "shard", 2, sent)]
        width = got.shape[1] // 2
        mine = [got[:, :width], got[:, width:]]
        other = yield [(beside(1), "replica", 1, mine[0]), (beside(2), "replica", 2, mine[1])]
        if whole_block:
            far = [self.both(bit, m, o, 1) for bit, m, o in zip((1, 2), mine, other)]
            far = [jnp.concatenate(far, axis=1)]
        else:
            far = [
                jnp.concatenate(
                    [
                        jnp.where(self.bit(bit) == (n == 1), m, o)
                        for bit, m, o in zip((1, 2), mine, other)
                    ],
                    axis=1,
                )
                for n in range(2)
            ]
        behind = yield [("core", "shard", 1, f) for f in far]
        return list(zip(far, behind))


LATENCY = 2.0
PACE = {"core": 2.0, "y": 22.5, "x": 22.5, "z2": 22.5, "small": 1.0}
MOST_FLYING = 5


class Flow:
    def __init__(self, steps):
        self.steps, self.value, self.done = steps, None, False
        self.flying, self.parts, self.ready = [], [], 0.0
        self.asked = next(steps)

    def give(self, arrays):
        try:
            self.asked = self.steps.send(arrays)
        except StopIteration as end:
            self.asked, self.value, self.done = [], end.value, True


class Pipeline:
    def __init__(self, token):
        self.now, self.free, self.flows, self.token = 0.0, {}, [], token

    def add(self, steps, urgent=False):
        flow = Flow(steps)
        self.flows.insert(0 if urgent else len(self.flows), flow)
        return flow

    def tie(self, arrays):
        if not arrays:
            return []
        *arrays, self.token = lax.optimization_barrier((*arrays, self.token))
        return arrays

    def turn(self, window=None, slack=1.0, ahead=6.0):
        landed = [f for f in self.flows if f.flying and f.ready <= self.now + slack]
        arrived = [array for flow in landed for array in flow.flying]
        tied = self.tie(arrived)
        for flow in landed:
            got, tied = tied[: len(flow.flying)], tied[len(flow.flying) :]
            flow.flying = []
            if flow.asked[0][0].endswith("/"):
                flow.parts += got
                if flow.asked[0][3].shape[0]:
                    continue
                got, flow.parts = [jnp.concatenate(flow.parts, axis=0)], []
            flow.give(got)
            if flow.done and isinstance(flow.value, jax.Array):
                (flow.value,) = self.tie([flow.value])
        for flow in self.flows:
            if not flow.done and not flow.flying and not flow.asked:
                flow.give([])
        self.flows = [flow for flow in self.flows if not flow.done]
        issued = []
        for flow in self.flows:
            if flow.flying or not flow.asked:
                continue
            count = sum(len(f.flying) for f in self.flows) + len(flow.asked)
            links = [link.strip("/") for link, *_ in flow.asked]
            until = self.now + ahead if window is None else self.now + window - 8.0
            if count > MOST_FLYING or any(self.free.get(k, 0.0) > until for k in links):
                continue
            for n, (link, axis, bit, values) in enumerate(flow.asked):
                if link.endswith("/"):
                    link = link.strip("/")
                    rows = values.shape[0]
                    pace = PACE[link] * values.size * values.dtype.itemsize / MIB / rows
                    busy = max(0.0, self.free.get(link, 0.0) - self.now)
                    room = int(((window or 1000) - LATENCY - busy) / pace + 8) // 16 * 16
                    if rows - room > 16 and window is not None:
                        rows = max(room, 32)
                    flow.asked[n] = (link + "/", axis, bit, values[rows:])
                    values = values[:rows]
                issued.append((flow, len(flow.flying), axis, bit, values))
                flow.flying.append(values)
                size = values.size * values.dtype.itemsize / MIB
                start = max(self.now, self.free.get(link, 0.0))
                self.free[link] = start + size * PACE.get(link, 45.0)
                flow.ready = max(flow.ready, self.free[link] + LATENCY)
        started = {id(flow) for flow, *_ in issued}
        pending = [
            flow for flow in self.flows if not flow.flying and flow.asked and id(flow) not in started
        ]
        pending = [(flow, n) for flow in pending for n in range(len(flow.asked))]
        operands = [values for *_, values in issued] + [f.asked[n][3] for f, n in pending]
        operands = self.tie(operands)
        for (flow, n, axis, bit, _), values in zip(issued, operands):
            flow.flying[n] = swap(values, axis, bit)
        for (flow, n), values in zip(pending, operands[len(issued) :]):
            flow.asked[n] = (*flow.asked[n][:3], values)
        return arrived + [self.token]

    def spend(self, length, token):
        self.now += length
        self.token = token

    def wait(self):
        times = [flow.ready for flow in self.flows if flow.flying]
        return max(0.0, min(times) - self.now) if times else 0.0

    def skip(self, wait=0.0):
        times = [flow.ready for flow in self.flows if flow.flying]
        self.now = max(self.now, min(times) + wait) if times else self.now + 1.0

    def reach(self, flow, link):
        self.turn()
        while flow.asked[0][0] != link:
            self.skip()
            if flow.flying and flow.ready <= self.now + 1.0:
                return
            self.turn()

    def finish(self, *flows, window=None, wait=0.0):
        after = self.turn(window)
        while not all(flow.done for flow in flows):
            self.skip(wait)
            after = self.turn(window)
        return after


def on_device(
    tokens,
    out_grad,
    kept_count,
    attn_w,
    mlp_w,
    vectors,
    attn_m,
    mlp_m,
    small_m,
    attn_v,
    mlp_v,
    small_v,
):
    images, slots, _ = tokens.shape
    rows = images * slots
    links = Links()
    order = links.order
    owned = vectors.shape[0]
    image_total = images * links.replicas * links.shards

    attn_low, mlp_low, wo_low = (a.astype(BF16) for a in (attn_w, mlp_w, attn_w[:, 3 * D :]))
    small_low = jnp.pad(vectors.astype(BF16).T, ((0, 4), (0, 0)))
    at = jnp.arange(slots, dtype=jnp.int32)
    valid = (at[None, :] < (BUF + kept_count)[:, None]).reshape(rows, 1)
    gy = jnp.where(valid, out_grad.reshape(rows, D), jnp.zeros((), BF16))
    pipe = Pipeline(order)
    if links.direct:

        def half(array, first, width, bit):
            return lax.dynamic_slice_in_dim(array, first + links.place(bit) * width, width, 1)

        def halves(array, first, second, width):
            sent = [half(array, first, width, 1), half(array, second, width, 2)]
            return jnp.concatenate(sent, axis=1).astype(BF16)

        pair = 3 * D // 2
        qkv_flow = pipe.add(links.shared_steps(halves(attn_w, 0, pair, pair // 2), True))
        vec_flow = pipe.add(links.small_steps(small_low))
        near_flow = pipe.add(links.near_steps(attn_low))
        sends = [halves(mlp_w, n, FF + n, PART) for n in range(0, FF, 2 * PART)]
        pipe.turn()
        sends[0], sends[1], mlp_low, wo_low, gy = pipe.tie([*sends, mlp_low, wo_low, gy])
        mlp_flows = [pipe.add(links.shared_steps(sends[0], False))]
        wo_flow = pipe.add(links.far_steps(wo_low))
        mlp_flows.append(pipe.add(links.shared_steps(sends[1], False)))
        after = pipe.finish(qkv_flow, vec_flow, near_flow, window=12, wait=3.0)
        attn_near, ((attn_far, behind),) = near_flow.value, qkv_flow.value
        wqkv = [Piece(array, 0, 0) for array in (attn_low, attn_near, attn_far, behind)]
        small_full = vec_flow.value.transpose(1, 0, 2).reshape(16, D)
    else:
        gather = lambda array, axis: lax.all_gather(array, "shard", axis=axis, tiled=True)
        attn_full, mlp_full = gather(attn_low, 0), gather(mlp_low, 0)
        small_full = gather(small_low, 1)
        wqkv = [Piece(attn_full, j, 0) for j in range(BLOCKS)]
        wo = [Piece(attn_full, j, 3) for j in range(BLOCKS)]
        wups = [[Piece(mlp_full, j, p) for j in range(BLOCKS)] for p in range(PARTS)]
        wdns = [[Piece(mlp_full, j, 4 + p) for j in range(BLOCKS)] for p in range(PARTS)]
        after = []
    vec = small_full.astype(F32)

    totals = []

    def summed(send, keep, urgent=False):
        if links.direct:
            return pipe.add(links.part_steps(send, keep, True), urgent)
        return (send, keep)

    def chunk(name, *parts):
        if links.direct:
            totals.append((name, pipe.add(links.chunk_steps(parts), name[0] == "attn")))
            return
        stacked = [jnp.stack([k[0], s[0], k[1], s[1]]).reshape(D, -1) for s, k in parts]
        part = lax.psum_scatter(
            jnp.concatenate(stacked, axis=1), "shard", scatter_dimension=0, tiled=True
        )
        totals.append((name, lax.psum(part, "replica")))

    h1, qkv = qkv_forward(order, tokens, wqkv, vec, after)
    pipe.spend(17, h1)
    if links.direct:
        mlp_near_flow = pipe.add(links.near_steps(mlp_low))
    mixed = attn_mix(kept_count, qkv, images, pipe.turn(17))
    pipe.spend(17, mixed)
    if links.direct:
        after = pipe.finish(wo_flow, window=10)
        wo_far, behind = wo_flow.value
        wo = [Piece(attn_low, 0, 3), Piece(attn_near, 0, 3), Piece(wo_far, 0, 0), Piece(behind, 0, 0)]
    middle, h2 = out_project(order, tokens, mixed, wo, vec, after)
    pipe.spend(10, h2)

    acts, dpres, gbus = [], [], []
    if links.direct:
        wups, wdns = [], []
    for p in range(PARTS):
        if links.direct:
            flow = mlp_flows[p // 2]
            after = pipe.finish(flow, mlp_near_flow, window=17)
            far, behind = flow.value[p % 2]
            near = [(mlp_low, p, 4 + p), (mlp_near_flow.value, p, 4 + p)]
            four = [*near, (far, 0, 1), (behind, 0, 1)]
            wups.append([Piece(array, 0, up) for array, up, _ in four])
            wdns.append([Piece(array, 0, down) for array, _, down in four])
        act, dpre, send, keep, gbu = mlp_part(
            order, h2, gy, wups[p], wdns[p], vec[8 + p : 9 + p], after
        )
        acts.append(act)
        dpres.append(dpre)
        gbus.append(gbu)
        pipe.spend(17, gbu)
        part = summed(send, keep)
        if p % 2:
            chunk(("mlp", 3 + p, p - 1, 4 + p, p), before, part)
        before = part
        if p == 0 and links.direct:
            pipe.reach(part, "y/")
    dmid, da, two_sums, send, keep = mlp_back(
        order, dpres, wups, middle, gy, vec, mixed, pipe.turn(26)
    )
    pipe.spend(26, two_sums)
    out_part = summed(send, keep)

    split = images // 2
    dqkv, sums_a = attn_back(order, kept_count, da, wo, qkv, slots, 0, split, None, pipe.turn(19))
    pipe.spend(19, sums_a)
    dqkv, sums_b = attn_back(
        order, kept_count, da, wo, qkv, slots, split, images - split, dqkv, pipe.turn(19)
    )
    pipe.spend(19, sums_b)
    qkv_sums = sums_a + sums_b
    send, keep = weight_grad(order, h1, dqkv, D, pipe.turn(9), 2 * D)
    pipe.spend(9, send)
    chunk(("attn", 1, 2), summed(send, keep, True))
    send, keep = weight_grad(order, h1, dqkv, 0, pipe.turn(9), D)
    pipe.spend(9, send)
    chunk(("attn", 0, 3), summed(send, keep, True), out_part)
    in_grad, one_sums = input_back(order, dqkv, wqkv, tokens, dmid, vec, pipe.turn(19))
    pipe.spend(19, one_sums)

    g_down = jnp.sum(gy, axis=0, dtype=F32, keepdims=True)
    small = jnp.concatenate(
        [
            one_sums[0:2],
            qkv_sums[0:1],
            qkv_sums[2:3],
            two_sums[2:3],
            two_sums[0:2],
            g_down,
            *gbus,
            jnp.zeros((4, D), F32),
        ],
        axis=0,
    )
    if links.direct:
        totals.append(("small", pipe.add(links.total_steps(small))))
    else:
        totals.append(("small", lax.psum(small, ("replica", "shard"))))
    result = mlp_out(order, acts, wdns, middle, valid.astype(F32), vec, pipe.turn(17))
    pipe.spend(17, result)
    result = result.reshape(images, slots, D)

    outs = {"attn": [], "mlp": []}
    state = {
        "attn": (attn_w, attn_m, attn_v, image_total, 0.1, 0.05),
        "mlp": (mlp_w, mlp_m, mlp_v, image_total, 0.05, 0.05),
    }
    small_out, pieces = None, []
    while totals or pieces:
        after = pipe.turn()
        through = lambda total: not isinstance(total, Flow) or total.done
        for name, total in [entry for entry in totals if through(entry[1])]:
            total = total.value if isinstance(total, Flow) else total
            if name == "small":
                total = lax.dynamic_slice_in_dim(
                    total, lax.axis_index("shard") * owned, owned, 1
                )
                gradient = total[:12].T / image_total
                small_out = adam_terms(vectors, small_m, small_v, gradient, 1.0, 0.0)
                continue
            pieces += [(name[0], total, n, column) for n, column in enumerate(name[1:])]
        totals = [entry for entry in totals if not through(entry[1])]
        wait = pipe.wait() if totals else 1000.0
        kind, total, first, _ = pieces[0] if pieces else (None,) * 4
        columns = [c for k, t, _, c in pieces if t is total][: int((wait + 1.0) / 4.0)]
        if columns:
            outs[kind], mark = adam_part(total, first, columns, *state[kind], outs[kind], after)
            pipe.spend(4.0 * len(columns), mark)
            pieces = pieces[len(columns) :]
        elif totals:
            pipe.skip(1.5)
    attn_out, mlp_out_ = outs["attn"], outs["mlp"]
    return (result, in_grad, *attn_out, *mlp_out_, *small_out)


def solution(mesh):
    tokens = P(("replica", "shard"), None, None)
    owned = P("shard", None)
    in_specs = (tokens, tokens, P(("replica", "shard")), *[owned] * 9)
    out_specs = (tokens, tokens, *[owned] * 15)
    return jax.shard_map(
        on_device, mesh=mesh, in_specs=in_specs, out_specs=out_specs, check_vma=False
    )
```

```python
import jax
import jax.numpy as jnp
from jax import lax
from jax.experimental import pallas as pl
from jax.experimental.pallas import tpu as pltpu
from jax.sharding import PartitionSpec as P

D = 1024
HEADS = 16
HEAD_DIM = 64
FF = 4096
BUF = 64
STEP = 10
BLOCKS = 4
BLOCK = D // BLOCKS
PARTS = 4
PART = FF // PARTS
GROUP = 4
GROUP_W = GROUP * HEAD_DIM

EPS_NORM = 1e-06
MASKED = -1000000000.0
BETA_ONE = 0.9
BETA_TWO = 0.999
EPS_ADAM = 1e-08

BF16 = jnp.bfloat16
F32 = jnp.float32
MIB = 1 << 20


def normalize(values):
    average = jnp.mean(values, axis=-1, keepdims=True)
    centred = values - average
    inverse = lax.rsqrt(jnp.mean(centred * centred, axis=-1, keepdims=True) + EPS_NORM)
    return (centred * inverse, inverse)


def norm_back(upstream, normed, inverse):
    first_term = jnp.mean(upstream, axis=-1, keepdims=True)
    second_term = normed * jnp.mean(upstream * normed, axis=-1, keepdims=True)
    return inverse * (upstream - first_term - second_term)


def dot(left, right):
    return jnp.dot(left, right, preferred_element_type=F32)


def dot_nt(left, right):
    return lax.dot_general(left, right, (((1,), (1,)), ((), ())), preferred_element_type=F32)


def dot_tn(left, right):
    return lax.dot_general(left, right, (((0,), (0,)), ((), ())), preferred_element_type=F32)


def gelu_pair(values):
    size = jnp.abs(values)
    denominator = 1.0 + size * (0.3275911 * 0.7071067811865476)
    ratio = pl.reciprocal(denominator, approx=True)
    ratio = ratio * (2.0 - denominator * ratio)
    bell = jnp.exp(values * values * (-0.5))
    poly = 0.5 * 1.061405429 * ratio - 0.5 * 1.453152027
    poly = poly * ratio + 0.5 * 1.421413741
    poly = poly * ratio - 0.5 * 0.284496736
    poly = poly * ratio + 0.5 * 0.254829592
    tail = poly * ratio * bell
    below = jnp.where(values >= 0, 1.0 - tail, tail)
    return (values * below, below + values * bell * 0.3989422804014327)


def whole(array):
    rank = len(array.shape)
    return pl.BlockSpec(array.shape, lambda *_: (0,) * rank, pipeline_mode=pl.Buffered(1))


def params(limit):
    return pltpu.CompilerParams(vmem_limit_bytes=limit * MIB)


def cost(flops, nbytes):
    return pl.CostEstimate(flops=int(flops), bytes_accessed=int(nbytes), transcendentals=0)


def call(body, *, scalars, ins, in_specs, outs, out_specs, grid, name, limit, work, scratch=(), after=(), aliases=None):
    first = len(scalars) + len(ins)
    ins = [
        pltpu.with_memory_space_constraint(a, pltpu.HBM)
        if a.size * a.dtype.itemsize >= MIB // 4
        else a
        for a in ins
    ]

    def with_after(*refs):
        body(*refs[:first], *refs[first + len(after) :])

    return pl.pallas_call(
        with_after,
        grid_spec=pltpu.PrefetchScalarGridSpec(
            num_scalar_prefetch=len(scalars),
            grid=grid,
            in_specs=[*in_specs, *[pl.BlockSpec(memory_space=pl.ANY)] * len(after)],
            out_specs=out_specs,
            scratch_shapes=list(scratch),
        ),
        out_shape=outs,
        input_output_aliases=aliases or {},
        compiler_params=params(limit),
        cost_estimate=cost(*work),
        name=name,
    )(*scalars, *ins, *after)


def like(shape, dtype):
    return pltpu.HBM(shape, dtype)


def place(order_ref, target, pieces):
    for j, piece in enumerate(pieces):
        at = pl.multiple_of(order_ref[j] * BLOCK, BLOCK)
        target[pl.ds(at, BLOCK), :] = piece[...]


ANY = pl.BlockSpec(memory_space=pl.ANY)


class Piece:
    def __init__(self, array, row, column):
        self.array, self.row, self.column = array, row, column

    def spec(self, width):
        return pl.BlockSpec(
            (BLOCK, width), lambda *_: (self.row, self.column), pipeline_mode=pl.Buffered(1)
        )

    def view(self, ref, width):
        return ref.at[
            self.row * BLOCK : (self.row + 1) * BLOCK,
            self.column * width : (self.column + 1) * width,
        ]


def arrays(pieces):
    return [piece.array for piece in pieces]


def heads_apart(values, scale=None):
    lane = lax.broadcasted_iota(jnp.int32, values.shape, 1) // HEAD_DIM
    if scale is not None:
        values = values * jnp.asarray(scale, values.dtype)
    zero = jnp.zeros_like(values)
    return jnp.concatenate([jnp.where(lane == h, values, zero) for h in range(GROUP)], axis=0)


def heads_together(values, slots):
    lane = lax.broadcasted_iota(jnp.int32, (slots, GROUP_W), 1) // HEAD_DIM
    out = values[:slots]
    for h in range(1, GROUP):
        out = jnp.where(lane == h, values[h * slots : (h + 1) * slots], out)
    return out


def probs_of(keys, queries_apart, shift):
    scores = dot_nt(keys, queries_apart) + shift
    scores = jnp.exp(scores - jnp.max(scores, axis=0, keepdims=True))
    return scores * (1.0 / jnp.sum(scores, axis=0, keepdims=True))


def key_shift(kept, slots):
    at = lax.broadcasted_iota(jnp.int32, (slots, 1), 0)
    return jnp.where(at < BUF + kept, 0.0, MASKED).astype(F32)


def row_spec(slots, width):
    return pl.BlockSpec((slots, width), lambda i, *_: (i, 0))


def qkv_forward(order, h1, wqkv, vec, after, width=512):
    rows = h1.shape[0]

    def body(order_ref, h1_ref, *refs):
        w_refs, (bias_ref, qkv_ref, w_s) = refs[:BLOCKS], refs[BLOCKS:]
        place(order_ref, w_s, w_refs)
        qkv_ref[...] = (dot(h1_ref[...], w_s[...]) + bias_ref[...]).astype(BF16)

    bias = jnp.concatenate([vec[2:3], jnp.zeros_like(vec[2:3]), vec[3:4]], axis=1)
    return call(
        body,
        scalars=[order],
        ins=[h1, *arrays(wqkv), bias],
        in_specs=[whole(h1)]
        + [pl.BlockSpec((BLOCK, width), lambda i, *_, row=w.row: (row, i)) for w in wqkv]
        + [pl.BlockSpec((1, width), lambda i, *_: (0, i))],
        outs=[like((rows, 3 * D), BF16)],
        out_specs=[pl.BlockSpec((rows, width), lambda i, *_: (0, i))],
        scratch=[pltpu.VMEM((D, width), BF16)],
        grid=(3 * D // width,),
        name="qkv_forward",
        limit=30,
        work=(10 * rows * D * D, 18 * MIB),
        after=after,
    )[0]


def attn_mix(kept, qkv, images, after):
    rows = qkv.shape[0]
    slots = rows // images

    def body(kept_ref, qkv_ref, mixed_ref):
        shift = key_shift(kept_ref[pl.program_id(0)], slots)
        for g in range(HEADS // GROUP):
            at = g * GROUP_W
            q, k, v = (qkv_ref[:, n * D + at : n * D + at + GROUP_W] for n in range(3))
            probs = probs_of(k, heads_apart(q, HEAD_DIM**-0.5), shift).astype(BF16)
            mixed_ref[:, at : at + GROUP_W] = heads_together(dot_tn(probs, v), slots).astype(BF16)

    return call(
        body,
        scalars=[kept],
        ins=[qkv],
        in_specs=[row_spec(slots, 3 * D)],
        outs=[like((rows, D), BF16)],
        out_specs=[row_spec(slots, D)],
        grid=(images,),
        name="attn_mix",
        limit=30,
        work=(14 * rows * D * D, 8 * MIB),
        after=after,
    )[0]


def out_project(order, x, mixed, wo, vec, after):
    images, slots, _ = x.shape
    rows = images * slots

    def body(order_ref, x_ref, mixed_ref, *refs):
        wo_refs, (vec_ref, middle_ref, h2_ref, wo_s) = refs[:BLOCKS], refs[BLOCKS:]

        @pl.when(pl.program_id(0) == 0)
        def _():
            place(order_ref, wo_s, wo_refs)

        branch = dot(mixed_ref[...], wo_s[...]) + vec_ref[4:5, :]
        for n in range(2):
            span = slice(n * slots, (n + 1) * slots)
            middle = x_ref[n].astype(F32) + branch[span]
            middle_ref[span, :] = middle
            normed, _ = normalize(middle)
            h2_ref[span, :] = (normed * vec_ref[5:6, :] + vec_ref[6:7, :]).astype(BF16)

    return call(
        body,
        scalars=[order],
        ins=[x, mixed, *arrays(wo), vec],
        in_specs=[pl.BlockSpec((2, slots, D), lambda i, *_: (i, 0, 0)), row_spec(2 * slots, D)]
        + [w.spec(D) for w in wo]
        + [whole(vec)],
        outs=[like((rows, D), F32), like((rows, D), BF16)],
        out_specs=[row_spec(2 * slots, D)] * 2,
        scratch=[pltpu.VMEM((D, D), BF16)],
        grid=(images // 2,),
        name="out_project",
        limit=30,
        work=(6 * rows * D * D, 12 * MIB),
        after=after,
    )


def mlp_part(order, h2, dm, wup, wdn, bu, after, width=512):
    rows = h2.shape[0]
    weights = [*wup, *wdn]

    def body(order_ref, h2_hbm, dm_hbm, *refs):
        weight_refs, (bu_ref, *outs, gbu_ref) = refs[: 2 * BLOCKS], refs[2 * BLOCKS : -10]
        h2_ref, dm_ref, up_s, dn_s, act_ref, dpre_ref, send, keep, in_sems, out_sems = refs[-10:]
        flying = []

        def put(n, source, index):
            copy = pltpu.make_async_copy(
                source.at[index], outs[n].at[index], out_sems.at[len(flying)]
            )
            copy.start()
            flying.append(copy)

        def fetch(n, source, target, first):
            copies = [pltpu.make_async_copy(source, target, in_sems.at[n])]
            for j in range(BLOCKS):
                at = pl.multiple_of(order_ref[j] * BLOCK, BLOCK)
                copies.append(
                    pltpu.make_async_copy(
                        weights[first + j].view(weight_refs[first + j], PART),
                        (dn_s if first else up_s).at[pl.ds(at, BLOCK), :],
                        in_sems.at[n + 1 + j],
                    )
                )
            for copy in copies:
                copy.start()
            return copies

        def arrive(copies):
            for copy in copies:
                copy.wait()

        ups = fetch(0, h2_hbm, h2_ref, 0)
        dns = fetch(1 + BLOCKS, dm_hbm, dm_ref, BLOCKS)

        def front(n, span):
            if n == 0:
                arrive(ups)
            pre = dot(h2_ref[...], up_s[:, span]) + bu_ref[:, span]
            if n == 0:
                arrive(dns)
            return (pre, dot(dm_ref[...], dn_s[:, span]))

        def middle(span, pre, dact):
            act, slope = gelu_pair(pre)
            act = act.astype(BF16)
            dpre = (dact * slope).astype(BF16)
            act_ref[:, span] = act
            dpre_ref[:, span] = dpre
            gbu_ref[:, span] = jnp.sum(dpre.astype(F32), axis=0, keepdims=True)
            return (act, dpre)

        def back(span, act, dpre):
            for first, left_ref, right in ((0, dm_ref, act), (PART, h2_ref, dpre)):
                there = slice(first + span.start, first + span.stop)
                for j in range(BLOCKS):
                    at = pl.multiple_of(order_ref[j] * BLOCK, BLOCK)
                    grad = dot_tn(left_ref[:, pl.ds(at, BLOCK)], right).astype(BF16)
                    (send if j % 2 else keep)[j // 2, :, there] = grad

        def out(span):
            put(0, act_ref, (slice(None), span))
            put(1, dpre_ref, (slice(None), span))
            for first in (0, PART):
                there = slice(first + span.start, first + span.stop)
                put(2, send, (slice(None), slice(None), there))
                put(3, keep, (slice(None), slice(None), there))

        spans = [slice(at, at + width) for at in range(0, PART, width)]
        fresh = front(0, spans[0])
        held = None
        for n, span in enumerate(spans):
            later = front(n + 1, spans[n + 1]) if n + 1 < len(spans) else None
            now = middle(span, *fresh)
            if held is not None:
                back(spans[n - 1], *held)
                out(spans[n - 1])
            held, fresh = now, later
        back(spans[-1], *held)
        out(spans[-1])
        for copy in flying:
            copy.wait()

    one = pl.BlockSpec((1, PART), lambda i, *_: (0, 0))
    return call(
        body,
        scalars=[order],
        ins=[h2, dm, *arrays(weights), bu],
        in_specs=[ANY] * (2 + len(weights)) + [whole(bu)],
        outs=[like((rows, PART), BF16)] * 2
        + [like((2, BLOCK, 2 * PART), BF16)] * 2
        + [like((1, PART), F32)],
        out_specs=[ANY] * 4 + [one],
        scratch=[pltpu.VMEM((rows, D), BF16)] * 2
        + [pltpu.VMEM((D, PART), BF16)] * 2
        + [pltpu.VMEM((rows, PART), BF16)] * 2
        + [pltpu.VMEM((2, BLOCK, 2 * PART), BF16)] * 2
        + [
            pltpu.SemaphoreType.DMA((2 + 2 * BLOCKS,)),
            pltpu.SemaphoreType.DMA((PART // width * 6,)),
        ],
        grid=(1,),
        name="mlp_part",
        limit=40,
        work=(12 * rows * D * PART, 12 * MIB),
        after=after,
    )


def streamed(order_ref, sides, side_refs, weights, weight_refs, side_s, weight_s, sems, use):
    def copies(p):
        slot = p % 2
        yield pltpu.make_async_copy(side_refs[p], side_s.at[slot], sems.at[slot, BLOCKS])
        for j in range(BLOCKS):
            at = pl.multiple_of(order_ref[j] * BLOCK, BLOCK)
            piece = weights[p][j]
            yield pltpu.make_async_copy(
                piece.view(weight_refs[p * BLOCKS + j], PART),
                weight_s.at[slot, pl.ds(at, BLOCK), :],
                sems.at[slot, j],
            )

    for copy in copies(0):
        copy.start()
    for p in range(PARTS):
        if p + 1 < PARTS:
            for copy in copies(p + 1):
                copy.start()
        for copy in copies(p):
            copy.wait()
        use(p, side_s[p % 2], weight_s[p % 2])


def stream_scratch(rows):
    return [
        pltpu.VMEM((2, rows, PART), BF16),
        pltpu.VMEM((2, D, PART), BF16),
        pltpu.SemaphoreType.DMA((2, BLOCKS + 1)),
        pltpu.VMEM((rows, D), F32),
        pltpu.VMEM((rows, D), F32),
        pltpu.SemaphoreType.DMA((1,)),
    ]


def mlp_back(order, dpres, wups, middle, gy, vec, mixed, after):
    rows = middle.shape[0]
    flat = [w for part in wups for w in part]

    def body(order_ref, *refs):
        dpre_refs, refs = refs[:PARTS], refs[PARTS:]
        up_refs, refs = refs[: PARTS * BLOCKS], refs[PARTS * BLOCKS :]
        middle_ref, gy_ref, vec_ref, mixed_ref, da_ref, sums_ref, send, keep = refs[:8]
        side_s, weight_s, sems, acc, middle_s, middle_sem = refs[8:]

        def use(p, side, weight):
            if p == 0:
                pltpu.make_async_copy(middle_ref, middle_s, middle_sem.at[0]).start()
                acc[...] = dot_nt(side, weight)
            else:
                acc[...] += dot_nt(side, weight)

        streamed(order_ref, dpres, dpre_refs, wups, up_refs, side_s, weight_s, sems, use)
        pltpu.make_async_copy(middle_ref, middle_s, middle_sem.at[0]).wait()
        gain, shift, bias, down = (jnp.zeros((1, D), F32) for _ in range(4))
        step = rows // 6
        for r in range(0, rows, step):
            span = slice(r, r + step)
            dh2 = acc[span, :]
            normed, inverse = normalize(middle_s[span, :])
            gain += jnp.sum(dh2 * normed, axis=0, keepdims=True)
            shift += jnp.sum(dh2, axis=0, keepdims=True)
            dmid = norm_back(dh2 * vec_ref[5:6, :], normed, inverse) + gy_ref[span, :].astype(F32)
            da = dmid.astype(BF16)
            da_ref[span, :] = da
            bias += jnp.sum(da.astype(F32), axis=0, keepdims=True)
            down += jnp.sum(gy_ref[span, :].astype(F32), axis=0, keepdims=True)
        sums_ref[...] = jnp.concatenate([gain, shift, bias, down, jnp.zeros((4, D), F32)], axis=0)
        for j in range(BLOCKS):
            at = pl.multiple_of(order_ref[j] * BLOCK, BLOCK)
            grad = dot_tn(mixed_ref[:, pl.ds(at, BLOCK)], da_ref[...]).astype(BF16)
            (send if j % 2 else keep)[j // 2] = grad

    return call(
        body,
        scalars=[order],
        ins=[*dpres, *arrays(flat), middle, gy, vec, mixed],
        in_specs=[ANY] * (PARTS + len(flat) + 1) + [whole(gy), whole(vec), whole(mixed)],
        outs=[like((rows, D), BF16), like((8, D), F32)]
        + [like((2, BLOCK, D), BF16)] * 2,
        out_specs=[
            pl.BlockSpec((rows, D), lambda i, *_: (0, 0)),
            pl.BlockSpec((8, D), lambda i, *_: (0, 0)),
            pl.BlockSpec((2, BLOCK, D), lambda i, *_: (0, 0, 0)),
            pl.BlockSpec((2, BLOCK, D), lambda i, *_: (0, 0, 0)),
        ],
        scratch=stream_scratch(rows),
        grid=(1,),
        name="mlp_back",
        limit=40,
        work=(3 * rows * D * FF, 30 * MIB),
        after=after,
    )


def mlp_out(order, acts, wdns, middle, valid, vec, after):
    rows = middle.shape[0]
    flat = [w for part in wdns for w in part]

    def body(order_ref, *refs):
        act_refs, refs = refs[:PARTS], refs[PARTS:]
        dn_refs, refs = refs[: PARTS * BLOCKS], refs[PARTS * BLOCKS :]
        middle_ref, valid_ref, vec_ref, out_ref = refs[:4]
        side_s, weight_s, sems, acc, middle_s, middle_sem = refs[4:]

        def use(p, side, weight):
            if p == 0:
                pltpu.make_async_copy(middle_ref, middle_s, middle_sem.at[0]).start()
                acc[...] = dot_nt(side, weight)
            elif p + 1 < PARTS:
                acc[...] += dot_nt(side, weight)
            else:
                pltpu.make_async_copy(middle_ref, middle_s, middle_sem.at[0]).wait()
                total = acc[...] + dot_nt(side, weight) + middle_s[...] + vec_ref[7:8, :]
                out_ref[...] = (total * valid_ref[...]).astype(BF16)

        streamed(order_ref, acts, act_refs, wdns, dn_refs, side_s, weight_s, sems, use)

    return call(
        body,
        scalars=[order],
        ins=[*acts, *arrays(flat), middle, valid, vec],
        in_specs=[ANY] * (PARTS + len(flat) + 1) + [whole(valid), whole(vec)],
        outs=[like((rows, D), BF16)],
        out_specs=[pl.BlockSpec((rows, D), lambda i, *_: (0, 0))],
        scratch=stream_scratch(rows),
        grid=(1,),
        name="mlp_out",
        limit=40,
        work=(3 * rows * D * FF, 24 * MIB),
        after=after,
    )[0]


def attn_back(order, kept, da, wo, qkv, slots, first, count, before, after):
    rows = da.shape[0]

    def body(order_ref, kept_ref, da_ref, *refs):
        wo_refs, refs = refs[:BLOCKS], refs[BLOCKS:]
        qkv_ref, dqkv_ref, sums_ref, wo_s = refs[0], *refs[-3:]
        image = pl.program_id(0)

        @pl.when(image == 0)
        def _():
            place(order_ref, wo_s, wo_refs)
            sums_ref[...] = jnp.zeros_like(sums_ref)

        shift = key_shift(kept_ref[first + image], slots)
        da = da_ref[...]
        scale = HEAD_DIM**-0.5
        for g in range(HEADS // GROUP):
            at = g * GROUP_W
            spans = [slice(n * D + at, n * D + at + GROUP_W) for n in range(3)]
            q, k, v = (qkv_ref[:, span] for span in spans)
            dmix = dot_nt(da, wo_s[at : at + GROUP_W, :]).astype(BF16)
            apart = heads_apart(q, scale)
            probs = probs_of(k, apart, shift)
            dmix_apart = heads_apart(dmix)
            dv = dot(probs.astype(BF16), dmix_apart).astype(BF16)
            dprob = dot_nt(v, dmix_apart)
            product = probs * dprob
            dsc = (product - probs * jnp.sum(product, axis=0, keepdims=True)).astype(BF16)
            dk = dot(dsc, apart).astype(BF16)
            dq = (heads_together(dot_tn(dsc, k), slots) * scale).astype(BF16)
            for n, grad in enumerate((dq, dk, dv)):
                dqkv_ref[:, spans[n]] = grad
                if n != 1:
                    sums_ref[n : n + 1, at : at + GROUP_W] += jnp.sum(
                        grad.astype(F32), axis=0, keepdims=True
                    )

    row = lambda width: pl.BlockSpec((slots, width), lambda i, *_: (first + i, 0))
    extra = [] if before is None else [before]
    return call(
        body,
        scalars=[order, kept],
        ins=[da, *arrays(wo), qkv, *extra],
        in_specs=[row(D)]
        + [w.spec(D) for w in wo]
        + [row(3 * D)]
        + [pl.BlockSpec(memory_space=pl.ANY)] * len(extra),
        outs=[like((rows, 3 * D), BF16), like((8, D), F32)],
        out_specs=[row(3 * D), pl.BlockSpec((8, D), lambda i, *_: (0, 0))],
        scratch=[pltpu.VMEM((D, D), BF16)],
        grid=(count,),
        aliases={4 + BLOCKS: 0} if extra else None,
        name="attn_back",
        limit=30,
        work=(12 * rows * D * D, 18 * MIB),
        after=after,
    )


def input_back(order, dqkv, wqkv, x, da, vec, after):
    images, slots, _ = x.shape
    rows = images * slots

    def body(order_ref, dqkv_ref, *refs):
        wq_refs = refs[:BLOCKS]
        x_ref, da_ref, vec_ref, out_ref, sums_ref, acc = refs[BLOCKS:]

        @pl.when(pl.program_id(0) == 0)
        def _():
            sums_ref[...] = jnp.zeros_like(sums_ref)

        grad = dqkv_ref[...]
        for j in range(BLOCKS):
            at = pl.multiple_of(order_ref[j] * BLOCK, BLOCK)
            acc[:, pl.ds(at, BLOCK)] = dot_nt(grad, wq_refs[j][...])
        for n in range(2):
            dh1 = acc[n * slots : (n + 1) * slots, :]
            normed, inverse = normalize(x_ref[n].astype(F32))
            sums_ref[0:1, :] += jnp.sum(dh1 * normed, axis=0, keepdims=True)
            sums_ref[1:2, :] += jnp.sum(dh1, axis=0, keepdims=True)
            total = norm_back(dh1 * vec_ref[0:1, :], normed, inverse)
            out_ref[n] = (total + da_ref[n * slots : (n + 1) * slots, :].astype(F32)).astype(BF16)

    image = pl.BlockSpec((2, slots, D), lambda i, *_: (i, 0, 0))
    return call(
        body,
        scalars=[order],
        ins=[dqkv, *arrays(wqkv), x, da, vec],
        in_specs=[row_spec(2 * slots, 3 * D)]
        + [w.spec(3 * D) for w in wqkv]
        + [image, row_spec(2 * slots, D), whole(vec)],
        outs=[like((images, slots, D), BF16), like((8, D), F32)],
        out_specs=[image, pl.BlockSpec((8, D), lambda i, *_: (0, 0))],
        scratch=[pltpu.VMEM((2 * slots, D), F32)],
        grid=(images // 2,),
        name="input_back",
        limit=30,
        work=(8 * rows * D * D, 24 * MIB),
        after=after,
    )


def kv_grad(order, left, right, after, width=512):
    rows = right.shape[0]
    steps = D // width

    def body(order_ref, left_ref, right_ref, send, keep):
        for j in range(BLOCKS):
            at = pl.multiple_of(order_ref[j] * BLOCK, BLOCK)
            grad = dot_tn(left_ref[:, pl.ds(at, BLOCK)], right_ref[...]).astype(BF16)
            (send if j % 2 else keep)[j // 2] = grad

    grads = pl.BlockSpec((2, BLOCK, width), lambda i, *_: (0, 0, i))
    return call(
        body,
        scalars=[order],
        ins=[left, right],
        in_specs=[whole(left), pl.BlockSpec((rows, width), lambda i, *_: (0, steps + i))],
        outs=[like((2, BLOCK, 2 * D), BF16)] * 2,
        out_specs=[grads] * 2,
        grid=(2 * steps,),
        name="kv_grad",
        limit=30,
        work=(8 * rows * D * D, 16 * MIB),
        after=after,
    )


def query_grad(order, left, right, small, after):
    rows = right.shape[0]
    columns = D + 128

    def body(order_ref, left_ref, right_ref, small_ref, send, keep):
        for j in range(BLOCKS):
            at = pl.multiple_of(order_ref[j] * BLOCK, BLOCK)
            target = send if j % 2 else keep
            grad = dot_tn(left_ref[:, pl.ds(at, BLOCK)], right_ref[...]).astype(BF16)
            target[j // 2, :, :D] = grad
            some = small_ref[:, pl.ds(at, BLOCK)]
            some = jnp.concatenate([some, jnp.zeros((112, BLOCK), F32)], axis=0)
            target[j // 2, :, D:] = some.T.astype(BF16)

    out = pl.BlockSpec((2, BLOCK, columns), lambda i, *_: (0, 0, 0))
    return call(
        body,
        scalars=[order],
        ins=[left, right, small],
        in_specs=[whole(left), pl.BlockSpec((rows, D), lambda i, *_: (0, 0)), whole(small)],
        outs=[like((2, BLOCK, columns), BF16)] * 2,
        out_specs=[out] * 2,
        grid=(1,),
        name="query_grad",
        limit=30,
        work=(6 * rows * D * D, 10 * MIB),
        after=after,
    )


def adam_terms(weight, first_mom, second_mom, gradient, rate, decay):
    first_new = BETA_ONE * first_mom + (1.0 - BETA_ONE) * gradient
    second_new = BETA_TWO * second_mom + (1.0 - BETA_TWO) * gradient * gradient
    first_hat = first_new * (1.0 / (1.0 - BETA_ONE**STEP))
    second_hat = second_new * (1.0 / (1.0 - BETA_TWO**STEP))
    weight_new = weight - rate * (first_hat / (jnp.sqrt(second_hat) + EPS_ADAM) + decay * weight)
    return (gradient, first_new, second_new, weight_new, weight_new.astype(BF16))


def adam_part(halves, second, first, columns, weight, first_mom, second_mom, count, rate, decay, before, after):
    half = halves[0].shape[0]
    rows = 2 * half
    width = D if len(columns) > 1 else D // 2
    steps = D // width

    def body(columns_ref, second_ref, a_ref, b_ref, w_ref, m_ref, v_ref, *refs):
        lower = second_ref[0] == 1
        a, b = (ref[...].astype(F32) * (1.0 / count) for ref in (a_ref, b_ref))
        for n, gradient in enumerate((jnp.where(lower, b, a), jnp.where(lower, a, b))):
            span = slice(n * half, (n + 1) * half)
            terms = (w_ref[span, :], m_ref[span, :], v_ref[span, :])
            outs = adam_terms(*terms, gradient, rate, decay)
            for ref, value in zip(refs[-6:], outs):
                ref[span, :] = value
        refs[-1][...] = jnp.zeros_like(refs[-1])

    there = pl.BlockSpec((rows, width), lambda i, n, where, _: (0, where[i] * steps + n))
    shape = weight.shape
    *outs, mark = call(
        body,
        scalars=[jnp.array(columns, jnp.int32), second],
        ins=[*halves, weight, first_mom, second_mom, *before],
        in_specs=[pl.BlockSpec((half, width), lambda i, n, *_: (0, (first + i) * steps + n))] * 2
        + [there] * 3
        + [ANY] * len(before),
        outs=[jax.ShapeDtypeStruct(shape, F32)] * 4
        + [jax.ShapeDtypeStruct(shape, BF16), jax.ShapeDtypeStruct((8, 128), F32)],
        out_specs=[there] * 5 + [pl.BlockSpec((8, 128), lambda i, n, *_: (0, 0))],
        grid=(len(columns), steps),
        aliases={7 + n: n for n in range(len(before))},
        name="adam_part",
        limit=30,
        work=(3 * MIB * 1024 * len(columns), 10 * MIB),
        after=after,
    )
    return (outs, mark)


def swap(values, axis, bit):
    size = lax.axis_size(axis)
    return lax.ppermute(values, axis, [(i, i ^ bit) for i in range(size)])


def bits_of(size):
    return [1 << n for n in range(size.bit_length() - 1)]


def beside(bit):
    return "x" if bit == 1 else f"z{bit}"


def added(terms):
    return sum(t.astype(F32) for t in terms).astype(BF16)


class Links:
    def __init__(self):
        self.shards = lax.axis_size("shard")
        self.replicas = lax.axis_size("replica")
        self.direct = self.shards == BLOCKS and self.replicas >= 4
        self.direct = self.direct and self.replicas & (self.replicas - 1) == 0
        index = jnp.arange(BLOCKS, dtype=jnp.int32)
        self.order = index ^ lax.axis_index("shard") if self.direct else index
        self.replica = lax.axis_index("replica")

    def bit(self, bit):
        return (self.replica & bit) != 0

    def place(self, bit):
        return self.bit(bit).astype(jnp.int32)

    def both(self, bit, mine, other, axis):
        return jnp.where(
            self.bit(bit),
            jnp.concatenate([other, mine], axis=axis),
            jnp.concatenate([mine, other], axis=axis),
        )


    def halving(self, terms, bits):
        for bit in bits:
            half = terms[0].shape[1] // 2
            up = self.place(bit)
            size = (1, half, terms[0].shape[2])
            piece = lambda at: [lax.dynamic_slice(t, (0, at * half, 0), size) for t in terms]
            (got,) = yield [(beside(bit), "replica", bit, added(piece(1 - up)))]
            terms = piece(up) + [got]
        return terms

    def part_steps(self, send, keep):
        (got,) = yield [("core", "shard", 1, send)]
        terms = [keep, got]
        (got,) = yield [("y/", "shard", 2, added([t[1] for t in terms]))]
        terms += [got[None]]
        terms = yield from self.halving(terms, bits_of(self.replicas)[:1])
        return added(terms)

    def chunk_steps(self, parts):
        while not all(part.done for part in parts):
            yield []
        bits = bits_of(self.replicas)
        terms = [jnp.concatenate([part.value for part in parts], axis=2)]
        terms = yield from self.halving(terms, bits[1:])
        now = added(terms)[0]
        for bit in reversed(bits[1:]):
            (got,) = yield [(beside(bit), "replica", bit, now)]
            now = self.both(bit, now, got, 0)
        link = beside(1) + ("/" if now.shape[1] > 3 * D else "")
        (got,) = yield [(link, "replica", 1, now)]
        return (now, got)

    def small_steps(self, own):
        (got,) = yield [("small", "shard", 1, own)]
        pair = jnp.stack([own, got])
        (got,) = yield [("small", "shard", 2, pair)]
        return jnp.concatenate([pair, got])[self.order]

    def near_steps(self, own):
        (got,) = yield [("core", "shard", 1, own)]
        return got

    def far_steps(self, own):
        (far,) = yield [("y/", "shard", 2, own)]
        (behind,) = yield [("core", "shard", 1, far)]
        return (far, behind)

    def shared_steps(self, sent, whole_block):
        (got,) = yield [("y" if whole_block else "y/", "shard", 2, sent)]
        width = got.shape[1] // 2
        mine = [got[:, :width], got[:, width:]]
        other = yield [(beside(1), "replica", 1, mine[0]), (beside(2), "replica", 2, mine[1])]
        if whole_block:
            far = [self.both(bit, m, o, 1) for bit, m, o in zip((1, 2), mine, other)]
            far = [jnp.concatenate(far, axis=1)]
        else:
            far = [
                jnp.concatenate(
                    [
                        jnp.where(self.bit(bit) == (n == 1), m, o)
                        for bit, m, o in zip((1, 2), mine, other)
                    ],
                    axis=1,
                )
                for n in range(2)
            ]
        behind = yield [("core", "shard", 1, f) for f in far]
        return list(zip(far, behind))


LATENCY = 2.0
PACE = {"core": 2.0, "y": 22.5, "x": 22.5, "z2": 22.5, "small": 1.0}
MOST_FLYING = 5


class Flow:
    def __init__(self, steps, rank):
        self.steps, self.rank, self.value, self.done = steps, rank, None, False
        self.flying, self.parts, self.ready = [], [], 0.0
        self.asked, self.sent = next(steps), 0

    def give(self, arrays):
        try:
            self.asked, self.sent = self.steps.send(arrays), 0
        except StopIteration as end:
            self.asked, self.value, self.done = [], end.value, True


class Pipeline:
    def __init__(self, token):
        self.now, self.free, self.flows, self.token, self.landed = 0.0, {}, [], token, []

    def add(self, steps, rank=1):
        flow = Flow(steps, rank)
        self.flows = sorted([*self.flows, flow], key=lambda flow: flow.rank)
        return flow

    def tie(self, arrays):
        if not arrays:
            return []
        *arrays, self.token = lax.optimization_barrier((*arrays, self.token))
        return arrays

    def land(self, slack=2.0):
        landed = [f for f in self.flows if f.flying and f.ready <= self.now + slack]
        arrived = [array for flow in landed for array in flow.flying]
        self.landed += arrived
        tied = self.tie(arrived)
        for flow in landed:
            got, tied = tied[: len(flow.flying)], tied[len(flow.flying) :]
            flow.flying = []
            if flow.asked[0][0].endswith("/"):
                flow.parts += got
                if flow.sent < flow.asked[0][3].shape[0]:
                    continue
                got, flow.parts = [jnp.concatenate(flow.parts, axis=0)], []
            flow.give(got)
            if flow.done and isinstance(flow.value, jax.Array):
                (flow.value,) = self.tie([flow.value])
        for flow in self.flows:
            if not flow.done and not flow.flying and not flow.asked:
                flow.give([])
        self.flows = [flow for flow in self.flows if not flow.done]

    def start(self, window=None, ahead=6.0, only=None):
        issued = []
        until = self.now + (ahead if window is None else window - 5.0)
        for flow in self.flows:
            if flow.flying or not flow.asked or (only is not None and flow is not only):
                continue
            count = sum(len(f.flying) for f in self.flows) + len(flow.asked)
            links = [link.strip("/") for link, *_ in flow.asked]
            if count > MOST_FLYING or any(self.free.get(k, 0.0) > until for k in links):
                continue
            if window is not None and not all(self.fits(window, *asked) for asked in flow.asked):
                continue
            for n, (link, axis, bit, values) in enumerate(flow.asked):
                if link.endswith("/"):
                    link, rows = link.strip("/"), values.shape[0]
                    left = rows - flow.sent
                    pace = PACE[link] * values.size * values.dtype.itemsize / MIB / rows
                    busy = max(0.0, self.free.get(link, 0.0) - self.now)
                    room = int(((window or 1000) - LATENCY - busy) / pace + 8) // 16 * 16
                    if left - room > 16 and window is not None:
                        left = room
                    if left < 32:
                        continue
                    values = values[flow.sent : flow.sent + left]
                    flow.sent += left
                issued.append((flow, len(flow.flying), axis, bit, values))
                flow.flying.append(values)
                size = values.size * values.dtype.itemsize / MIB
                start = max(self.now, self.free.get(link, 0.0))
                self.free[link] = start + size * PACE.get(link, 45.0)
                flow.ready = max(flow.ready, self.free[link] + LATENCY)
        pending = [flow for flow in self.flows if not flow.flying and flow.asked]
        pending = [(flow, n) for flow in pending for n in range(len(flow.asked))]
        operands = [values for *_, values in issued] + [f.asked[n][3] for f, n in pending]
        operands = self.tie(operands)
        for (flow, n, axis, bit, _), values in zip(issued, operands):
            flow.flying[n] = swap(values, axis, bit)
        for (flow, n), values in zip(pending, operands[len(issued) :]):
            flow.asked[n] = (*flow.asked[n][:3], values)
        after, self.landed = self.landed + [self.token], []
        return after

    def fits(self, window, link, axis, bit, values):
        if link.endswith("/"):
            return True
        busy = max(0.0, self.free.get(link, 0.0) - self.now)
        length = values.size * values.dtype.itemsize / MIB * PACE.get(link, 45.0)
        return busy + length + LATENCY <= window + 1.5

    def turn(self, window=None):
        self.land()
        return self.start(window)

    def spend(self, length, token):
        self.now += length
        self.token = token

    def wait(self):
        times = [flow.ready for flow in self.flows if flow.flying]
        return max(0.0, min(times) - self.now) if times else 1.0

    def skip(self, wait=0.0):
        self.now += self.wait() + wait

    def reach(self, flow, link, gap=None, wait=0.0, alone=False):
        self.land()
        while flow.asked[0][0] != link:
            self.start(gap, only=flow if alone else None)
            self.now = max(self.now, flow.ready) if alone else self.now + self.wait() + wait
            self.land()

    def finish(self, *flows, window=None, gap=None, wait=0.0):
        self.land()
        while not all(flow.done for flow in flows):
            self.start(gap)
            self.skip(wait)
            self.land()
        return self.start(window)


def on_device(
    tokens,
    out_grad,
    kept_count,
    attn_w,
    mlp_w,
    vectors,
    attn_m,
    mlp_m,
    small_m,
    attn_v,
    mlp_v,
    small_v,
):
    images, slots, _ = tokens.shape
    rows = images * slots
    links = Links()
    order = links.order
    owned = vectors.shape[0]
    image_total = images * links.replicas * links.shards

    small_low = jnp.pad(vectors.astype(BF16).T, ((0, 4), (0, 0)))
    at = jnp.arange(slots, dtype=jnp.int32)
    valid = (at[None, :] < (BUF + kept_count)[:, None]).reshape(rows, 1)
    gy = jnp.where(valid, out_grad.reshape(rows, D), jnp.zeros((), BF16))
    pipe = Pipeline(order)

    def first_norm(small_full):
        normed, _ = normalize(tokens.reshape(rows, D).astype(F32))
        vec = small_full.astype(F32)
        return (normed * vec[0:1] + vec[1:2]).astype(BF16)

    if links.direct:

        def half(array, first, width, bit):
            return lax.dynamic_slice_in_dim(array, first + links.place(bit) * width, width, 1)

        def halves(array, first, second, width):
            sent = [half(array, first, width, 1), half(array, second, width, 2)]
            return jnp.concatenate(sent, axis=1).astype(BF16)

        pair = 3 * D // 2
        qkv_flow = pipe.add(links.shared_steps(halves(attn_w, 0, pair, pair // 2), True), 0)
        vec_flow = pipe.add(links.small_steps(small_low), 0)
        pipe.turn()
        attn_after, mlp_after = pipe.tie([attn_w, mlp_w])
        attn_low, mlp_low = attn_after.astype(BF16), mlp_after.astype(BF16)
        wo_low = attn_after[:, 3 * D :].astype(BF16)
        sends = [halves(mlp_after, n, FF + n, PART) for n in range(0, FF, 2 * PART)]
        pipe.turn()
        sends[0], sends[1], mlp_low, wo_low, gy = pipe.tie([*sends, mlp_low, wo_low, gy])
        mlp_flows = [pipe.add(links.shared_steps(sends[0], False), 0)]
        wo_flow = pipe.add(links.far_steps(wo_low), 0)
        mlp_flows.append(pipe.add(links.shared_steps(sends[1], False), 0))
        pipe.reach(qkv_flow, beside(1), gap=5)
        near_flow = pipe.add(links.near_steps(attn_low), 0)
        small_full = vec_flow.value.transpose(1, 0, 2).reshape(16, D)
        pipe.start(12)
        (h1,) = pipe.tie([first_norm(small_full)])
        pipe.now = max(flow.ready for flow in pipe.flows if flow.flying)
        pipe.land()
        after = pipe.finish(qkv_flow, vec_flow, near_flow, window=13, gap=14)
        attn_near, ((attn_far, behind),) = near_flow.value, qkv_flow.value
        wqkv = [Piece(array, 0, 0) for array in (attn_low, attn_near, attn_far, behind)]
    else:
        attn_low, mlp_low = attn_w.astype(BF16), mlp_w.astype(BF16)
        gather = lambda array, axis: lax.all_gather(array, "shard", axis=axis, tiled=True)
        attn_full, mlp_full = gather(attn_low, 0), gather(mlp_low, 0)
        small_full = gather(small_low, 1)
        wqkv = [Piece(attn_full, j, 0) for j in range(BLOCKS)]
        wo = [Piece(attn_full, j, 3) for j in range(BLOCKS)]
        wups = [[Piece(mlp_full, j, p) for j in range(BLOCKS)] for p in range(PARTS)]
        wdns = [[Piece(mlp_full, j, 4 + p) for j in range(BLOCKS)] for p in range(PARTS)]
        after = []
        h1 = first_norm(small_full)
    vec = small_full.astype(F32)

    totals = []

    def summed(send, keep, urgent=False):
        if links.direct:
            return pipe.add(links.part_steps(send, keep), 1 if urgent else 2)
        return (send, keep)

    def chunk(name, *parts):
        if links.direct:
            totals.append((name, pipe.add(links.chunk_steps(parts), 1 if name[0] == "attn" else 2)))
            return
        stacked = [jnp.stack([k[0], s[0], k[1], s[1]]).reshape(D, -1) for s, k in parts]
        part = lax.psum_scatter(
            jnp.concatenate(stacked, axis=1), "shard", scatter_dimension=0, tiled=True
        )
        part = lax.psum(part, "replica")
        totals.append((name, (part[: part.shape[0] // 2], part[part.shape[0] // 2 :])))

    qkv = qkv_forward(order, h1, wqkv, vec, after)
    pipe.spend(15, qkv)
    if links.direct:
        mlp_near_flow = pipe.add(links.near_steps(mlp_low), 0)
    mixed = attn_mix(kept_count, qkv, images, pipe.turn(17))
    pipe.spend(17, mixed)
    if links.direct:
        after = pipe.finish(wo_flow, window=10, gap=16)
        wo_far, behind = wo_flow.value
        wo = [Piece(attn_low, 0, 3), Piece(attn_near, 0, 3), Piece(wo_far, 0, 0), Piece(behind, 0, 0)]
    middle, h2 = out_project(order, tokens, mixed, wo, vec, after)
    pipe.spend(10, h2)

    acts, dpres, gbus = [], [], []
    if links.direct:
        wups, wdns = [], []
    for p in range(PARTS):
        if links.direct:
            flow = mlp_flows[p // 2]
            after = pipe.finish(flow, mlp_near_flow, window=17)
            far, behind = flow.value[p % 2]
            near = [(mlp_low, p, 4 + p), (mlp_near_flow.value, p, 4 + p)]
            four = [*near, (far, 0, 1), (behind, 0, 1)]
            wups.append([Piece(array, 0, up) for array, up, _ in four])
            wdns.append([Piece(array, 0, down) for array, _, down in four])
        act, dpre, send, keep, gbu = mlp_part(
            order, h2, gy, wups[p], wdns[p], vec[8 + p : 9 + p], after
        )
        acts.append(act)
        dpres.append(dpre)
        gbus.append(gbu)
        pipe.spend(17, gbu)
        part = summed(send, keep)
        if p == PARTS - 1:
            chunk(("mlp", 3 + p, p - 1, 4 + p, p), before, part)
        elif p < PARTS - 2:
            chunk(("mlp", 4 + p, p), part)
        before = part
        if p == 0 and links.direct:
            pipe.reach(part, "y/", alone=True)
    da, two_sums, send, keep = mlp_back(
        order, dpres, wups, middle, gy, vec, mixed, pipe.turn(26)
    )
    pipe.spend(26, two_sums)
    out_part = summed(send, keep)

    split = images // 2
    dqkv, sums_a = attn_back(order, kept_count, da, wo, qkv, slots, 0, split, None, pipe.turn(19))
    pipe.spend(19, sums_a)
    dqkv, sums_b = attn_back(
        order, kept_count, da, wo, qkv, slots, split, images - split, dqkv, pipe.turn(19)
    )
    pipe.spend(19, sums_b)
    qkv_sums = sums_a + sums_b
    send, keep = kv_grad(order, h1, dqkv, pipe.turn(14))
    pipe.spend(14, send)
    kv_part = summed(send, keep, True)
    chunk(("attn", 1, 2), kv_part)
    if links.direct:
        pipe.reach(kv_part, "y/", alone=True)
    in_grad, one_sums = input_back(order, dqkv, wqkv, tokens, da, vec, pipe.turn(19))
    pipe.spend(19, one_sums)

    small = jnp.concatenate(
        [
            one_sums[0:2],
            qkv_sums[0:1],
            qkv_sums[2:3],
            two_sums[2:3],
            two_sums[0:2],
            two_sums[3:4],
            *gbus,
            jnp.zeros((4, D), F32),
        ],
        axis=0,
    )
    send, keep = query_grad(order, h1, dqkv, small, pipe.turn(10))
    pipe.spend(10, send)
    chunk(("attn", 3, 0), out_part, summed(send, keep, True))
    result = mlp_out(order, acts, wdns, middle, valid.astype(F32), vec, pipe.turn(17))
    pipe.spend(17, result)
    result = result.reshape(images, slots, D)

    outs = {"attn": [], "mlp": []}
    state = {
        "attn": (attn_w, attn_m, attn_v, image_total, 0.1, 0.05),
        "mlp": (mlp_w, mlp_m, mlp_v, image_total, 0.05, 0.05),
    }
    small_out, pieces = None, []
    second = (links.place(1) if links.direct else jnp.zeros((), jnp.int32)).reshape(1)
    while totals or pieces:
        after = pipe.turn()
        through = lambda total: not isinstance(total, Flow) or total.done
        for name, total in [entry for entry in totals if through(entry[1])]:
            total = total.value if isinstance(total, Flow) else total
            if total[0].shape[1] % D:
                some = [half[:, 2 * D : 2 * D + 12] for half in total]
                gradient = jnp.where(
                    second[0] == 1, jnp.concatenate(some[::-1]), jnp.concatenate(some)
                )
                gradient = gradient.astype(F32) / image_total
                small_out = adam_terms(vectors, small_m, small_v, gradient, 1.0, 0.0)
            pieces += [(name[0], total, n, column) for n, column in enumerate(name[1:])]
        totals = [entry for entry in totals if not through(entry[1])]
        wait = pipe.wait() if totals else 1000.0
        kind, total, first, _ = pieces[0] if pieces else (None,) * 4
        fit = 1 if totals else 4
        columns = [c for k, t, _, c in pieces if t is total][:fit]
        if columns:
            outs[kind], mark = adam_part(total, second, first, columns, *state[kind], outs[kind], after)
            pipe.spend(1.0 + 3.2 * len(columns), mark)
            pieces = pieces[len(columns) :]
        elif totals:
            pipe.skip(1.5)
    attn_out, mlp_out_ = outs["attn"], outs["mlp"]
    return (result, in_grad, *attn_out, *mlp_out_, *small_out)


def solution(mesh):
    tokens = P(("replica", "shard"), None, None)
    owned = P("shard", None)
    in_specs = (tokens, tokens, P(("replica", "shard")), *[owned] * 9)
    out_specs = (tokens, tokens, *[owned] * 15)
    return jax.shard_map(
        on_device, mesh=mesh, in_specs=in_specs, out_specs=out_specs, check_vma=False
    )
```

```python
import jax
import jax.numpy as jnp
from jax import lax
from jax.experimental import pallas as pl
from jax.experimental.pallas import tpu as pltpu
from jax.sharding import PartitionSpec as P

D = 1024
HEADS = 16
HEAD_DIM = 64
FF = 4096
BUF = 64
STEP = 10
BLOCKS = 4
BLOCK = D // BLOCKS
PARTS = 4
PART = FF // PARTS
GROUP = 4
GROUP_W = GROUP * HEAD_DIM

EPS_NORM = 1e-06
MASKED = -1000000000.0
BETA_ONE = 0.9
BETA_TWO = 0.999
EPS_ADAM = 1e-08

BF16 = jnp.bfloat16
F32 = jnp.float32
MIB = 1 << 20


def normalize(values):
    average = jnp.mean(values, axis=-1, keepdims=True)
    centred = values - average
    inverse = lax.rsqrt(jnp.mean(centred * centred, axis=-1, keepdims=True) + EPS_NORM)
    return (centred * inverse, inverse)


def norm_back(upstream, normed, inverse):
    first_term = jnp.mean(upstream, axis=-1, keepdims=True)
    second_term = normed * jnp.mean(upstream * normed, axis=-1, keepdims=True)
    return inverse * (upstream - first_term - second_term)


def dot(left, right):
    return jnp.dot(left, right, preferred_element_type=F32)


def dot_nt(left, right):
    return lax.dot_general(left, right, (((1,), (1,)), ((), ())), preferred_element_type=F32)


def dot_tn(left, right):
    return lax.dot_general(left, right, (((0,), (0,)), ((), ())), preferred_element_type=F32)


def gelu_pair(values):
    size = jnp.abs(values)
    denominator = 1.0 + size * (0.3275911 * 0.7071067811865476)
    ratio = pl.reciprocal(denominator, approx=True)
    ratio = ratio * (2.0 - denominator * ratio)
    bell = jnp.exp(values * values * (-0.5))
    poly = 0.5 * 1.061405429 * ratio - 0.5 * 1.453152027
    poly = poly * ratio + 0.5 * 1.421413741
    poly = poly * ratio - 0.5 * 0.284496736
    poly = poly * ratio + 0.5 * 0.254829592
    tail = poly * ratio * bell
    below = jnp.where(values >= 0, 1.0 - tail, tail)
    return (values * below, below + values * bell * 0.3989422804014327)


def whole(array):
    rank = len(array.shape)
    return pl.BlockSpec(array.shape, lambda *_: (0,) * rank, pipeline_mode=pl.Buffered(1))


def params(limit):
    return pltpu.CompilerParams(vmem_limit_bytes=limit * MIB)


def cost(flops, nbytes):
    return pl.CostEstimate(flops=int(flops), bytes_accessed=int(nbytes), transcendentals=0)


def call(body, *, scalars, ins, in_specs, outs, out_specs, grid, name, limit, work, scratch=(), after=(), aliases=None):
    first = len(scalars) + len(ins)
    ins = [
        pltpu.with_memory_space_constraint(a, pltpu.HBM)
        if a.size * a.dtype.itemsize >= MIB // 4
        else a
        for a in ins
    ]

    def with_after(*refs):
        body(*refs[:first], *refs[first + len(after) :])

    return pl.pallas_call(
        with_after,
        grid_spec=pltpu.PrefetchScalarGridSpec(
            num_scalar_prefetch=len(scalars),
            grid=grid,
            in_specs=[*in_specs, *[pl.BlockSpec(memory_space=pl.ANY)] * len(after)],
            out_specs=out_specs,
            scratch_shapes=list(scratch),
        ),
        out_shape=outs,
        input_output_aliases=aliases or {},
        compiler_params=params(limit),
        cost_estimate=cost(*work),
        name=name,
    )(*scalars, *ins, *after)


def like(shape, dtype):
    return pltpu.HBM(shape, dtype)


def place(order_ref, target, pieces):
    for j, piece in enumerate(pieces):
        at = pl.multiple_of(order_ref[j] * BLOCK, BLOCK)
        target[pl.ds(at, BLOCK), :] = piece[...]


ANY = pl.BlockSpec(memory_space=pl.ANY)


class Piece:
    def __init__(self, array, row, column):
        self.array, self.row, self.column = array, row, column

    def spec(self, width):
        return pl.BlockSpec(
            (BLOCK, width), lambda *_: (self.row, self.column), pipeline_mode=pl.Buffered(1)
        )

    def view(self, ref, width):
        return ref.at[
            self.row * BLOCK : (self.row + 1) * BLOCK,
            self.column * width : (self.column + 1) * width,
        ]


def arrays(pieces):
    return [piece.array for piece in pieces]


def heads_apart(values, scale=None):
    lane = lax.broadcasted_iota(jnp.int32, values.shape, 1) // HEAD_DIM
    if scale is not None:
        values = values * jnp.asarray(scale, values.dtype)
    zero = jnp.zeros_like(values)
    return jnp.concatenate([jnp.where(lane == h, values, zero) for h in range(GROUP)], axis=0)


def heads_together(values, slots):
    lane = lax.broadcasted_iota(jnp.int32, (slots, GROUP_W), 1) // HEAD_DIM
    out = values[:slots]
    for h in range(1, GROUP):
        out = jnp.where(lane == h, values[h * slots : (h + 1) * slots], out)
    return out


def probs_of(keys, queries_apart, shift):
    scores = dot_nt(keys, queries_apart) + shift
    scores = jnp.exp(scores - jnp.max(scores, axis=0, keepdims=True))
    return scores * (1.0 / jnp.sum(scores, axis=0, keepdims=True))


def key_shift(kept, slots):
    at = lax.broadcasted_iota(jnp.int32, (slots, 1), 0)
    return jnp.where(at < BUF + kept, 0.0, MASKED).astype(F32)


def row_spec(slots, width):
    return pl.BlockSpec((slots, width), lambda i, *_: (i, 0))


def qkv_forward(order, h1, wqkv, vec, after, width=512):
    rows = h1.shape[0]

    def body(order_ref, h1_ref, *refs):
        w_refs, (bias_ref, qkv_ref, w_s) = refs[:BLOCKS], refs[BLOCKS:]
        place(order_ref, w_s, w_refs)
        qkv_ref[...] = (dot(h1_ref[...], w_s[...]) + bias_ref[...]).astype(BF16)

    bias = jnp.concatenate([vec[2:3], jnp.zeros_like(vec[2:3]), vec[3:4]], axis=1)
    return call(
        body,
        scalars=[order],
        ins=[h1, *arrays(wqkv), bias],
        in_specs=[whole(h1)]
        + [pl.BlockSpec((BLOCK, width), lambda i, *_, row=w.row: (row, i)) for w in wqkv]
        + [pl.BlockSpec((1, width), lambda i, *_: (0, i))],
        outs=[like((rows, 3 * D), BF16)],
        out_specs=[pl.BlockSpec((rows, width), lambda i, *_: (0, i))],
        scratch=[pltpu.VMEM((D, width), BF16)],
        grid=(3 * D // width,),
        name="qkv_forward",
        limit=30,
        work=(10 * rows * D * D, 18 * MIB),
        after=after,
    )[0]


def attn_mix(kept, qkv, images, after):
    rows = qkv.shape[0]
    slots = rows // images

    def body(kept_ref, qkv_ref, mixed_ref):
        shift = key_shift(kept_ref[pl.program_id(0)], slots)
        for g in range(HEADS // GROUP):
            at = g * GROUP_W
            q, k, v = (qkv_ref[:, n * D + at : n * D + at + GROUP_W] for n in range(3))
            probs = probs_of(k, heads_apart(q, HEAD_DIM**-0.5), shift).astype(BF16)
            mixed_ref[:, at : at + GROUP_W] = heads_together(dot_tn(probs, v), slots).astype(BF16)

    return call(
        body,
        scalars=[kept],
        ins=[qkv],
        in_specs=[row_spec(slots, 3 * D)],
        outs=[like((rows, D), BF16)],
        out_specs=[row_spec(slots, D)],
        grid=(images,),
        name="attn_mix",
        limit=30,
        work=(14 * rows * D * D, 8 * MIB),
        after=after,
    )[0]


def out_project(order, x, mixed, wo, vec, after):
    images, slots, _ = x.shape
    rows = images * slots

    def body(order_ref, x_ref, mixed_ref, *refs):
        wo_refs, (vec_ref, middle_ref, h2_ref, wo_s) = refs[:BLOCKS], refs[BLOCKS:]

        @pl.when(pl.program_id(0) == 0)
        def _():
            place(order_ref, wo_s, wo_refs)

        branch = dot(mixed_ref[...], wo_s[...]) + vec_ref[4:5, :]
        for n in range(2):
            span = slice(n * slots, (n + 1) * slots)
            middle = x_ref[n].astype(F32) + branch[span]
            middle_ref[span, :] = middle
            normed, _ = normalize(middle)
            h2_ref[span, :] = (normed * vec_ref[5:6, :] + vec_ref[6:7, :]).astype(BF16)

    return call(
        body,
        scalars=[order],
        ins=[x, mixed, *arrays(wo), vec],
        in_specs=[pl.BlockSpec((2, slots, D), lambda i, *_: (i, 0, 0)), row_spec(2 * slots, D)]
        + [w.spec(D) for w in wo]
        + [whole(vec)],
        outs=[like((rows, D), F32), like((rows, D), BF16)],
        out_specs=[row_spec(2 * slots, D)] * 2,
        scratch=[pltpu.VMEM((D, D), BF16)],
        grid=(images // 2,),
        name="out_project",
        limit=30,
        work=(6 * rows * D * D, 12 * MIB),
        after=after,
    )


def mlp_part(order, h2, dm, wup, wdn, bu, after, width=512):
    rows = h2.shape[0]
    weights = [*wup, *wdn]

    def body(order_ref, h2_hbm, dm_hbm, *refs):
        weight_refs, (bu_ref, *outs, gbu_ref) = refs[: 2 * BLOCKS], refs[2 * BLOCKS : -10]
        h2_ref, dm_ref, up_s, dn_s, act_ref, dpre_ref, send, keep, in_sems, out_sems = refs[-10:]
        flying = []

        def put(n, source, index):
            copy = pltpu.make_async_copy(
                source.at[index], outs[n].at[index], out_sems.at[len(flying)]
            )
            copy.start()
            flying.append(copy)

        def fetch(n, source, target, first):
            copies = [pltpu.make_async_copy(source, target, in_sems.at[n])]
            for j in range(BLOCKS):
                at = pl.multiple_of(order_ref[j] * BLOCK, BLOCK)
                copies.append(
                    pltpu.make_async_copy(
                        weights[first + j].view(weight_refs[first + j], PART),
                        (dn_s if first else up_s).at[pl.ds(at, BLOCK), :],
                        in_sems.at[n + 1 + j],
                    )
                )
            for copy in copies:
                copy.start()
            return copies

        def arrive(copies):
            for copy in copies:
                copy.wait()

        ups = fetch(0, h2_hbm, h2_ref, 0)
        dns = fetch(1 + BLOCKS, dm_hbm, dm_ref, BLOCKS)

        def front(n, span):
            if n == 0:
                arrive(ups)
            pre = dot(h2_ref[...], up_s[:, span]) + bu_ref[:, span]
            if n == 0:
                arrive(dns)
            return (pre, dot(dm_ref[...], dn_s[:, span]))

        def middle(span, pre, dact):
            act, slope = gelu_pair(pre)
            act = act.astype(BF16)
            dpre = (dact * slope).astype(BF16)
            act_ref[:, span] = act
            dpre_ref[:, span] = dpre
            gbu_ref[:, span] = jnp.sum(dpre.astype(F32), axis=0, keepdims=True)
            return (act, dpre)

        def back(span, act, dpre):
            for first, left_ref, right in ((0, dm_ref, act), (PART, h2_ref, dpre)):
                there = slice(first + span.start, first + span.stop)
                for j in range(BLOCKS):
                    at = pl.multiple_of(order_ref[j] * BLOCK, BLOCK)
                    grad = dot_tn(left_ref[:, pl.ds(at, BLOCK)], right).astype(BF16)
                    (send if j % 2 else keep)[j // 2, :, there] = grad

        def out(span):
            put(0, act_ref, (slice(None), span))
            put(1, dpre_ref, (slice(None), span))
            for first in (0, PART):
                there = slice(first + span.start, first + span.stop)
                put(2, send, (slice(None), slice(None), there))
                put(3, keep, (slice(None), slice(None), there))

        spans = [slice(at, at + width) for at in range(0, PART, width)]
        fresh = front(0, spans[0])
        held = None
        for n, span in enumerate(spans):
            later = front(n + 1, spans[n + 1]) if n + 1 < len(spans) else None
            now = middle(span, *fresh)
            if held is not None:
                back(spans[n - 1], *held)
                out(spans[n - 1])
            held, fresh = now, later
        back(spans[-1], *held)
        out(spans[-1])
        for copy in flying:
            copy.wait()

    one = pl.BlockSpec((1, PART), lambda i, *_: (0, 0))
    return call(
        body,
        scalars=[order],
        ins=[h2, dm, *arrays(weights), bu],
        in_specs=[ANY] * (2 + len(weights)) + [whole(bu)],
        outs=[like((rows, PART), BF16)] * 2
        + [like((2, BLOCK, 2 * PART), BF16)] * 2
        + [like((1, PART), F32)],
        out_specs=[ANY] * 4 + [one],
        scratch=[pltpu.VMEM((rows, D), BF16)] * 2
        + [pltpu.VMEM((D, PART), BF16)] * 2
        + [pltpu.VMEM((rows, PART), BF16)] * 2
        + [pltpu.VMEM((2, BLOCK, 2 * PART), BF16)] * 2
        + [
            pltpu.SemaphoreType.DMA((2 + 2 * BLOCKS,)),
            pltpu.SemaphoreType.DMA((PART // width * 6,)),
        ],
        grid=(1,),
        name="mlp_part",
        limit=40,
        work=(12 * rows * D * PART, 12 * MIB),
        after=after,
    )


def streamed(order_ref, sides, side_refs, weights, weight_refs, side_s, weight_s, sems, use):
    def copies(p):
        slot = p % 2
        yield pltpu.make_async_copy(side_refs[p], side_s.at[slot], sems.at[slot, BLOCKS])
        for j in range(BLOCKS):
            at = pl.multiple_of(order_ref[j] * BLOCK, BLOCK)
            piece = weights[p][j]
            yield pltpu.make_async_copy(
                piece.view(weight_refs[p * BLOCKS + j], PART),
                weight_s.at[slot, pl.ds(at, BLOCK), :],
                sems.at[slot, j],
            )

    for copy in copies(0):
        copy.start()
    for p in range(PARTS):
        if p + 1 < PARTS:
            for copy in copies(p + 1):
                copy.start()
        for copy in copies(p):
            copy.wait()
        use(p, side_s[p % 2], weight_s[p % 2])


def stream_scratch(rows):
    return [
        pltpu.VMEM((2, rows, PART), BF16),
        pltpu.VMEM((2, D, PART), BF16),
        pltpu.SemaphoreType.DMA((2, BLOCKS + 1)),
        pltpu.VMEM((rows, D), F32),
        pltpu.VMEM((rows, D), F32),
        pltpu.SemaphoreType.DMA((1,)),
    ]


def mlp_back(order, dpres, wups, middle, gy, vec, mixed, after):
    rows = middle.shape[0]
    flat = [w for part in wups for w in part]

    def body(order_ref, *refs):
        dpre_refs, refs = refs[:PARTS], refs[PARTS:]
        up_refs, refs = refs[: PARTS * BLOCKS], refs[PARTS * BLOCKS :]
        middle_ref, gy_ref, vec_ref, mixed_ref, da_ref, sums_ref, send, keep = refs[:8]
        side_s, weight_s, sems, acc, middle_s, middle_sem = refs[8:]

        def use(p, side, weight):
            if p == 0:
                pltpu.make_async_copy(middle_ref, middle_s, middle_sem.at[0]).start()
                acc[...] = dot_nt(side, weight)
            else:
                acc[...] += dot_nt(side, weight)

        streamed(order_ref, dpres, dpre_refs, wups, up_refs, side_s, weight_s, sems, use)
        pltpu.make_async_copy(middle_ref, middle_s, middle_sem.at[0]).wait()
        gain, shift, bias, down = (jnp.zeros((1, D), F32) for _ in range(4))
        step = rows // 6
        for r in range(0, rows, step):
            span = slice(r, r + step)
            dh2 = acc[span, :]
            normed, inverse = normalize(middle_s[span, :])
            gain += jnp.sum(dh2 * normed, axis=0, keepdims=True)
            shift += jnp.sum(dh2, axis=0, keepdims=True)
            dmid = norm_back(dh2 * vec_ref[5:6, :], normed, inverse) + gy_ref[span, :].astype(F32)
            da = dmid.astype(BF16)
            da_ref[span, :] = da
            bias += jnp.sum(da.astype(F32), axis=0, keepdims=True)
            down += jnp.sum(gy_ref[span, :].astype(F32), axis=0, keepdims=True)
        sums_ref[...] = jnp.concatenate([gain, shift, bias, down, jnp.zeros((4, D), F32)], axis=0)
        for j in range(BLOCKS):
            at = pl.multiple_of(order_ref[j] * BLOCK, BLOCK)
            grad = dot_tn(mixed_ref[:, pl.ds(at, BLOCK)], da_ref[...]).astype(BF16)
            (send if j % 2 else keep)[j // 2] = grad

    return call(
        body,
        scalars=[order],
        ins=[*dpres, *arrays(flat), middle, gy, vec, mixed],
        in_specs=[ANY] * (PARTS + len(flat) + 1) + [whole(gy), whole(vec), whole(mixed)],
        outs=[like((rows, D), BF16), like((8, D), F32)]
        + [like((2, BLOCK, D), BF16)] * 2,
        out_specs=[
            pl.BlockSpec((rows, D), lambda i, *_: (0, 0)),
            pl.BlockSpec((8, D), lambda i, *_: (0, 0)),
            pl.BlockSpec((2, BLOCK, D), lambda i, *_: (0, 0, 0)),
            pl.BlockSpec((2, BLOCK, D), lambda i, *_: (0, 0, 0)),
        ],
        scratch=stream_scratch(rows),
        grid=(1,),
        name="mlp_back",
        limit=40,
        work=(3 * rows * D * FF, 30 * MIB),
        after=after,
    )


def mlp_out(order, acts, wdns, middle, valid, vec, after):
    rows = middle.shape[0]
    flat = [w for part in wdns for w in part]

    def body(order_ref, *refs):
        act_refs, refs = refs[:PARTS], refs[PARTS:]
        dn_refs, refs = refs[: PARTS * BLOCKS], refs[PARTS * BLOCKS :]
        middle_ref, valid_ref, vec_ref, out_ref = refs[:4]
        side_s, weight_s, sems, acc, middle_s, middle_sem = refs[4:]

        def use(p, side, weight):
            if p == 0:
                pltpu.make_async_copy(middle_ref, middle_s, middle_sem.at[0]).start()
                acc[...] = dot_nt(side, weight)
            elif p + 1 < PARTS:
                acc[...] += dot_nt(side, weight)
            else:
                pltpu.make_async_copy(middle_ref, middle_s, middle_sem.at[0]).wait()
                total = acc[...] + dot_nt(side, weight) + middle_s[...] + vec_ref[7:8, :]
                out_ref[...] = (total * valid_ref[...]).astype(BF16)

        streamed(order_ref, acts, act_refs, wdns, dn_refs, side_s, weight_s, sems, use)

    return call(
        body,
        scalars=[order],
        ins=[*acts, *arrays(flat), middle, valid, vec],
        in_specs=[ANY] * (PARTS + len(flat) + 1) + [whole(valid), whole(vec)],
        outs=[like((rows, D), BF16)],
        out_specs=[pl.BlockSpec((rows, D), lambda i, *_: (0, 0))],
        scratch=stream_scratch(rows),
        grid=(1,),
        name="mlp_out",
        limit=40,
        work=(3 * rows * D * FF, 24 * MIB),
        after=after,
    )[0]


def attn_back(order, kept, da, wo, qkv, slots, first, count, before, after):
    rows = da.shape[0]

    def body(order_ref, kept_ref, da_ref, *refs):
        wo_refs, refs = refs[:BLOCKS], refs[BLOCKS:]
        qkv_ref, dqkv_ref, sums_ref, wo_s = refs[0], *refs[-3:]
        image = pl.program_id(0)

        @pl.when(image == 0)
        def _():
            place(order_ref, wo_s, wo_refs)
            sums_ref[...] = jnp.zeros_like(sums_ref)

        shift = key_shift(kept_ref[first + image], slots)
        da = da_ref[...]
        scale = HEAD_DIM**-0.5
        for g in range(HEADS // GROUP):
            at = g * GROUP_W
            spans = [slice(n * D + at, n * D + at + GROUP_W) for n in range(3)]
            q, k, v = (qkv_ref[:, span] for span in spans)
            dmix = dot_nt(da, wo_s[at : at + GROUP_W, :]).astype(BF16)
            apart = heads_apart(q, scale)
            probs = probs_of(k, apart, shift)
            dmix_apart = heads_apart(dmix)
            dv = dot(probs.astype(BF16), dmix_apart).astype(BF16)
            dprob = dot_nt(v, dmix_apart)
            product = probs * dprob
            dsc = (product - probs * jnp.sum(product, axis=0, keepdims=True)).astype(BF16)
            dk = dot(dsc, apart).astype(BF16)
            dq = (heads_together(dot_tn(dsc, k), slots) * scale).astype(BF16)
            for n, grad in enumerate((dq, dk, dv)):
                dqkv_ref[:, spans[n]] = grad
                if n != 1:
                    sums_ref[n : n + 1, at : at + GROUP_W] += jnp.sum(
                        grad.astype(F32), axis=0, keepdims=True
                    )

    row = lambda width: pl.BlockSpec((slots, width), lambda i, *_: (first + i, 0))
    extra = [] if before is None else [before]
    return call(
        body,
        scalars=[order, kept],
        ins=[da, *arrays(wo), qkv, *extra],
        in_specs=[row(D)]
        + [w.spec(D) for w in wo]
        + [row(3 * D)]
        + [pl.BlockSpec(memory_space=pl.ANY)] * len(extra),
        outs=[like((rows, 3 * D), BF16), like((8, D), F32)],
        out_specs=[row(3 * D), pl.BlockSpec((8, D), lambda i, *_: (0, 0))],
        scratch=[pltpu.VMEM((D, D), BF16)],
        grid=(count,),
        aliases={4 + BLOCKS: 0} if extra else None,
        name="attn_back",
        limit=30,
        work=(12 * rows * D * D, 18 * MIB),
        after=after,
    )


def input_back(order, dqkv, wqkv, x, da, vec, after):
    images, slots, _ = x.shape
    rows = images * slots

    def body(order_ref, dqkv_ref, *refs):
        wq_refs = refs[:BLOCKS]
        x_ref, da_ref, vec_ref, out_ref, sums_ref, acc = refs[BLOCKS:]

        @pl.when(pl.program_id(0) == 0)
        def _():
            sums_ref[...] = jnp.zeros_like(sums_ref)

        grad = dqkv_ref[...]
        for j in range(BLOCKS):
            at = pl.multiple_of(order_ref[j] * BLOCK, BLOCK)
            acc[:, pl.ds(at, BLOCK)] = dot_nt(grad, wq_refs[j][...])
        for n in range(2):
            dh1 = acc[n * slots : (n + 1) * slots, :]
            normed, inverse = normalize(x_ref[n].astype(F32))
            sums_ref[0:1, :] += jnp.sum(dh1 * normed, axis=0, keepdims=True)
            sums_ref[1:2, :] += jnp.sum(dh1, axis=0, keepdims=True)
            total = norm_back(dh1 * vec_ref[0:1, :], normed, inverse)
            out_ref[n] = (total + da_ref[n * slots : (n + 1) * slots, :].astype(F32)).astype(BF16)

    image = pl.BlockSpec((2, slots, D), lambda i, *_: (i, 0, 0))
    return call(
        body,
        scalars=[order],
        ins=[dqkv, *arrays(wqkv), x, da, vec],
        in_specs=[row_spec(2 * slots, 3 * D)]
        + [w.spec(3 * D) for w in wqkv]
        + [image, row_spec(2 * slots, D), whole(vec)],
        outs=[like((images, slots, D), BF16), like((8, D), F32)],
        out_specs=[image, pl.BlockSpec((8, D), lambda i, *_: (0, 0))],
        scratch=[pltpu.VMEM((2 * slots, D), F32)],
        grid=(images // 2,),
        name="input_back",
        limit=30,
        work=(8 * rows * D * D, 24 * MIB),
        after=after,
    )


def kv_grad(order, left, right, after, width=512):
    rows = right.shape[0]
    steps = D // width

    def body(order_ref, left_ref, right_ref, send, keep):
        for j in range(BLOCKS):
            at = pl.multiple_of(order_ref[j] * BLOCK, BLOCK)
            grad = dot_tn(left_ref[:, pl.ds(at, BLOCK)], right_ref[...]).astype(BF16)
            (send if j % 2 else keep)[j // 2] = grad

    grads = pl.BlockSpec((2, BLOCK, width), lambda i, *_: (0, 0, i))
    return call(
        body,
        scalars=[order],
        ins=[left, right],
        in_specs=[whole(left), pl.BlockSpec((rows, width), lambda i, *_: (0, steps + i))],
        outs=[like((2, BLOCK, 2 * D), BF16)] * 2,
        out_specs=[grads] * 2,
        grid=(2 * steps,),
        name="kv_grad",
        limit=30,
        work=(8 * rows * D * D, 16 * MIB),
        after=after,
    )


def query_grad(order, left, right, small, after):
    rows = right.shape[0]
    columns = D + 128

    def body(order_ref, left_ref, right_ref, small_ref, send, keep):
        for j in range(BLOCKS):
            at = pl.multiple_of(order_ref[j] * BLOCK, BLOCK)
            target = send if j % 2 else keep
            grad = dot_tn(left_ref[:, pl.ds(at, BLOCK)], right_ref[...]).astype(BF16)
            target[j // 2, :, :D] = grad
            some = small_ref[:, pl.ds(at, BLOCK)]
            some = jnp.concatenate([some, jnp.zeros((112, BLOCK), F32)], axis=0)
            target[j // 2, :, D:] = some.T.astype(BF16)

    out = pl.BlockSpec((2, BLOCK, columns), lambda i, *_: (0, 0, 0))
    return call(
        body,
        scalars=[order],
        ins=[left, right, small],
        in_specs=[whole(left), pl.BlockSpec((rows, D), lambda i, *_: (0, 0)), whole(small)],
        outs=[like((2, BLOCK, columns), BF16)] * 2,
        out_specs=[out] * 2,
        grid=(1,),
        name="query_grad",
        limit=30,
        work=(6 * rows * D * D, 10 * MIB),
        after=after,
    )


def adam_terms(weight, first_mom, second_mom, gradient, rate, decay):
    first_new = BETA_ONE * first_mom + (1.0 - BETA_ONE) * gradient
    second_new = BETA_TWO * second_mom + (1.0 - BETA_TWO) * gradient * gradient
    first_hat = first_new * (1.0 / (1.0 - BETA_ONE**STEP))
    second_hat = second_new * (1.0 / (1.0 - BETA_TWO**STEP))
    weight_new = weight - rate * (first_hat / (jnp.sqrt(second_hat) + EPS_ADAM) + decay * weight)
    return (gradient, first_new, second_new, weight_new, weight_new.astype(BF16))


def adam_part(halves, second, first, columns, weight, first_mom, second_mom, count, rate, decay, before, after):
    half = halves[0].shape[0]
    rows = 2 * half
    width = D if len(columns) > 1 else D // 2
    steps = D // width

    def body(columns_ref, second_ref, a_ref, b_ref, w_ref, m_ref, v_ref, *refs):
        lower = second_ref[0] == 1
        a, b = (ref[...].astype(F32) * (1.0 / count) for ref in (a_ref, b_ref))
        for n, gradient in enumerate((jnp.where(lower, b, a), jnp.where(lower, a, b))):
            span = slice(n * half, (n + 1) * half)
            terms = (w_ref[span, :], m_ref[span, :], v_ref[span, :])
            outs = adam_terms(*terms, gradient, rate, decay)
            for ref, value in zip(refs[-6:], outs):
                ref[span, :] = value
        refs[-1][...] = jnp.zeros_like(refs[-1])

    there = pl.BlockSpec((rows, width), lambda i, n, where, _: (0, where[i] * steps + n))
    shape = weight.shape
    *outs, mark = call(
        body,
        scalars=[jnp.array(columns, jnp.int32), second],
        ins=[*halves, weight, first_mom, second_mom, *before],
        in_specs=[pl.BlockSpec((half, width), lambda i, n, *_: (0, (first + i) * steps + n))] * 2
        + [there] * 3
        + [ANY] * len(before),
        outs=[jax.ShapeDtypeStruct(shape, F32)] * 4
        + [jax.ShapeDtypeStruct(shape, BF16), jax.ShapeDtypeStruct((8, 128), F32)],
        out_specs=[there] * 5 + [pl.BlockSpec((8, 128), lambda i, n, *_: (0, 0))],
        grid=(len(columns), steps),
        aliases={7 + n: n for n in range(len(before))},
        name="adam_part",
        limit=30,
        work=(3 * MIB * 1024 * len(columns), 10 * MIB),
        after=after,
    )
    return (outs, mark)


def swap(values, axis, bit):
    size = lax.axis_size(axis)
    return lax.ppermute(values, axis, [(i, i ^ bit) for i in range(size)])


def bits_of(size):
    return [1 << n for n in range(size.bit_length() - 1)]


def beside(bit):
    return "x" if bit == 1 else f"z{bit}"


def added(terms):
    return sum(t.astype(F32) for t in terms).astype(BF16)


class Links:
    def __init__(self):
        self.shards = lax.axis_size("shard")
        self.replicas = lax.axis_size("replica")
        self.direct = self.shards == BLOCKS and self.replicas >= 4
        self.direct = self.direct and self.replicas & (self.replicas - 1) == 0
        index = jnp.arange(BLOCKS, dtype=jnp.int32)
        self.order = index ^ lax.axis_index("shard") if self.direct else index
        self.replica = lax.axis_index("replica")

    def bit(self, bit):
        return (self.replica & bit) != 0

    def place(self, bit):
        return self.bit(bit).astype(jnp.int32)

    def both(self, bit, mine, other, axis):
        return jnp.where(
            self.bit(bit),
            jnp.concatenate([other, mine], axis=axis),
            jnp.concatenate([mine, other], axis=axis),
        )


    def halving(self, terms, bits):
        for bit in bits:
            half = terms[0].shape[1] // 2
            up = self.place(bit)
            size = (1, half, terms[0].shape[2])
            piece = lambda at: [lax.dynamic_slice(t, (0, at * half, 0), size) for t in terms]
            (got,) = yield [(beside(bit), "replica", bit, added(piece(1 - up)))]
            terms = piece(up) + [got]
        return terms

    def part_steps(self, send, keep):
        (got,) = yield [("core", "shard", 1, send)]
        terms = [keep, got]
        (got,) = yield [("y/", "shard", 2, added([t[1] for t in terms]))]
        terms += [got[None]]
        terms = yield from self.halving(terms, bits_of(self.replicas)[:1])
        return added(terms)

    def chunk_steps(self, parts):
        while not all(part.done for part in parts):
            yield []
        bits = bits_of(self.replicas)
        terms = [jnp.concatenate([part.value for part in parts], axis=2)]
        terms = yield from self.halving(terms, bits[1:])
        now = added(terms)[0]
        for bit in reversed(bits[1:]):
            (got,) = yield [(beside(bit), "replica", bit, now)]
            now = self.both(bit, now, got, 0)
        link = beside(1) + ("/" if now.shape[1] > 3 * D else "")
        (got,) = yield [(link, "replica", 1, now)]
        return (now, got)

    def small_steps(self, own):
        (got,) = yield [("small", "shard", 1, own)]
        pair = jnp.stack([own, got])
        (got,) = yield [("small", "shard", 2, pair)]
        return jnp.concatenate([pair, got])[self.order]

    def near_steps(self, own):
        (got,) = yield [("core", "shard", 1, own)]
        return got

    def far_steps(self, own):
        (far,) = yield [("y/", "shard", 2, own)]
        (behind,) = yield [("core", "shard", 1, far)]
        return (far, behind)

    def shared_steps(self, sent, whole_block):
        (got,) = yield [("y" if whole_block else "y/", "shard", 2, sent)]
        width = got.shape[1] // 2
        mine = [got[:, :width], got[:, width:]]
        other = yield [(beside(1), "replica", 1, mine[0]), (beside(2), "replica", 2, mine[1])]
        if whole_block:
            far = [self.both(bit, m, o, 1) for bit, m, o in zip((1, 2), mine, other)]
            far = [jnp.concatenate(far, axis=1)]
        else:
            far = [
                jnp.concatenate(
                    [
                        jnp.where(self.bit(bit) == (n == 1), m, o)
                        for bit, m, o in zip((1, 2), mine, other)
                    ],
                    axis=1,
                )
                for n in range(2)
            ]
        behind = yield [("core", "shard", 1, f) for f in far]
        return list(zip(far, behind))


LATENCY = 2.0
PACE = {"core": 2.0, "y": 22.5, "x": 22.5, "z2": 22.5, "small": 1.0}
MOST_FLYING = 5


class Flow:
    def __init__(self, steps, rank):
        self.steps, self.rank, self.value, self.done = steps, rank, None, False
        self.flying, self.parts, self.ready = [], [], 0.0
        self.asked, self.sent = next(steps), 0

    def give(self, arrays):
        try:
            self.asked, self.sent = self.steps.send(arrays), 0
        except StopIteration as end:
            self.asked, self.value, self.done = [], end.value, True


class Pipeline:
    def __init__(self, token):
        self.now, self.free, self.flows, self.token, self.landed = 0.0, {}, [], token, []

    def add(self, steps, rank=1):
        flow = Flow(steps, rank)
        self.flows = sorted([*self.flows, flow], key=lambda flow: flow.rank)
        return flow

    def tie(self, arrays):
        if not arrays:
            return []
        *arrays, self.token = lax.optimization_barrier((*arrays, self.token))
        return arrays

    def land(self, slack=2.0):
        landed = [f for f in self.flows if f.flying and f.ready <= self.now + slack]
        arrived = [array for flow in landed for array in flow.flying]
        self.landed += arrived
        tied = self.tie(arrived)
        for flow in landed:
            got, tied = tied[: len(flow.flying)], tied[len(flow.flying) :]
            flow.flying = []
            if flow.asked[0][0].endswith("/"):
                flow.parts += got
                if flow.sent < flow.asked[0][3].shape[0]:
                    continue
                got, flow.parts = [jnp.concatenate(flow.parts, axis=0)], []
            flow.give(got)
            if flow.done and isinstance(flow.value, jax.Array):
                (flow.value,) = self.tie([flow.value])
        for flow in self.flows:
            if not flow.done and not flow.flying and not flow.asked:
                flow.give([])
        self.flows = [flow for flow in self.flows if not flow.done]

    def start(self, window=None, ahead=6.0, only=None):
        issued = []
        until = self.now + (ahead if window is None else window - 5.0)
        for flow in self.flows:
            if flow.flying or not flow.asked or (only is not None and flow is not only):
                continue
            count = sum(len(f.flying) for f in self.flows) + len(flow.asked)
            links = [link.strip("/") for link, *_ in flow.asked]
            if count > MOST_FLYING or any(self.free.get(k, 0.0) > until for k in links):
                continue
            if window is not None and not all(self.fits(window, *asked) for asked in flow.asked):
                continue
            for n, (link, axis, bit, values) in enumerate(flow.asked):
                if link.endswith("/"):
                    link, rows = link.strip("/"), values.shape[0]
                    left = rows - flow.sent
                    pace = PACE[link] * values.size * values.dtype.itemsize / MIB / rows
                    busy = max(0.0, self.free.get(link, 0.0) - self.now)
                    room = int(((window or 1000) - LATENCY - busy) / pace + 8) // 16 * 16
                    if left - room > 16 and window is not None:
                        left = room
                    if left < 32:
                        continue
                    values = values[flow.sent : flow.sent + left]
                    flow.sent += left
                issued.append((flow, len(flow.flying), axis, bit, values))
                flow.flying.append(values)
                size = values.size * values.dtype.itemsize / MIB
                start = max(self.now, self.free.get(link, 0.0))
                self.free[link] = start + size * PACE.get(link, 45.0)
                flow.ready = max(flow.ready, self.free[link] + LATENCY)
        pending = [flow for flow in self.flows if not flow.flying and flow.asked]
        pending = [(flow, n) for flow in pending for n in range(len(flow.asked))]
        operands = [values for *_, values in issued] + [f.asked[n][3] for f, n in pending]
        operands = self.tie(operands)
        for (flow, n, axis, bit, _), values in zip(issued, operands):
            flow.flying[n] = swap(values, axis, bit)
        for (flow, n), values in zip(pending, operands[len(issued) :]):
            flow.asked[n] = (*flow.asked[n][:3], values)
        after, self.landed = self.landed + [self.token], []
        return after

    def fits(self, window, link, axis, bit, values):
        if link.endswith("/"):
            return True
        busy = max(0.0, self.free.get(link, 0.0) - self.now)
        length = values.size * values.dtype.itemsize / MIB * PACE.get(link, 45.0)
        return busy + length + LATENCY <= window + 1.5

    def turn(self, window=None):
        self.land()
        return self.start(window)

    def spend(self, length, token):
        self.now += length
        self.token = token

    def wait(self):
        times = [flow.ready for flow in self.flows if flow.flying]
        return max(0.0, min(times) - self.now) if times else 1.0

    def skip(self, wait=0.0):
        self.now += self.wait() + wait

    def reach(self, flow, link, gap=None, wait=0.0, alone=False):
        self.land()
        while flow.asked[0][0] != link:
            self.start(gap, only=flow if alone else None)
            self.now = max(self.now, flow.ready) if alone else self.now + self.wait() + wait
            self.land()

    def finish(self, *flows, window=None, gap=None, wait=0.0):
        self.land()
        while not all(flow.done for flow in flows):
            self.start(gap)
            self.skip(wait)
            self.land()
        return self.start(window)


def on_device(
    tokens,
    out_grad,
    kept_count,
    attn_w,
    mlp_w,
    vectors,
    attn_m,
    mlp_m,
    small_m,
    attn_v,
    mlp_v,
    small_v,
):
    images, slots, _ = tokens.shape
    rows = images * slots
    links = Links()
    order = links.order
    owned = vectors.shape[0]
    image_total = images * links.replicas * links.shards

    small_low = jnp.pad(vectors.astype(BF16).T, ((0, 4), (0, 0)))
    at = jnp.arange(slots, dtype=jnp.int32)
    valid = (at[None, :] < (BUF + kept_count)[:, None]).reshape(rows, 1)
    gy = jnp.where(valid, out_grad.reshape(rows, D), jnp.zeros((), BF16))
    pipe = Pipeline(order)

    def first_norm(small_full):
        normed, _ = normalize(tokens.reshape(rows, D).astype(F32))
        vec = small_full.astype(F32)
        return (normed * vec[0:1] + vec[1:2]).astype(BF16)

    if links.direct:

        def half(array, first, width, bit):
            return lax.dynamic_slice_in_dim(array, first + links.place(bit) * width, width, 1)

        def halves(array, first, second, width):
            sent = [half(array, first, width, 1), half(array, second, width, 2)]
            return jnp.concatenate(sent, axis=1).astype(BF16)

        pair = 3 * D // 2
        qkv_flow = pipe.add(links.shared_steps(halves(attn_w, 0, pair, pair // 2), True), 0)
        vec_flow = pipe.add(links.small_steps(small_low), 0)
        pipe.turn()
        attn_after, mlp_after = pipe.tie([attn_w, mlp_w])
        attn_low, mlp_low = attn_after.astype(BF16), mlp_after.astype(BF16)
        wo_low = attn_after[:, 3 * D :].astype(BF16)
        sends = [halves(mlp_after, n, FF + n, PART) for n in range(0, FF, 2 * PART)]
        pipe.turn()
        sends[0], sends[1], mlp_low, wo_low, gy = pipe.tie([*sends, mlp_low, wo_low, gy])
        mlp_flows = [pipe.add(links.shared_steps(sends[0], False), 0)]
        wo_flow = pipe.add(links.far_steps(wo_low), 0)
        mlp_flows.append(pipe.add(links.shared_steps(sends[1], False), 0))
        pipe.reach(qkv_flow, beside(1), gap=5)
        near_flow = pipe.add(links.near_steps(attn_low), 0)
        small_full = vec_flow.value.transpose(1, 0, 2).reshape(16, D)
        pipe.start(12)
        (h1,) = pipe.tie([first_norm(small_full)])
        pipe.now = max(flow.ready for flow in pipe.flows if flow.flying)
        pipe.land()
        after = pipe.finish(qkv_flow, vec_flow, near_flow, window=13, gap=14)
        attn_near, ((attn_far, behind),) = near_flow.value, qkv_flow.value
        wqkv = [Piece(array, 0, 0) for array in (attn_low, attn_near, attn_far, behind)]
    else:
        attn_low, mlp_low = attn_w.astype(BF16), mlp_w.astype(BF16)
        gather = lambda array, axis: lax.all_gather(array, "shard", axis=axis, tiled=True)
        attn_full, mlp_full = gather(attn_low, 0), gather(mlp_low, 0)
        small_full = gather(small_low, 1)
        wqkv = [Piece(attn_full, j, 0) for j in range(BLOCKS)]
        wo = [Piece(attn_full, j, 3) for j in range(BLOCKS)]
        wups = [[Piece(mlp_full, j, p) for j in range(BLOCKS)] for p in range(PARTS)]
        wdns = [[Piece(mlp_full, j, 4 + p) for j in range(BLOCKS)] for p in range(PARTS)]
        after = []
        h1 = first_norm(small_full)
    vec = small_full.astype(F32)

    totals = []

    def summed(send, keep, urgent=False):
        if links.direct:
            return pipe.add(links.part_steps(send, keep), 1 if urgent else 2)
        return (send, keep)

    def chunk(name, *parts):
        if links.direct:
            totals.append((name, pipe.add(links.chunk_steps(parts), 1 if name[0] == "attn" else 2)))
            return
        stacked = [jnp.stack([k[0], s[0], k[1], s[1]]).reshape(D, -1) for s, k in parts]
        part = lax.psum_scatter(
            jnp.concatenate(stacked, axis=1), "shard", scatter_dimension=0, tiled=True
        )
        part = lax.psum(part, "replica")
        totals.append((name, (part[: part.shape[0] // 2], part[part.shape[0] // 2 :])))

    outs = {"attn": [], "mlp": []}
    state = {
        "attn": (attn_w, attn_m, attn_v, image_total, 0.1, 0.05),
        "mlp": (mlp_w, mlp_m, mlp_v, image_total, 0.05, 0.05),
    }
    small_outs, pieces = [], []
    second = (links.place(1) if links.direct else jnp.zeros((), jnp.int32)).reshape(1)

    def collect():
        through = lambda total: not isinstance(total, Flow) or total.done
        for name, total in [entry for entry in totals if through(entry[1])]:
            total = total.value if isinstance(total, Flow) else total
            if total[0].shape[1] % D:
                some = [half[:, 2 * D : 2 * D + 12] for half in total]
                gradient = jnp.where(
                    second[0] == 1, jnp.concatenate(some[::-1]), jnp.concatenate(some)
                )
                gradient = gradient.astype(F32) / image_total
                small_outs.extend(adam_terms(vectors, small_m, small_v, gradient, 1.0, 0.0))
            pieces.extend((name[0], total, n, column) for n, column in enumerate(name[1:]))
        totals[:] = [entry for entry in totals if not through(entry[1])]

    def adam_some(after, fit):
        kind, total, first, _ = pieces[0]
        columns = [c for k, t, _, c in pieces if t is total][:fit]
        outs[kind], mark = adam_part(total, second, first, columns, *state[kind], outs[kind], after)
        pipe.spend(1.0 + 3.2 * len(columns), mark)
        del pieces[: len(columns)]

    qkv = qkv_forward(order, h1, wqkv, vec, after)
    pipe.spend(15, qkv)
    if links.direct:
        mlp_near_flow = pipe.add(links.near_steps(mlp_low), 0)
    mixed = attn_mix(kept_count, qkv, images, pipe.turn(17))
    pipe.spend(17, mixed)
    if links.direct:
        after = pipe.finish(wo_flow, window=10, gap=16)
        wo_far, behind = wo_flow.value
        wo = [Piece(attn_low, 0, 3), Piece(attn_near, 0, 3), Piece(wo_far, 0, 0), Piece(behind, 0, 0)]
    middle, h2 = out_project(order, tokens, mixed, wo, vec, after)
    pipe.spend(10, h2)

    acts, dpres, gbus = [], [], []
    if links.direct:
        wups, wdns = [], []
    for p in range(PARTS):
        if links.direct:
            flow = mlp_flows[p // 2]
            after = pipe.finish(flow, mlp_near_flow, window=17)
            far, behind = flow.value[p % 2]
            near = [(mlp_low, p, 4 + p), (mlp_near_flow.value, p, 4 + p)]
            four = [*near, (far, 0, 1), (behind, 0, 1)]
            wups.append([Piece(array, 0, up) for array, up, _ in four])
            wdns.append([Piece(array, 0, down) for array, _, down in four])
        act, dpre, send, keep, gbu = mlp_part(
            order, h2, gy, wups[p], wdns[p], vec[8 + p : 9 + p], after
        )
        acts.append(act)
        dpres.append(dpre)
        gbus.append(gbu)
        pipe.spend(17, gbu)
        part = summed(send, keep)
        if p == PARTS - 1:
            chunk(("mlp", 3 + p, p - 1, 4 + p, p), before, part)
        elif p < PARTS - 2:
            chunk(("mlp", 4 + p, p), part)
        before = part
        if p == 0 and links.direct:
            pipe.reach(part, "y/", alone=True)
    da, two_sums, send, keep = mlp_back(
        order, dpres, wups, middle, gy, vec, mixed, pipe.turn(26)
    )
    pipe.spend(26, two_sums)
    out_part = summed(send, keep)

    split = images // 2
    dqkv, sums_a = attn_back(order, kept_count, da, wo, qkv, slots, 0, split, None, pipe.turn(19))
    pipe.spend(19, sums_a)
    dqkv, sums_b = attn_back(
        order, kept_count, da, wo, qkv, slots, split, images - split, dqkv, pipe.turn(19)
    )
    pipe.spend(19, sums_b)
    qkv_sums = sums_a + sums_b
    send, keep = kv_grad(order, h1, dqkv, pipe.turn(14))
    pipe.spend(14, send)
    kv_part = summed(send, keep, True)
    chunk(("attn", 1, 2), kv_part)
    if links.direct:
        pipe.reach(kv_part, "y/", alone=True)
    in_grad, one_sums = input_back(order, dqkv, wqkv, tokens, da, vec, pipe.turn(19))
    pipe.spend(19, one_sums)

    small = jnp.concatenate(
        [
            one_sums[0:2],
            qkv_sums[0:1],
            qkv_sums[2:3],
            two_sums[2:3],
            two_sums[0:2],
            two_sums[3:4],
            *gbus,
            jnp.zeros((4, D), F32),
        ],
        axis=0,
    )
    send, keep = query_grad(order, h1, dqkv, small, pipe.turn(10))
    pipe.spend(10, send)
    chunk(("attn", 3, 0), out_part, summed(send, keep, True))
    if links.direct:
        after = pipe.turn(5)
        collect()
        if pieces:
            adam_some(after, 1)
    result = mlp_out(order, acts, wdns, middle, valid.astype(F32), vec, pipe.turn(17))
    pipe.spend(17, result)
    result = result.reshape(images, slots, D)

    while totals or pieces:
        after = pipe.turn()
        collect()
        if pieces:
            adam_some(after, (2 if len(totals) < 3 else 1) if totals else 4)
        elif totals:
            pipe.skip(1.5)
    attn_out, mlp_out_ = outs["attn"], outs["mlp"]
    return (result, in_grad, *attn_out, *mlp_out_, *small_outs)


def solution(mesh):
    tokens = P(("replica", "shard"), None, None)
    owned = P("shard", None)
    in_specs = (tokens, tokens, P(("replica", "shard")), *[owned] * 9)
    out_specs = (tokens, tokens, *[owned] * 15)
    return jax.shard_map(
        on_device, mesh=mesh, in_specs=in_specs, out_specs=out_specs, check_vma=False
    )
```

```python
import jax
import jax.numpy as jnp
from jax import lax
from jax.experimental import pallas as pl
from jax.experimental.pallas import tpu as pltpu
from jax.sharding import PartitionSpec as P

D = 1024
HEADS = 16
HEAD_DIM = 64
FF = 4096
BUF = 64
STEP = 10
BLOCKS = 4
BLOCK = D // BLOCKS
PARTS = 4
PART = FF // PARTS
GROUP = 4
GROUP_W = GROUP * HEAD_DIM

EPS_NORM = 1e-06
MASKED = -1000000000.0
BETA_ONE = 0.9
BETA_TWO = 0.999
EPS_ADAM = 1e-08

BF16 = jnp.bfloat16
F32 = jnp.float32
MIB = 1 << 20


def normalize(values):
    average = jnp.mean(values, axis=-1, keepdims=True)
    centred = values - average
    inverse = lax.rsqrt(jnp.mean(centred * centred, axis=-1, keepdims=True) + EPS_NORM)
    return (centred * inverse, inverse)


def norm_back(upstream, normed, inverse):
    first_term = jnp.mean(upstream, axis=-1, keepdims=True)
    second_term = normed * jnp.mean(upstream * normed, axis=-1, keepdims=True)
    return inverse * (upstream - first_term - second_term)


def dot(left, right):
    return jnp.dot(left, right, preferred_element_type=F32)


def dot_nt(left, right):
    return lax.dot_general(left, right, (((1,), (1,)), ((), ())), preferred_element_type=F32)


def dot_tn(left, right):
    return lax.dot_general(left, right, (((0,), (0,)), ((), ())), preferred_element_type=F32)


def gelu_pair(values):
    size = jnp.abs(values)
    denominator = 1.0 + size * (0.3275911 * 0.7071067811865476)
    ratio = pl.reciprocal(denominator, approx=True)
    ratio = ratio * (2.0 - denominator * ratio)
    bell = jnp.exp(values * values * (-0.5))
    poly = 0.5 * 1.061405429 * ratio - 0.5 * 1.453152027
    poly = poly * ratio + 0.5 * 1.421413741
    poly = poly * ratio - 0.5 * 0.284496736
    poly = poly * ratio + 0.5 * 0.254829592
    tail = poly * ratio * bell
    below = jnp.where(values >= 0, 1.0 - tail, tail)
    return (values * below, below + values * bell * 0.3989422804014327)


def whole(array):
    rank = len(array.shape)
    return pl.BlockSpec(array.shape, lambda *_: (0,) * rank, pipeline_mode=pl.Buffered(1))


def params(limit):
    return pltpu.CompilerParams(vmem_limit_bytes=limit * MIB)


def cost(flops, nbytes):
    return pl.CostEstimate(flops=int(flops), bytes_accessed=int(nbytes), transcendentals=0)


def call(body, *, scalars, ins, in_specs, outs, out_specs, grid, name, limit, work, scratch=(), after=(), aliases=None):
    first = len(scalars) + len(ins)
    ins = [
        pltpu.with_memory_space_constraint(a, pltpu.HBM)
        if a.size * a.dtype.itemsize >= MIB // 4
        else a
        for a in ins
    ]

    def with_after(*refs):
        body(*refs[:first], *refs[first + len(after) :])

    return pl.pallas_call(
        with_after,
        grid_spec=pltpu.PrefetchScalarGridSpec(
            num_scalar_prefetch=len(scalars),
            grid=grid,
            in_specs=[*in_specs, *[pl.BlockSpec(memory_space=pl.ANY)] * len(after)],
            out_specs=out_specs,
            scratch_shapes=list(scratch),
        ),
        out_shape=outs,
        input_output_aliases=aliases or {},
        compiler_params=params(limit),
        cost_estimate=cost(*work),
        name=name,
    )(*scalars, *ins, *after)


def like(shape, dtype):
    return pltpu.HBM(shape, dtype)


def place(order_ref, target, pieces):
    for j, piece in enumerate(pieces):
        at = pl.multiple_of(order_ref[j] * BLOCK, BLOCK)
        target[pl.ds(at, BLOCK), :] = piece[...]


ANY = pl.BlockSpec(memory_space=pl.ANY)


class Piece:
    def __init__(self, array, row, column):
        self.array, self.row, self.column = array, row, column

    def spec(self, width):
        return pl.BlockSpec(
            (BLOCK, width), lambda *_: (self.row, self.column), pipeline_mode=pl.Buffered(1)
        )

    def view(self, ref, width):
        return ref.at[
            self.row * BLOCK : (self.row + 1) * BLOCK,
            self.column * width : (self.column + 1) * width,
        ]


def arrays(pieces):
    return [piece.array for piece in pieces]


def heads_apart(values, scale=None):
    lane = lax.broadcasted_iota(jnp.int32, values.shape, 1) // HEAD_DIM
    if scale is not None:
        values = values * jnp.asarray(scale, values.dtype)
    zero = jnp.zeros_like(values)
    return jnp.concatenate([jnp.where(lane == h, values, zero) for h in range(GROUP)], axis=0)


def heads_together(values, slots):
    lane = lax.broadcasted_iota(jnp.int32, (slots, GROUP_W), 1) // HEAD_DIM
    out = values[:slots]
    for h in range(1, GROUP):
        out = jnp.where(lane == h, values[h * slots : (h + 1) * slots], out)
    return out


def probs_of(keys, queries_apart, shift):
    scores = dot_nt(keys, queries_apart) + shift
    scores = jnp.exp(scores - jnp.max(scores, axis=0, keepdims=True))
    return scores * (1.0 / jnp.sum(scores, axis=0, keepdims=True))


def key_shift(kept, slots):
    at = lax.broadcasted_iota(jnp.int32, (slots, 1), 0)
    return jnp.where(at < BUF + kept, 0.0, MASKED).astype(F32)


def row_spec(slots, width):
    return pl.BlockSpec((slots, width), lambda i, *_: (i, 0))


def qkv_forward(order, h1, wqkv, vec, after, width=512):
    rows = h1.shape[0]

    def body(order_ref, h1_ref, *refs):
        w_refs, (bias_ref, qkv_ref, w_s) = refs[:BLOCKS], refs[BLOCKS:]
        place(order_ref, w_s, w_refs)
        qkv_ref[...] = (dot(h1_ref[...], w_s[...]) + bias_ref[...]).astype(BF16)

    bias = jnp.concatenate([vec[2:3], jnp.zeros_like(vec[2:3]), vec[3:4]], axis=1)
    return call(
        body,
        scalars=[order],
        ins=[h1, *arrays(wqkv), bias],
        in_specs=[whole(h1)]
        + [pl.BlockSpec((BLOCK, width), lambda i, *_, row=w.row: (row, i)) for w in wqkv]
        + [pl.BlockSpec((1, width), lambda i, *_: (0, i))],
        outs=[like((rows, 3 * D), BF16)],
        out_specs=[pl.BlockSpec((rows, width), lambda i, *_: (0, i))],
        scratch=[pltpu.VMEM((D, width), BF16)],
        grid=(3 * D // width,),
        name="qkv_forward",
        limit=30,
        work=(10 * rows * D * D, 18 * MIB),
        after=after,
    )[0]


def attn_mix(kept, qkv, images, after):
    rows = qkv.shape[0]
    slots = rows // images

    def body(kept_ref, qkv_ref, mixed_ref):
        shift = key_shift(kept_ref[pl.program_id(0)], slots)
        for g in range(HEADS // GROUP):
            at = g * GROUP_W
            q, k, v = (qkv_ref[:, n * D + at : n * D + at + GROUP_W] for n in range(3))
            probs = probs_of(k, heads_apart(q, HEAD_DIM**-0.5), shift).astype(BF16)
            mixed_ref[:, at : at + GROUP_W] = heads_together(dot_tn(probs, v), slots).astype(BF16)

    return call(
        body,
        scalars=[kept],
        ins=[qkv],
        in_specs=[row_spec(slots, 3 * D)],
        outs=[like((rows, D), BF16)],
        out_specs=[row_spec(slots, D)],
        grid=(images,),
        name="attn_mix",
        limit=30,
        work=(14 * rows * D * D, 8 * MIB),
        after=after,
    )[0]


def out_project(order, x, mixed, wo, vec, after):
    images, slots, _ = x.shape
    rows = images * slots

    def body(order_ref, x_ref, mixed_ref, *refs):
        wo_refs, (vec_ref, middle_ref, h2_ref, wo_s) = refs[:BLOCKS], refs[BLOCKS:]

        @pl.when(pl.program_id(0) == 0)
        def _():
            place(order_ref, wo_s, wo_refs)

        branch = dot(mixed_ref[...], wo_s[...]) + vec_ref[4:5, :]
        for n in range(2):
            span = slice(n * slots, (n + 1) * slots)
            middle = x_ref[n].astype(F32) + branch[span]
            middle_ref[span, :] = middle
            normed, _ = normalize(middle)
            h2_ref[span, :] = (normed * vec_ref[5:6, :] + vec_ref[6:7, :]).astype(BF16)

    return call(
        body,
        scalars=[order],
        ins=[x, mixed, *arrays(wo), vec],
        in_specs=[pl.BlockSpec((2, slots, D), lambda i, *_: (i, 0, 0)), row_spec(2 * slots, D)]
        + [w.spec(D) for w in wo]
        + [whole(vec)],
        outs=[like((rows, D), F32), like((rows, D), BF16)],
        out_specs=[row_spec(2 * slots, D)] * 2,
        scratch=[pltpu.VMEM((D, D), BF16)],
        grid=(images // 2,),
        name="out_project",
        limit=30,
        work=(6 * rows * D * D, 12 * MIB),
        after=after,
    )


def mlp_part(order, h2, dm, wup, wdn, bu, after, width=512):
    rows = h2.shape[0]
    weights = [*wup, *wdn]

    def body(order_ref, h2_hbm, dm_hbm, *refs):
        weight_refs, (bu_ref, *outs, gbu_ref) = refs[: 2 * BLOCKS], refs[2 * BLOCKS : -10]
        h2_ref, dm_ref, up_s, dn_s, act_ref, dpre_ref, send, keep, in_sems, out_sems = refs[-10:]
        flying = []

        def put(n, source, index):
            copy = pltpu.make_async_copy(
                source.at[index], outs[n].at[index], out_sems.at[len(flying)]
            )
            copy.start()
            flying.append(copy)

        def fetch(n, source, target, first):
            copies = [pltpu.make_async_copy(source, target, in_sems.at[n])]
            for j in range(BLOCKS):
                at = pl.multiple_of(order_ref[j] * BLOCK, BLOCK)
                copies.append(
                    pltpu.make_async_copy(
                        weights[first + j].view(weight_refs[first + j], PART),
                        (dn_s if first else up_s).at[pl.ds(at, BLOCK), :],
                        in_sems.at[n + 1 + j],
                    )
                )
            for copy in copies:
                copy.start()
            return copies

        def arrive(copies):
            for copy in copies:
                copy.wait()

        ups = fetch(0, h2_hbm, h2_ref, 0)
        dns = fetch(1 + BLOCKS, dm_hbm, dm_ref, BLOCKS)

        def front(n, span):
            if n == 0:
                arrive(ups)
            pre = dot(h2_ref[...], up_s[:, span]) + bu_ref[:, span]
            if n == 0:
                arrive(dns)
            return (pre, dot(dm_ref[...], dn_s[:, span]))

        def middle(span, pre, dact):
            act, slope = gelu_pair(pre)
            act = act.astype(BF16)
            dpre = (dact * slope).astype(BF16)
            act_ref[:, span] = act
            dpre_ref[:, span] = dpre
            gbu_ref[:, span] = jnp.sum(dpre.astype(F32), axis=0, keepdims=True)
            return (act, dpre)

        def back(span, act, dpre):
            for first, left_ref, right in ((0, dm_ref, act), (PART, h2_ref, dpre)):
                there = slice(first + span.start, first + span.stop)
                for j in range(BLOCKS):
                    at = pl.multiple_of(order_ref[j] * BLOCK, BLOCK)
                    grad = dot_tn(left_ref[:, pl.ds(at, BLOCK)], right).astype(BF16)
                    (send if j % 2 else keep)[j // 2, :, there] = grad

        def out(span):
            put(0, act_ref, (slice(None), span))
            put(1, dpre_ref, (slice(None), span))
            for first in (0, PART):
                there = slice(first + span.start, first + span.stop)
                put(2, send, (slice(None), slice(None), there))
                put(3, keep, (slice(None), slice(None), there))

        spans = [slice(at, at + width) for at in range(0, PART, width)]
        fresh = front(0, spans[0])
        held = None
        for n, span in enumerate(spans):
            later = front(n + 1, spans[n + 1]) if n + 1 < len(spans) else None
            now = middle(span, *fresh)
            if held is not None:
                back(spans[n - 1], *held)
                out(spans[n - 1])
            held, fresh = now, later
        back(spans[-1], *held)
        out(spans[-1])
        for copy in flying:
            copy.wait()

    one = pl.BlockSpec((1, PART), lambda i, *_: (0, 0))
    return call(
        body,
        scalars=[order],
        ins=[h2, dm, *arrays(weights), bu],
        in_specs=[ANY] * (2 + len(weights)) + [whole(bu)],
        outs=[like((rows, PART), BF16)] * 2
        + [like((2, BLOCK, 2 * PART), BF16)] * 2
        + [like((1, PART), F32)],
        out_specs=[ANY] * 4 + [one],
        scratch=[pltpu.VMEM((rows, D), BF16)] * 2
        + [pltpu.VMEM((D, PART), BF16)] * 2
        + [pltpu.VMEM((rows, PART), BF16)] * 2
        + [pltpu.VMEM((2, BLOCK, 2 * PART), BF16)] * 2
        + [
            pltpu.SemaphoreType.DMA((2 + 2 * BLOCKS,)),
            pltpu.SemaphoreType.DMA((PART // width * 6,)),
        ],
        grid=(1,),
        name="mlp_part",
        limit=40,
        work=(12 * rows * D * PART, 12 * MIB),
        after=after,
    )


def streamed(order_ref, sides, side_refs, weights, weight_refs, side_s, weight_s, sems, use):
    def copies(p):
        slot = p % 2
        yield pltpu.make_async_copy(side_refs[p], side_s.at[slot], sems.at[slot, BLOCKS])
        for j in range(BLOCKS):
            at = pl.multiple_of(order_ref[j] * BLOCK, BLOCK)
            piece = weights[p][j]
            yield pltpu.make_async_copy(
                piece.view(weight_refs[p * BLOCKS + j], PART),
                weight_s.at[slot, pl.ds(at, BLOCK), :],
                sems.at[slot, j],
            )

    for copy in copies(0):
        copy.start()
    for p in range(PARTS):
        if p + 1 < PARTS:
            for copy in copies(p + 1):
                copy.start()
        for copy in copies(p):
            copy.wait()
        use(p, side_s[p % 2], weight_s[p % 2])


def stream_scratch(rows):
    return [
        pltpu.VMEM((2, rows, PART), BF16),
        pltpu.VMEM((2, D, PART), BF16),
        pltpu.SemaphoreType.DMA((2, BLOCKS + 1)),
        pltpu.VMEM((rows, D), F32),
        pltpu.VMEM((rows, D), F32),
        pltpu.SemaphoreType.DMA((1,)),
    ]


def mlp_back(order, dpres, wups, middle, gy, vec, mixed, after):
    rows = middle.shape[0]
    flat = [w for part in wups for w in part]

    def body(order_ref, *refs):
        dpre_refs, refs = refs[:PARTS], refs[PARTS:]
        up_refs, refs = refs[: PARTS * BLOCKS], refs[PARTS * BLOCKS :]
        middle_ref, gy_ref, vec_ref, mixed_ref, da_ref, sums_ref, send, keep = refs[:8]
        side_s, weight_s, sems, acc, middle_s, middle_sem = refs[8:]

        def use(p, side, weight):
            if p == 0:
                pltpu.make_async_copy(middle_ref, middle_s, middle_sem.at[0]).start()
                acc[...] = dot_nt(side, weight)
            else:
                acc[...] += dot_nt(side, weight)

        streamed(order_ref, dpres, dpre_refs, wups, up_refs, side_s, weight_s, sems, use)
        pltpu.make_async_copy(middle_ref, middle_s, middle_sem.at[0]).wait()
        gain, shift, bias, down = (jnp.zeros((1, D), F32) for _ in range(4))
        step = rows // 6
        for r in range(0, rows, step):
            span = slice(r, r + step)
            dh2 = acc[span, :]
            normed, inverse = normalize(middle_s[span, :])
            gain += jnp.sum(dh2 * normed, axis=0, keepdims=True)
            shift += jnp.sum(dh2, axis=0, keepdims=True)
            dmid = norm_back(dh2 * vec_ref[5:6, :], normed, inverse) + gy_ref[span, :].astype(F32)
            da = dmid.astype(BF16)
            da_ref[span, :] = da
            bias += jnp.sum(da.astype(F32), axis=0, keepdims=True)
            down += jnp.sum(gy_ref[span, :].astype(F32), axis=0, keepdims=True)
        sums_ref[...] = jnp.concatenate([gain, shift, bias, down, jnp.zeros((4, D), F32)], axis=0)
        for j in range(BLOCKS):
            at = pl.multiple_of(order_ref[j] * BLOCK, BLOCK)
            grad = dot_tn(mixed_ref[:, pl.ds(at, BLOCK)], da_ref[...]).astype(BF16)
            (send if j % 2 else keep)[j // 2] = grad

    return call(
        body,
        scalars=[order],
        ins=[*dpres, *arrays(flat), middle, gy, vec, mixed],
        in_specs=[ANY] * (PARTS + len(flat) + 1) + [whole(gy), whole(vec), whole(mixed)],
        outs=[like((rows, D), BF16), like((8, D), F32)]
        + [like((2, BLOCK, D), BF16)] * 2,
        out_specs=[
            pl.BlockSpec((rows, D), lambda i, *_: (0, 0)),
            pl.BlockSpec((8, D), lambda i, *_: (0, 0)),
            pl.BlockSpec((2, BLOCK, D), lambda i, *_: (0, 0, 0)),
            pl.BlockSpec((2, BLOCK, D), lambda i, *_: (0, 0, 0)),
        ],
        scratch=stream_scratch(rows),
        grid=(1,),
        name="mlp_back",
        limit=40,
        work=(3 * rows * D * FF, 30 * MIB),
        after=after,
    )


def mlp_out(order, acts, wdns, middle, valid, vec, after):
    rows = middle.shape[0]
    flat = [w for part in wdns for w in part]

    def body(order_ref, *refs):
        act_refs, refs = refs[:PARTS], refs[PARTS:]
        dn_refs, refs = refs[: PARTS * BLOCKS], refs[PARTS * BLOCKS :]
        middle_ref, valid_ref, vec_ref, out_ref = refs[:4]
        side_s, weight_s, sems, acc, middle_s, middle_sem = refs[4:]

        def use(p, side, weight):
            if p == 0:
                pltpu.make_async_copy(middle_ref, middle_s, middle_sem.at[0]).start()
                acc[...] = dot_nt(side, weight)
            elif p + 1 < PARTS:
                acc[...] += dot_nt(side, weight)
            else:
                pltpu.make_async_copy(middle_ref, middle_s, middle_sem.at[0]).wait()
                total = acc[...] + dot_nt(side, weight) + middle_s[...] + vec_ref[7:8, :]
                out_ref[...] = (total * valid_ref[...]).astype(BF16)

        streamed(order_ref, acts, act_refs, wdns, dn_refs, side_s, weight_s, sems, use)

    return call(
        body,
        scalars=[order],
        ins=[*acts, *arrays(flat), middle, valid, vec],
        in_specs=[ANY] * (PARTS + len(flat) + 1) + [whole(valid), whole(vec)],
        outs=[like((rows, D), BF16)],
        out_specs=[pl.BlockSpec((rows, D), lambda i, *_: (0, 0))],
        scratch=stream_scratch(rows),
        grid=(1,),
        name="mlp_out",
        limit=40,
        work=(3 * rows * D * FF, 24 * MIB),
        after=after,
    )[0]


def attn_back(order, kept, da, wo, qkv, slots, first, count, before, after):
    rows = da.shape[0]

    def body(order_ref, kept_ref, da_ref, *refs):
        wo_refs, refs = refs[:BLOCKS], refs[BLOCKS:]
        qkv_ref, dqkv_ref, sums_ref, wo_s = refs[0], *refs[-3:]
        image = pl.program_id(0)

        @pl.when(image == 0)
        def _():
            place(order_ref, wo_s, wo_refs)
            sums_ref[...] = jnp.zeros_like(sums_ref)

        shift = key_shift(kept_ref[first + image], slots)
        da = da_ref[...]
        scale = HEAD_DIM**-0.5
        for g in range(HEADS // GROUP):
            at = g * GROUP_W
            spans = [slice(n * D + at, n * D + at + GROUP_W) for n in range(3)]
            q, k, v = (qkv_ref[:, span] for span in spans)
            dmix = dot_nt(da, wo_s[at : at + GROUP_W, :]).astype(BF16)
            apart = heads_apart(q, scale)
            probs = probs_of(k, apart, shift)
            dmix_apart = heads_apart(dmix)
            dv = dot(probs.astype(BF16), dmix_apart).astype(BF16)
            dprob = dot_nt(v, dmix_apart)
            product = probs * dprob
            dsc = (product - probs * jnp.sum(product, axis=0, keepdims=True)).astype(BF16)
            dk = dot(dsc, apart).astype(BF16)
            dq = (heads_together(dot_tn(dsc, k), slots) * scale).astype(BF16)
            for n, grad in enumerate((dq, dk, dv)):
                dqkv_ref[:, spans[n]] = grad
                if n != 1:
                    sums_ref[n : n + 1, at : at + GROUP_W] += jnp.sum(
                        grad.astype(F32), axis=0, keepdims=True
                    )

    row = lambda width: pl.BlockSpec((slots, width), lambda i, *_: (first + i, 0))
    extra = [] if before is None else [before]
    return call(
        body,
        scalars=[order, kept],
        ins=[da, *arrays(wo), qkv, *extra],
        in_specs=[row(D)]
        + [w.spec(D) for w in wo]
        + [row(3 * D)]
        + [pl.BlockSpec(memory_space=pl.ANY)] * len(extra),
        outs=[like((rows, 3 * D), BF16), like((8, D), F32)],
        out_specs=[row(3 * D), pl.BlockSpec((8, D), lambda i, *_: (0, 0))],
        scratch=[pltpu.VMEM((D, D), BF16)],
        grid=(count,),
        aliases={4 + BLOCKS: 0} if extra else None,
        name="attn_back",
        limit=30,
        work=(12 * rows * D * D, 18 * MIB),
        after=after,
    )


def input_back(order, dqkv, wqkv, x, da, vec, after):
    images, slots, _ = x.shape
    rows = images * slots

    def body(order_ref, dqkv_ref, *refs):
        wq_refs = refs[:BLOCKS]
        x_ref, da_ref, vec_ref, out_ref, sums_ref, acc = refs[BLOCKS:]

        @pl.when(pl.program_id(0) == 0)
        def _():
            sums_ref[...] = jnp.zeros_like(sums_ref)

        grad = dqkv_ref[...]
        for j in range(BLOCKS):
            at = pl.multiple_of(order_ref[j] * BLOCK, BLOCK)
            acc[:, pl.ds(at, BLOCK)] = dot_nt(grad, wq_refs[j][...])
        for n in range(2):
            dh1 = acc[n * slots : (n + 1) * slots, :]
            normed, inverse = normalize(x_ref[n].astype(F32))
            sums_ref[0:1, :] += jnp.sum(dh1 * normed, axis=0, keepdims=True)
            sums_ref[1:2, :] += jnp.sum(dh1, axis=0, keepdims=True)
            total = norm_back(dh1 * vec_ref[0:1, :], normed, inverse)
            out_ref[n] = (total + da_ref[n * slots : (n + 1) * slots, :].astype(F32)).astype(BF16)

    image = pl.BlockSpec((2, slots, D), lambda i, *_: (i, 0, 0))
    return call(
        body,
        scalars=[order],
        ins=[dqkv, *arrays(wqkv), x, da, vec],
        in_specs=[row_spec(2 * slots, 3 * D)]
        + [w.spec(3 * D) for w in wqkv]
        + [image, row_spec(2 * slots, D), whole(vec)],
        outs=[like((images, slots, D), BF16), like((8, D), F32)],
        out_specs=[image, pl.BlockSpec((8, D), lambda i, *_: (0, 0))],
        scratch=[pltpu.VMEM((2 * slots, D), F32)],
        grid=(images // 2,),
        name="input_back",
        limit=30,
        work=(8 * rows * D * D, 24 * MIB),
        after=after,
    )


def kv_grad(order, left, right, after, width=512):
    rows = right.shape[0]
    steps = D // width

    def body(order_ref, left_ref, right_ref, send, keep):
        for j in range(BLOCKS):
            at = pl.multiple_of(order_ref[j] * BLOCK, BLOCK)
            grad = dot_tn(left_ref[:, pl.ds(at, BLOCK)], right_ref[...]).astype(BF16)
            (send if j % 2 else keep)[j // 2] = grad

    grads = pl.BlockSpec((2, BLOCK, width), lambda i, *_: (0, 0, i))
    return call(
        body,
        scalars=[order],
        ins=[left, right],
        in_specs=[whole(left), pl.BlockSpec((rows, width), lambda i, *_: (0, steps + i))],
        outs=[like((2, BLOCK, 2 * D), BF16)] * 2,
        out_specs=[grads] * 2,
        grid=(2 * steps,),
        name="kv_grad",
        limit=30,
        work=(8 * rows * D * D, 16 * MIB),
        after=after,
    )


def query_grad(order, left, right, small, after):
    rows = right.shape[0]
    columns = D + 128

    def body(order_ref, left_ref, right_ref, small_ref, send, keep):
        for j in range(BLOCKS):
            at = pl.multiple_of(order_ref[j] * BLOCK, BLOCK)
            target = send if j % 2 else keep
            grad = dot_tn(left_ref[:, pl.ds(at, BLOCK)], right_ref[...]).astype(BF16)
            target[j // 2, :, :D] = grad
            some = small_ref[:, pl.ds(at, BLOCK)]
            some = jnp.concatenate([some, jnp.zeros((112, BLOCK), F32)], axis=0)
            target[j // 2, :, D:] = some.T.astype(BF16)

    out = pl.BlockSpec((2, BLOCK, columns), lambda i, *_: (0, 0, 0))
    return call(
        body,
        scalars=[order],
        ins=[left, right, small],
        in_specs=[whole(left), pl.BlockSpec((rows, D), lambda i, *_: (0, 0)), whole(small)],
        outs=[like((2, BLOCK, columns), BF16)] * 2,
        out_specs=[out] * 2,
        grid=(1,),
        name="query_grad",
        limit=30,
        work=(6 * rows * D * D, 10 * MIB),
        after=after,
    )


def adam_terms(weight, first_mom, second_mom, gradient, rate, decay):
    first_new = BETA_ONE * first_mom + (1.0 - BETA_ONE) * gradient
    second_new = BETA_TWO * second_mom + (1.0 - BETA_TWO) * gradient * gradient
    first_hat = first_new * (1.0 / (1.0 - BETA_ONE**STEP))
    second_hat = second_new * (1.0 / (1.0 - BETA_TWO**STEP))
    weight_new = weight - rate * (first_hat / (jnp.sqrt(second_hat) + EPS_ADAM) + decay * weight)
    return (gradient, first_new, second_new, weight_new, weight_new.astype(BF16))


def adam_part(halves, second, first, columns, weight, first_mom, second_mom, count, rate, decay, before, after):
    half = halves[0].shape[0]
    rows = 2 * half
    width = D if len(columns) > 1 else D // 2
    steps = D // width

    def body(columns_ref, second_ref, a_ref, b_ref, w_ref, m_ref, v_ref, *refs):
        lower = second_ref[0] == 1
        a, b = (ref[...].astype(F32) * (1.0 / count) for ref in (a_ref, b_ref))
        for n, gradient in enumerate((jnp.where(lower, b, a), jnp.where(lower, a, b))):
            span = slice(n * half, (n + 1) * half)
            terms = (w_ref[span, :], m_ref[span, :], v_ref[span, :])
            outs = adam_terms(*terms, gradient, rate, decay)
            for ref, value in zip(refs[-6:], outs):
                ref[span, :] = value
        refs[-1][...] = jnp.zeros_like(refs[-1])

    there = pl.BlockSpec((rows, width), lambda i, n, where, _: (0, where[i] * steps + n))
    shape = weight.shape
    *outs, mark = call(
        body,
        scalars=[jnp.array(columns, jnp.int32), second],
        ins=[*halves, weight, first_mom, second_mom, *before],
        in_specs=[pl.BlockSpec((half, width), lambda i, n, *_: (0, (first + i) * steps + n))] * 2
        + [there] * 3
        + [ANY] * len(before),
        outs=[jax.ShapeDtypeStruct(shape, F32)] * 4
        + [jax.ShapeDtypeStruct(shape, BF16), jax.ShapeDtypeStruct((8, 128), F32)],
        out_specs=[there] * 5 + [pl.BlockSpec((8, 128), lambda i, n, *_: (0, 0))],
        grid=(len(columns), steps),
        aliases={7 + n: n for n in range(len(before))},
        name="adam_part",
        limit=30,
        work=(3 * MIB * 1024 * len(columns), 10 * MIB),
        after=after,
    )
    return (outs, mark)


def swap(values, axis, bit):
    size = lax.axis_size(axis)
    return lax.ppermute(values, axis, [(i, i ^ bit) for i in range(size)])


def bits_of(size):
    return [1 << n for n in range(size.bit_length() - 1)]


def beside(bit):
    return "x" if bit == 1 else f"z{bit}"


def added(terms):
    return sum(t.astype(F32) for t in terms).astype(BF16)


class Links:
    def __init__(self):
        self.shards = lax.axis_size("shard")
        self.replicas = lax.axis_size("replica")
        self.direct = self.shards == BLOCKS and self.replicas >= 4
        self.direct = self.direct and self.replicas & (self.replicas - 1) == 0
        index = jnp.arange(BLOCKS, dtype=jnp.int32)
        self.order = index ^ lax.axis_index("shard") if self.direct else index
        self.replica = lax.axis_index("replica")

    def bit(self, bit):
        return (self.replica & bit) != 0

    def place(self, bit):
        return self.bit(bit).astype(jnp.int32)

    def both(self, bit, mine, other, axis):
        return jnp.where(
            self.bit(bit),
            jnp.concatenate([other, mine], axis=axis),
            jnp.concatenate([mine, other], axis=axis),
        )


    def halving(self, terms, bits):
        for bit in bits:
            half = terms[0].shape[1] // 2
            up = self.place(bit)
            size = (1, half, terms[0].shape[2])
            piece = lambda at: [lax.dynamic_slice(t, (0, at * half, 0), size) for t in terms]
            (got,) = yield [(beside(bit), "replica", bit, added(piece(1 - up)))]
            terms = piece(up) + [got]
        return terms

    def part_steps(self, send, keep):
        (got,) = yield [("core", "shard", 1, send)]
        terms = [keep, got]
        (got,) = yield [("y/", "shard", 2, added([t[1] for t in terms]))]
        terms += [got[None]]
        terms = yield from self.halving(terms, bits_of(self.replicas)[:1])
        return added(terms)

    def chunk_steps(self, parts):
        while not all(part.done for part in parts):
            yield []
        bits = bits_of(self.replicas)
        terms = [jnp.concatenate([part.value for part in parts], axis=2)]
        terms = yield from self.halving(terms, bits[1:])
        now = added(terms)[0]
        for bit in reversed(bits[1:]):
            (got,) = yield [(beside(bit), "replica", bit, now)]
            now = self.both(bit, now, got, 0)
        link = beside(1) + ("/" if now.shape[1] > 3 * D else "")
        (got,) = yield [(link, "replica", 1, now)]
        return (now, got)

    def small_steps(self, own):
        (got,) = yield [("small", "shard", 1, own)]
        pair = jnp.stack([own, got])
        (got,) = yield [("small", "shard", 2, pair)]
        return jnp.concatenate([pair, got])[self.order]

    def near_steps(self, own):
        (got,) = yield [("core", "shard", 1, own)]
        return got

    def far_steps(self, own):
        (far,) = yield [("y/", "shard", 2, own)]
        (behind,) = yield [("core", "shard", 1, far)]
        return (far, behind)

    def shared_steps(self, sent, whole_block):
        (got,) = yield [("y" if whole_block else "y/", "shard", 2, sent)]
        width = got.shape[1] // 2
        mine = [got[:, :width], got[:, width:]]
        other = yield [(beside(1), "replica", 1, mine[0]), (beside(2), "replica", 2, mine[1])]
        if whole_block:
            far = [self.both(bit, m, o, 1) for bit, m, o in zip((1, 2), mine, other)]
            far = [jnp.concatenate(far, axis=1)]
        else:
            far = [
                jnp.concatenate(
                    [
                        jnp.where(self.bit(bit) == (n == 1), m, o)
                        for bit, m, o in zip((1, 2), mine, other)
                    ],
                    axis=1,
                )
                for n in range(2)
            ]
        behind = yield [("core", "shard", 1, f) for f in far]
        return list(zip(far, behind))


LATENCY = 2.0
PACE = {"core": 2.0, "y": 22.5, "x": 22.5, "z2": 22.5, "small": 1.0}
MOST_FLYING = 5


class Flow:
    def __init__(self, steps, rank):
        self.steps, self.rank, self.value, self.done = steps, rank, None, False
        self.flying, self.parts, self.ready = [], [], 0.0
        self.asked, self.sent = next(steps), 0

    def give(self, arrays):
        try:
            self.asked, self.sent = self.steps.send(arrays), 0
        except StopIteration as end:
            self.asked, self.value, self.done = [], end.value, True


class Pipeline:
    def __init__(self, token):
        self.now, self.free, self.flows, self.token, self.landed = 0.0, {}, [], token, []

    def add(self, steps, rank=1):
        flow = Flow(steps, rank)
        self.flows = sorted([*self.flows, flow], key=lambda flow: flow.rank)
        return flow

    def tie(self, arrays):
        if not arrays:
            return []
        *arrays, self.token = lax.optimization_barrier((*arrays, self.token))
        return arrays

    def land(self, slack=2.0):
        landed = [f for f in self.flows if f.flying and f.ready <= self.now + slack]
        arrived = [array for flow in landed for array in flow.flying]
        self.landed += arrived
        tied = self.tie(arrived)
        for flow in landed:
            got, tied = tied[: len(flow.flying)], tied[len(flow.flying) :]
            flow.flying = []
            if flow.asked[0][0].endswith("/"):
                flow.parts += got
                if flow.sent < flow.asked[0][3].shape[0]:
                    continue
                got, flow.parts = [jnp.concatenate(flow.parts, axis=0)], []
            flow.give(got)
            if flow.done and isinstance(flow.value, jax.Array):
                (flow.value,) = self.tie([flow.value])
        for flow in self.flows:
            if not flow.done and not flow.flying and not flow.asked:
                flow.give([])
        self.flows = [flow for flow in self.flows if not flow.done]

    def start(self, window=None, ahead=6.0, only=None):
        issued = []
        until = self.now + (ahead if window is None else window - 5.0)
        for flow in self.flows:
            if flow.flying or not flow.asked or (only is not None and flow is not only):
                continue
            count = sum(len(f.flying) for f in self.flows) + len(flow.asked)
            links = [link.strip("/") for link, *_ in flow.asked]
            if count > MOST_FLYING or any(self.free.get(k, 0.0) > until for k in links):
                continue
            if window is not None and not all(self.fits(window, *asked) for asked in flow.asked):
                continue
            for n, (link, axis, bit, values) in enumerate(flow.asked):
                if link.endswith("/"):
                    link, rows = link.strip("/"), values.shape[0]
                    left = rows - flow.sent
                    pace = PACE[link] * values.size * values.dtype.itemsize / MIB / rows
                    busy = max(0.0, self.free.get(link, 0.0) - self.now)
                    room = int(((window or 1000) - LATENCY - busy) / pace + 8) // 16 * 16
                    if left - room > 16 and window is not None:
                        left = room
                    if left < 32:
                        continue
                    values = values[flow.sent : flow.sent + left]
                    flow.sent += left
                issued.append((flow, len(flow.flying), axis, bit, values))
                flow.flying.append(values)
                size = values.size * values.dtype.itemsize / MIB
                start = max(self.now, self.free.get(link, 0.0))
                self.free[link] = start + size * PACE.get(link, 45.0)
                flow.ready = max(flow.ready, self.free[link] + LATENCY)
        pending = [flow for flow in self.flows if not flow.flying and flow.asked]
        pending = [(flow, n) for flow in pending for n in range(len(flow.asked))]
        operands = [values for *_, values in issued] + [f.asked[n][3] for f, n in pending]
        operands = self.tie(operands)
        for (flow, n, axis, bit, _), values in zip(issued, operands):
            flow.flying[n] = swap(values, axis, bit)
        for (flow, n), values in zip(pending, operands[len(issued) :]):
            flow.asked[n] = (*flow.asked[n][:3], values)
        after, self.landed = self.landed + [self.token], []
        return after

    def fits(self, window, link, axis, bit, values):
        if link.endswith("/"):
            return True
        busy = max(0.0, self.free.get(link, 0.0) - self.now)
        length = values.size * values.dtype.itemsize / MIB * PACE.get(link, 45.0)
        return busy + length + LATENCY <= window + 1.5

    def turn(self, window=None):
        self.land()
        return self.start(window)

    def spend(self, length, token):
        self.now += length
        self.token = token

    def wait(self):
        times = [flow.ready for flow in self.flows if flow.flying]
        return max(0.0, min(times) - self.now) if times else 1.0

    def skip(self, wait=0.0):
        self.now += self.wait() + wait

    def reach(self, flow, link, gap=None, wait=0.0, alone=False):
        self.land()
        while flow.asked[0][0] != link:
            self.start(gap, only=flow if alone else None)
            self.now = max(self.now, flow.ready) if alone else self.now + self.wait() + wait
            self.land()

    def finish(self, *flows, window=None, gap=None, wait=0.0):
        self.land()
        while not all(flow.done for flow in flows):
            self.start(gap)
            self.skip(wait)
            self.land()
        return self.start(window)


def on_device(
    tokens,
    out_grad,
    kept_count,
    attn_w,
    mlp_w,
    vectors,
    attn_m,
    mlp_m,
    small_m,
    attn_v,
    mlp_v,
    small_v,
):
    images, slots, _ = tokens.shape
    rows = images * slots
    links = Links()
    order = links.order
    owned = vectors.shape[0]
    image_total = images * links.replicas * links.shards

    small_low = jnp.pad(vectors.astype(BF16).T, ((0, 4), (0, 0)))
    at = jnp.arange(slots, dtype=jnp.int32)
    valid = (at[None, :] < (BUF + kept_count)[:, None]).reshape(rows, 1)
    gy = jnp.where(valid, out_grad.reshape(rows, D), jnp.zeros((), BF16))
    pipe = Pipeline(order)

    def first_norm(small_full):
        normed, _ = normalize(tokens.reshape(rows, D).astype(F32))
        vec = small_full.astype(F32)
        return (normed * vec[0:1] + vec[1:2]).astype(BF16)

    if links.direct:

        def half(array, first, width, bit):
            return lax.dynamic_slice_in_dim(array, first + links.place(bit) * width, width, 1)

        def halves(array, first, second, width):
            sent = [half(array, first, width, 1), half(array, second, width, 2)]
            return jnp.concatenate(sent, axis=1).astype(BF16)

        pair = 3 * D // 2
        qkv_flow = pipe.add(links.shared_steps(halves(attn_w, 0, pair, pair // 2), True), 0)
        vec_flow = pipe.add(links.small_steps(small_low), 0)
        pipe.turn()
        attn_after, mlp_after = pipe.tie([attn_w, mlp_w])
        attn_low, mlp_low = attn_after.astype(BF16), mlp_after.astype(BF16)
        wo_low = attn_after[:, 3 * D :].astype(BF16)
        sends = [halves(mlp_after, n, FF + n, PART) for n in range(0, FF, 2 * PART)]
        pipe.turn()
        sends[0], sends[1], mlp_low, wo_low, gy = pipe.tie([*sends, mlp_low, wo_low, gy])
        mlp_flows = [pipe.add(links.shared_steps(sends[0], False), 0)]
        wo_flow = pipe.add(links.far_steps(wo_low), 0)
        mlp_flows.append(pipe.add(links.shared_steps(sends[1], False), 0))
        pipe.reach(qkv_flow, beside(1), gap=5)
        near_flow = pipe.add(links.near_steps(attn_low), 0)
        small_full = vec_flow.value.transpose(1, 0, 2).reshape(16, D)
        pipe.start(12)
        (h1,) = pipe.tie([first_norm(small_full)])
        pipe.now = max(flow.ready for flow in pipe.flows if flow.flying)
        pipe.land()
        after = pipe.finish(qkv_flow, vec_flow, near_flow, window=13, gap=14)
        attn_near, ((attn_far, behind),) = near_flow.value, qkv_flow.value
        wqkv = [Piece(array, 0, 0) for array in (attn_low, attn_near, attn_far, behind)]
    else:
        attn_low, mlp_low = attn_w.astype(BF16), mlp_w.astype(BF16)
        gather = lambda array, axis: lax.all_gather(array, "shard", axis=axis, tiled=True)
        attn_full, mlp_full = gather(attn_low, 0), gather(mlp_low, 0)
        small_full = gather(small_low, 1)
        wqkv = [Piece(attn_full, j, 0) for j in range(BLOCKS)]
        wo = [Piece(attn_full, j, 3) for j in range(BLOCKS)]
        wups = [[Piece(mlp_full, j, p) for j in range(BLOCKS)] for p in range(PARTS)]
        wdns = [[Piece(mlp_full, j, 4 + p) for j in range(BLOCKS)] for p in range(PARTS)]
        after = []
        h1 = first_norm(small_full)
    vec = small_full.astype(F32)

    totals = []

    def summed(send, keep, urgent=False):
        if links.direct:
            return pipe.add(links.part_steps(send, keep), 1 if urgent else 2)
        return (send, keep)

    def chunk(name, *parts):
        if links.direct:
            totals.append((name, pipe.add(links.chunk_steps(parts), 1 if name[0] == "attn" else 2)))
            return
        stacked = [jnp.stack([k[0], s[0], k[1], s[1]]).reshape(D, -1) for s, k in parts]
        part = lax.psum_scatter(
            jnp.concatenate(stacked, axis=1), "shard", scatter_dimension=0, tiled=True
        )
        part = lax.psum(part, "replica")
        totals.append((name, (part[: part.shape[0] // 2], part[part.shape[0] // 2 :])))

    qkv = qkv_forward(order, h1, wqkv, vec, after)
    pipe.spend(15, qkv)
    if links.direct:
        mlp_near_flow = pipe.add(links.near_steps(mlp_low), 0)
    mixed = attn_mix(kept_count, qkv, images, pipe.turn(17))
    pipe.spend(17, mixed)
    if links.direct:
        after = pipe.finish(wo_flow, window=10, gap=16)
        wo_far, behind = wo_flow.value
        wo = [Piece(attn_low, 0, 3), Piece(attn_near, 0, 3), Piece(wo_far, 0, 0), Piece(behind, 0, 0)]
    middle, h2 = out_project(order, tokens, mixed, wo, vec, after)
    pipe.spend(10, h2)

    acts, dpres, gbus = [], [], []
    if links.direct:
        wups, wdns = [], []
    for p in range(PARTS):
        if links.direct:
            flow = mlp_flows[p // 2]
            after = pipe.finish(flow, mlp_near_flow, window=17)
            far, behind = flow.value[p % 2]
            near = [(mlp_low, p, 4 + p), (mlp_near_flow.value, p, 4 + p)]
            four = [*near, (far, 0, 1), (behind, 0, 1)]
            wups.append([Piece(array, 0, up) for array, up, _ in four])
            wdns.append([Piece(array, 0, down) for array, _, down in four])
        act, dpre, send, keep, gbu = mlp_part(
            order, h2, gy, wups[p], wdns[p], vec[8 + p : 9 + p], after
        )
        acts.append(act)
        dpres.append(dpre)
        gbus.append(gbu)
        pipe.spend(17, gbu)
        part = summed(send, keep)
        if p == PARTS - 1:
            chunk(("mlp", 3 + p, p - 1, 4 + p, p), before, part)
        elif p < PARTS - 2:
            chunk(("mlp", 4 + p, p), part)
        before = part
        if p == 0 and links.direct:
            pipe.reach(part, "y/", alone=True)
    da, two_sums, send, keep = mlp_back(
        order, dpres, wups, middle, gy, vec, mixed, pipe.turn(26)
    )
    pipe.spend(26, two_sums)
    out_part = summed(send, keep)

    split = images // 2
    dqkv, sums_a = attn_back(order, kept_count, da, wo, qkv, slots, 0, split, None, pipe.turn(19))
    pipe.spend(19, sums_a)
    dqkv, sums_b = attn_back(
        order, kept_count, da, wo, qkv, slots, split, images - split, dqkv, pipe.turn(19)
    )
    pipe.spend(19, sums_b)
    qkv_sums = sums_a + sums_b
    send, keep = kv_grad(order, h1, dqkv, pipe.turn(14))
    pipe.spend(14, send)
    kv_part = summed(send, keep, True)
    chunk(("attn", 1, 2), kv_part)
    if links.direct:
        pipe.reach(kv_part, "y/", alone=True)
    in_grad, one_sums = input_back(order, dqkv, wqkv, tokens, da, vec, pipe.turn(19))
    pipe.spend(19, one_sums)

    small = jnp.concatenate(
        [
            one_sums[0:2],
            qkv_sums[0:1],
            qkv_sums[2:3],
            two_sums[2:3],
            two_sums[0:2],
            two_sums[3:4],
            *gbus,
            jnp.zeros((4, D), F32),
        ],
        axis=0,
    )
    send, keep = query_grad(order, h1, dqkv, small, pipe.turn(10))
    pipe.spend(10, send)
    chunk(("attn", 3, 0), out_part, summed(send, keep, True))
    result = mlp_out(order, acts, wdns, middle, valid.astype(F32), vec, pipe.turn(17))
    pipe.spend(17, result)
    result = result.reshape(images, slots, D)

    outs = {"attn": [], "mlp": []}
    state = {
        "attn": (attn_w, attn_m, attn_v, image_total, 0.1, 0.05),
        "mlp": (mlp_w, mlp_m, mlp_v, image_total, 0.05, 0.05),
    }
    small_out, pieces = None, []
    second = (links.place(1) if links.direct else jnp.zeros((), jnp.int32)).reshape(1)
    while totals or pieces:
        after = pipe.turn()
        through = lambda total: not isinstance(total, Flow) or total.done
        for name, total in [entry for entry in totals if through(entry[1])]:
            total = total.value if isinstance(total, Flow) else total
            if total[0].shape[1] % D:
                some = [half[:, 2 * D : 2 * D + 12] for half in total]
                gradient = jnp.where(
                    second[0] == 1, jnp.concatenate(some[::-1]), jnp.concatenate(some)
                )
                gradient = gradient.astype(F32) / image_total
                small_out = adam_terms(vectors, small_m, small_v, gradient, 1.0, 0.0)
            pieces += [(name[0], total, n, column) for n, column in enumerate(name[1:])]
        totals = [entry for entry in totals if not through(entry[1])]
        wait = pipe.wait() if totals else 1000.0
        kind, total, first, _ = pieces[0] if pieces else (None,) * 4
        fit = int(wait >= 4.0) if totals else 4
        columns = [c for k, t, _, c in pieces if t is total][:fit]
        if columns:
            outs[kind], mark = adam_part(total, second, first, columns, *state[kind], outs[kind], after)
            pipe.spend(1.0 + 3.2 * len(columns), mark)
            pieces = pieces[len(columns) :]
        elif totals:
            pipe.skip(1.5)
    attn_out, mlp_out_ = outs["attn"], outs["mlp"]
    return (result, in_grad, *attn_out, *mlp_out_, *small_out)


def solution(mesh):
    tokens = P(("replica", "shard"), None, None)
    owned = P("shard", None)
    in_specs = (tokens, tokens, P(("replica", "shard")), *[owned] * 9)
    out_specs = (tokens, tokens, *[owned] * 15)
    return jax.shard_map(
        on_device, mesh=mesh, in_specs=in_specs, out_specs=out_specs, check_vma=False
    )
```
